32 devices in a mesh: wide: 8 (over z, y), narrow: 4 (over x, core).
Axes of the slice: x: 2, y: 2, z: 4, core: 2. Of those that a mesh axis runs over, the one named last changes fastest.
Arguments:
- images: bfloat16 [512, 784, 192], P(('wide', 'narrow')), may hold values from -6 to 6
- token_mask: int32 [512, 784], P(('wide', 'narrow')), may hold values from 0 to 1, as said below
- w_short: float32 [192, 384], P(None, 'wide'), may hold values from -0.875 to 0.875
- w_qkv: float32 [192, 1152], P(None, 'wide'), may hold values from -0.875 to 0.875
- w_out: float32 [384, 384], P(None, 'wide'), may hold values from -1.25 to 1.25
- w_up: float32 [384, 1536], P(None, 'wide'), may hold values from -0.3125 to 0.3125
- w_down: float32 [1536, 384], P('wide'), may hold values from -0.15625 to 0.15625
- ln1_gain: float32 [192], replicated, may hold values from 0.25 to 1.75
- ln1_shift: float32 [192], replicated, may hold values from -4 to 4
- out_bias: float32 [384], replicated, may hold values from -4 to 4
- ln2_gain: float32 [384], replicated, may hold values from 0.25 to 1.75
- ln2_shift: float32 [384], replicated, may hold values from -4 to 4
- up_bias: float32 [1536], replicated, may hold values from -4 to 4
- down_bias: float32 [384], replicated, may hold values from -4 to 4
- rel_table: float32 [12, 729], replicated, may hold values from -4 to 4
- cotangent: bfloat16 [512, 196, 384], P(('wide', 'narrow')), may hold values from -6 to 6
Outputs:
- output: bfloat16 [512, 196, 384], P(('wide', 'narrow'))
- grad_images: bfloat16 [512, 784, 192], P(('wide', 'narrow'))
- grad_w_short: float32 [192, 384], P(None, 'wide')
- grad_w_qkv: float32 [192, 1152], P(None, 'wide')
- grad_w_out: float32 [384, 384], P(None, 'wide')
- grad_w_up: float32 [384, 1536], P(None, 'wide')
- grad_w_down: float32 [1536, 384], P('wide')
- grad_ln1_gain: float32 [192], replicated
- grad_ln1_shift: float32 [192], replicated
- grad_out_bias: float32 [384], replicated
- grad_ln2_gain: float32 [384], replicated
- grad_ln2_shift: float32 [384], replicated
- grad_up_bias: float32 [1536], replicated
- grad_down_bias: float32 [384], replicated
- grad_table: float32 [12, 729], replicated
The draws below stay inside these ranges and needn't reach their ends.
Inputs may be any that keep to these rules, and one draw needn't show every extreme that they name: `token_mask`: in each image the ones form the top-left rectangle of its 28 x 2 * 14 input grid; its height and width are each 7 to 28, drawn independently for each image.
All inputs are finite; a program needn't handle non-finite values.
Results may differ from the reference program's by a relative error of at most 0.017.
The reference program's roundings to bfloat16 on the way count: a program that leaves them out, or rounds other values in their place, can miss the bound.
Values may be sent and summed in bfloat16 or wider, within the bound.
No kernel may reach another device: no remote copies, remote signals or barrier semaphores. Data moves between devices by JAX's collectives and lax.ppermute only.
A program may use at most 320 MiB of HBM per device.

```python
import math
import jax
import jax.numpy as jnp
from jax import lax

D_IN = 192
D_OUT = 384
HEADS = 12
HEAD_DIM = 32
FF = 1536
GRID = 14
IMAGES = 512
TOK = 196
PIX = 784
REL = 729


def draw_token_mask(key, part):
    key = jax.random.fold_in(key, 11)
    height_key, width_key = jax.random.split(key)
    heights = jax.random.randint(height_key, (IMAGES, 1), 7, 2 * GRID + 1)
    widths = jax.random.randint(width_key, (IMAGES, 1), 7, 2 * GRID + 1)
    cells = jnp.arange(4 * GRID * GRID, dtype=jnp.int32)
    row_of = cells // (2 * GRID)
    col_of = cells % (2 * GRID)
    inside = (row_of[None, :] < heights) & (col_of[None, :] < widths)
    return inside.astype(jnp.int32)


def level_of(stream_key, dims, pieces, least, top_value):
    def one(position, blocks):
        steps = jax.random.uniform(jax.random.fold_in(jax.random.fold_in(stream_key, 6), position), (blocks,), jnp.float32, least / len(pieces), top_value / len(pieces))
        return jnp.repeat(jnp.exp(steps), dims[position] // blocks).reshape((-1,) + (1,) * (len(dims) - position - 1))

    factor_of = one(*pieces[0])
    for cut in pieces[1:]:
        factor_of = factor_of * one(*cut)
    return factor_of


def noise(rng, extent, scale, most, pieces=(), held_as=jnp.bfloat16):
    values = scale * jax.random.normal(rng, extent, jnp.float32)
    if pieces:
        values = values * level_of(rng, extent, pieces, -0.22, 0.18)
    return jnp.clip(values, -most, most).astype(held_as)


def setup_inputs(seed: int = 0) -> dict:
    splits = jax.random.split(jax.random.key(seed), 17)
    images = noise(splits[0], (IMAGES, PIX, D_IN), 1.0, 6.0, ((0, 32),))
    token_mask = draw_token_mask(jax.random.fold_in(splits[16], 71), 0)
    w_short = noise(splits[2], (D_IN, D_OUT), (D_IN // 4) ** -0.5, 0.875, ((1, 8),), jnp.float32)
    w_qkv = noise(splits[3], (D_IN, 3 * D_OUT), (D_IN // 4) ** -0.5, 0.875, ((1, 8),), jnp.float32)
    w_out = noise(splits[4], (D_OUT, D_OUT), (D_OUT // 16) ** -0.5, 1.25, ((1, 8),), jnp.float32)
    w_up = noise(splits[5], (D_OUT, FF), D_OUT ** -0.5, 0.3125, ((1, 8),), jnp.float32)
    w_down = noise(splits[6], (FF, D_OUT), FF ** -0.5, 0.15625, ((0, 8),), jnp.float32)
    ln1_gain = jnp.clip(1.0 + 0.15 * jax.random.normal(splits[7], (D_IN,), jnp.float32), 0.25, 1.75)
    ln1_shift = noise(splits[8], (D_IN,), 0.3, 4.0, (), jnp.float32)
    out_bias = noise(splits[9], (D_OUT,), 0.3, 4.0, (), jnp.float32)
    ln2_gain = jnp.clip(1.0 + 0.15 * jax.random.normal(splits[10], (D_OUT,), jnp.float32), 0.25, 1.75)
    ln2_shift = noise(splits[11], (D_OUT,), 0.3, 4.0, (), jnp.float32)
    up_bias = noise(splits[12], (FF,), 0.3, 4.0, (), jnp.float32)
    down_bias = noise(splits[13], (D_OUT,), 0.3, 4.0, (), jnp.float32)
    rel_table = noise(splits[14], (HEADS, REL), 0.5, 4.0, (), jnp.float32)
    cotangent = noise(splits[15], (IMAGES, TOK, D_OUT), 1.0, 6.0, ((0, 32),))
    return dict(images=images, token_mask=token_mask, w_short=w_short, w_qkv=w_qkv, w_out=w_out, w_up=w_up, w_down=w_down, ln1_gain=ln1_gain, ln1_shift=ln1_shift, out_bias=out_bias, ln2_gain=ln2_gain, ln2_shift=ln2_shift, up_bias=up_bias, down_bias=down_bias, rel_table=rel_table, cotangent=cotangent)


@jax.custom_vjp
def low(v):
    return lax.optimization_barrier(v.astype(jnp.bfloat16)).astype(jnp.float32)

@jax.custom_vjp
def low_back(v):
    return v

def low_keep(v):
    return (low(v), None)

def low_pass(kept, grad):
    return (grad,)

def back_keep(v):
    return (v, None)

def back_low(kept, grad):
    return (low(grad),)
low.defvjp(low_keep, low_pass)
low_back.defvjp(back_keep, back_low)

def product(left_side, right_side):
    return jnp.dot(left_side, right_side, precision=lax.Precision.HIGHEST, preferred_element_type=jnp.float32)

def layer_norm(values, norm_gain, norm_shift):
    center = lax.optimization_barrier(jnp.mean(values, axis=-1, keepdims=True))
    shifted = values - center
    spread = lax.optimization_barrier(jnp.mean(shifted * shifted, axis=-1, keepdims=True))
    return shifted * lax.rsqrt(spread + 1e-05) * norm_gain + norm_shift

def pool_mean(values, pix_weight):
    img_count = values.shape[0]
    channels = values.shape[-1]
    summed = lax.optimization_barrier(jnp.sum((values * pix_weight[:, :, None]).reshape(img_count, GRID, 2, GRID, 2, channels), axis=(2, 4)))
    counted = lax.optimization_barrier(jnp.sum(pix_weight.reshape(img_count, GRID, 2, GRID, 2), axis=(2, 4)))
    pooled = summed / jnp.maximum(counted, 1.0)[..., None]
    return (pooled.reshape(img_count, GRID * GRID, channels), counted.reshape(img_count, GRID * GRID))

def relative_index():
    cells = jnp.arange(GRID * GRID, dtype=jnp.int32)
    row_of = cells // GRID
    col_of = cells % GRID
    side = 2 * GRID - 1
    return ((row_of[:, None] - row_of[None, :] + GRID - 1) * side + col_of[:, None] - col_of[None, :] + GRID - 1).astype(jnp.int32)

def forward(image_f, w_short, w_qkv, w_out, w_up, w_down, ln1_gain, ln1_shift, out_bias, ln2_gain, ln2_shift, up_bias, down_bias, rel_table, pix_weight):
    img_count = image_f.shape[0]
    tok_rows = img_count * GRID * GRID
    normed = layer_norm(image_f, ln1_gain, ln1_shift)
    pooled, counted = pool_mean(normed, pix_weight)
    plain, unused = pool_mean(image_f, pix_weight)
    valid = (counted > 0.5).astype(jnp.float32)
    short_term = low_back(product(low(plain).reshape(tok_rows, D_IN), low(w_short)))
    qkv_all = low(low_back(product(low(pooled).reshape(tok_rows, D_IN), low(w_qkv))))
    qkv_all = qkv_all.reshape(img_count, GRID * GRID, 3, HEADS, HEAD_DIM)
    query = qkv_all[:, :, 0]
    key_part = qkv_all[:, :, 1]
    value_part = qkv_all[:, :, 2]
    full_bias = rel_table[:, relative_index()]
    scores = jnp.einsum('nqhd,nkhd->nhqk', query, key_part, precision=lax.Precision.HIGHEST) * HEAD_DIM ** (-0.5)
    scores = low_back(scores + full_bias[None])
    scores = jnp.where(valid[:, None, None, :] > 0.5, scores, -1e+30)
    top_score = lax.optimization_barrier(jnp.max(scores, axis=-1, keepdims=True))
    expo_part = jnp.exp(scores - top_score)
    probs = expo_part / lax.optimization_barrier(jnp.sum(expo_part, axis=-1, keepdims=True))
    mixed = low(low_back(jnp.einsum('nhqk,nkhd->nqhd', low(probs), value_part, precision=lax.Precision.HIGHEST)))
    attn_term = low_back(product(mixed.reshape(tok_rows, D_OUT), low(w_out))) + out_bias
    first = short_term + attn_term
    normed_two = layer_norm(first, ln2_gain, ln2_shift)
    hidden = low_back(product(low(normed_two), low(w_up))) + up_bias
    act_value = jax.nn.gelu(hidden, approximate=False)
    branch = low_back(product(low(act_value), low(w_down))) + down_bias
    result = (first + branch) * valid.reshape(tok_rows, 1)
    return result.reshape(img_count, GRID * GRID, D_OUT)

def reference(images, token_mask, w_short, w_qkv, w_out, w_up, w_down, ln1_gain, ln1_shift, out_bias, ln2_gain, ln2_shift, up_bias, down_bias, rel_table, cotangent):
    group = math.gcd(IMAGES, 16)
    rounds = IMAGES // group
    params = (w_short, w_qkv, w_out, w_up, w_down, ln1_gain, ln1_shift, out_bias, ln2_gain, ln2_shift, up_bias, down_bias, rel_table)
    image_groups = images.reshape(rounds, group, PIX, D_IN)
    mask_groups = token_mask.reshape(rounds, group, PIX)
    cot_groups = cotangent.reshape(rounds, group, TOK, D_OUT)

    def one_group(totals, item):
        image_part, mask_part, cot_part = item
        pix_weight = mask_part.astype(jnp.float32)

        def closed(image_f, *weights):
            return forward(image_f, *weights, pix_weight)
        result, pullback = jax.vjp(closed, image_part.astype(jnp.float32), *params)
        grads = pullback(cot_part.astype(jnp.float32))
        totals = tuple((acc + part_grad for acc, part_grad in zip(totals, grads[1:])))
        return (totals, (result.astype(jnp.bfloat16), grads[0].astype(jnp.bfloat16)))
    zeros_init = tuple((jnp.zeros(param.shape, jnp.float32) for param in params))
    totals, (outputs, grad_imgs) = lax.scan(one_group, zeros_init, (image_groups, mask_groups, cot_groups))
    return (outputs.reshape(IMAGES, TOK, D_OUT), grad_imgs.reshape(IMAGES, PIX, D_IN), totals[0], totals[1], totals[2], totals[3], totals[4], totals[5], totals[6], totals[7], totals[8], totals[9], totals[10], totals[11], totals[12])
```

```python
import functools
import math

import jax
import jax.numpy as jnp
from jax import lax
from jax.experimental import pallas as pl
from jax.experimental.pallas import tpu as pltpu
from jax.sharding import PartitionSpec as P

D_IN = 192
D_OUT = 384
HEADS = 12
HEAD_DIM = 32
FF = 1536
GRID = 14
SIDE = 2 * GRID - 1
TOK = GRID * GRID
PIX = 4 * TOK
EPS = 1e-05
LOG2E = math.log2(math.e)
SCORE_SCALE = HEAD_DIM ** (-0.5)

SLOT = 208
SMALL = 128
STRIP = 112
WIDE_ROWS = 16 * GRID
NARROW_ROWS = 16 * 8
BIAS_ROWS = HEADS * (WIDE_ROWS + NARROW_ROWS)
CHUNK = 256
PARTS = 8
BF = jnp.bfloat16
F32 = jnp.float32
NN = (((1,), (0,)), ((), ()))
NT = (((1,), (1,)), ((), ()))
TN = (((0,), (0,)), ((), ()))


def mm(left, right, dims=NN):
    return lax.dot_general(left, right, dims, preferred_element_type=F32)


def iota(shape, dim):
    return lax.broadcasted_iota(jnp.int32, shape, dim)


def geometry(meta, n):
    high, wide = meta[0, n], meta[1, n]
    rows, cols = (high + 1) >> 1, (wide + 1) >> 1
    stride = jnp.where(cols <= 8, 8, GRID)
    return high, wide, rows, cols, stride


def cell_of(index, stride):
    row = jnp.where(stride == 8, index >> 3, (index * 4682) >> 16)
    return row, index - stride * row


def packed_index(index, stride, rows, cols):
    row, col = cell_of(index, stride)
    return jnp.where((col < cols) & (row < rows), row * cols + col, -1)


def onehot(mask):
    return jnp.where(mask, 1.0, 0.0).astype(BF)


def packing(shape, stride, rows, cols):
    return onehot(iota(shape, 0) == packed_index(iota((1, shape[1]), 1), stride, rows, cols))


def unpacking(shape, stride, rows, cols):
    return onehot(iota(shape, 1) == packed_index(iota((shape[0], 1), 0), stride, rows, cols))


def split_two(values):
    high = values.astype(BF)
    return high, (values - high.astype(F32)).astype(BF)


def shift_map(cell, stride, lanes):
    spot = iota((1, lanes), 1)
    row, col = cell_of(spot, stride)
    pick = jnp.where((row < GRID) & (col < GRID), SIDE * row + col - cell + GRID - 1, -1)
    return onehot(iota((384, lanes), 0) == pick)


def norm_stats(values):
    center = jnp.mean(values, axis=-1, keepdims=True)
    shifted = values - center
    spread = jnp.mean(shifted * shifted, axis=-1, keepdims=True)
    return shifted, lax.rsqrt(spread + EPS)


def front_kernel(meta, img, cot, tab, hat, plain, cotp, bias, slot_scr, shift_scr):
    n = pl.program_id(0)
    high, wide, rows, cols, stride = geometry(meta, n)
    start = pl.multiple_of(meta[2, n], 16)

    @pl.when(n == 0)
    def _():
        shift_scr[...] = jnp.zeros_like(shift_scr)
        table = tab[...] * LOG2E
        for r in range(GRID):
            moved = pltpu.roll(table, (768 - SIDE * (GRID - 1 - r)) % 768, 1)
            for k in range(3):
                shift_scr[k, pl.ds(r, HEADS, stride=16), :] = moved[
                    :HEADS, 128 * k : 128 * k + 128
                ]
        top, rest = split_two(jnp.concatenate([shift_scr[k] for k in range(3)], axis=1))
        for cell in range(GRID):
            pick = shift_map(cell, GRID, 256)
            spread = mm(top, pick) + mm(rest, pick)
            for k in range(2):
                bias[k, pl.ds(cell, 192, stride=GRID), :] = spread[:, 128 * k : 128 * k + 128]
        for cell in range(8):
            pick = shift_map(cell, 8, 128)
            bias[0, pl.ds(HEADS * WIDE_ROWS + cell, 192, stride=8), :] = mm(top, pick) + mm(
                rest, pick
            )

    hat[...] = jnp.zeros_like(hat)
    slot_scr[...] = jnp.zeros_like(slot_scr)
    spot = iota((1, STRIP), 1)
    prow = (spot >= 28).astype(jnp.int32) + (spot >= 56) + (spot >= 84)
    pcol = spot - 28 * prow
    token = jnp.where(pcol < wide, (prow >> 1) * stride + (pcol >> 1), -1)
    base_hit = iota((32, STRIP), 0) == token

    def strip(i):
        pixels = img[0, STRIP * i : STRIP * (i + 1), :]
        shifted, scale = norm_stats(pixels.astype(F32))
        normed = (shifted * scale).astype(BF)
        hit = jnp.where(base_hit & (prow + 4 * i < high), 1.0, 0.0)
        share = 1.0 / jnp.maximum(jnp.sum(hit, axis=1, keepdims=True), 1.0)
        hit = hit.astype(BF)
        pooled = mm(hit, normed) * share
        pooled_plain = mm(hit, pixels) * share
        for step in (8, GRID):

            @pl.when(stride == step)
            def _():
                hat[0, 2 * step * i : 2 * step * i + 32, :] = pooled
                slot_scr[2 * step * i : 2 * step * i + 32, :] = pooled_plain

    for i in range(7):
        if i < 2:
            strip(i)
        else:
            pl.when(4 * i < high)(functools.partial(strip, i))

    def pack(size):
        pick = packing((size, SLOT), stride, rows, cols)
        plain[pl.ds(start, size), :] = mm(pick, slot_scr[...].astype(BF)).astype(BF)
        pick = packing((size, TOK), GRID, rows, cols)
        cotp[pl.ds(start, size), :] = mm(pick, cot[0]).astype(BF)

    pl.when(rows * cols <= SMALL)(functools.partial(pack, SMALL))
    pl.when(rows * cols > SMALL)(functools.partial(pack, SLOT))

    @pl.when(n == pl.num_programs(0) - 1)
    def _():
        total = pl.multiple_of(meta[3, 0], 16)
        plain[pl.ds(total, CHUNK), :] = jnp.zeros((CHUNK, D_IN), BF)
        cotp[pl.ds(total, CHUNK), :] = jnp.zeros((CHUNK, D_OUT), BF)


def fetch_shards(meta, mine, other, dest, sems):
    own, core = meta[3, 1], meta[3, 2]
    copies = []
    for d in range(PARTS):
        for k, source in enumerate((mine, other)):
            half = core if k == 0 else 1 - core
            copies.append(
                pltpu.make_async_copy(source.at[d], dest.at[own ^ d, half], sems.at[2 * d + k])
            )
    for copy in copies:
        copy.start()
    return copies


def unpack_qkv(att, qkv_scr):
    for j in range(PARTS):
        left = jnp.concatenate([att[j, 0, 48:80, 0:192], att[j, 1, 0:64, 0:192]], axis=0)
        qkv_scr[144 * j : 144 * j + 96, :] = left
        right = jnp.concatenate([att[j, 0, 48:80, 192:384], att[j, 1, 0:16, 192:384]], axis=0)
        qkv_scr[144 * j + 96 : 144 * j + 144, :] = right


def slot_valid(shape, dim, stride, rows, cols):
    row, col = cell_of(iota(shape, dim), stride)
    return (col < cols) & (row < rows)


def table_row(head, stride):
    row = jnp.where(stride == 8, HEADS * WIDE_ROWS + head * NARROW_ROWS, head * WIDE_ROWS)
    return pl.multiple_of(row, 8)


def attend_kernel(
    meta, hat, gains, att_mine, att_other, bias, qkvt, probs, mixed,
    wqkv_scr, mix_scr, att_scr, sems,
):
    n = pl.program_id(0)
    high, wide, rows, cols, stride = geometry(meta, n)
    start = pl.multiple_of(meta[2, n], 16)
    used = stride * rows

    @pl.when(n == 0)
    def _():
        for copy in fetch_shards(meta, att_mine, att_other, att_scr, sems):
            copy.wait()
        unpack_qkv(att_scr, wqkv_scr)

    def body(size):
        valid = slot_valid((size, 1), 0, stride, rows, cols)
        pooled = jnp.where(valid, hat[0, :size, :] * gains[0:1, :] + gains[1:2, :], 0.0)
        qkvt[0, :, :size] = mm(wqkv_scr[...], pooled.astype(BF), NT).astype(BF)
        lane_ok = slot_valid((1, size), 1, stride, rows, cols)
        first_row = iota((16, size), 0) == 0
        closed = jnp.where(first_row & ~lane_ok, -1e30, 0.0).astype(BF)
        ones = onehot(first_row)
        for head in range(HEADS):
            at = HEAD_DIM * head
            query = jnp.concatenate([qkvt[0, at : at + 32, :size], ones], axis=0)
            key = jnp.concatenate([qkvt[0, 384 + at : 416 + at, :size], closed], axis=0)
            value = qkvt[0, 768 + at : 800 + at, :size]
            if size == SMALL:
                shift = bias[0, pl.ds(table_row(head, stride), size), :]
            else:
                at_row = head * WIDE_ROWS
                shift = jnp.concatenate(
                    [bias[0, at_row : at_row + size, :], bias[1, at_row : at_row + size, : size - 128]],
                    axis=1,
                )
            scores = mm(key, query, TN) * (SCORE_SCALE * LOG2E) + shift
            expo = jnp.exp2(scores - jnp.max(scores, axis=0, keepdims=True))
            share = (expo * (1.0 / jnp.sum(expo, axis=0, keepdims=True))).astype(BF)
            probs[0, head, :size, :size] = share
            mix_scr[at : at + 32, :size] = mm(value, share).astype(BF)

        def pack(psize):
            pick = packing((psize, size), stride, rows, cols)
            mixed[pl.ds(start, psize), :] = mm(pick, mix_scr[:, :size], NT).astype(BF)

        if size == SMALL:
            pack(SMALL)
        else:
            pl.when(rows * cols <= SMALL)(functools.partial(pack, SMALL))
            pl.when(rows * cols > SMALL)(functools.partial(pack, SLOT))

    pl.when(used <= SMALL)(functools.partial(body, SMALL))
    pl.when(used > SMALL)(functools.partial(body, SLOT))

    @pl.when(n == pl.num_programs(0) - 1)
    def _():
        total = pl.multiple_of(meta[3, 0], 16)
        mixed[pl.ds(total, CHUNK), :] = jnp.zeros((CHUNK, D_OUT), BF)


def gelu_both(x):
    size = jnp.abs(x)
    t = pl.reciprocal(1.0 + (0.3275911 / math.sqrt(2.0)) * size, approx=True)
    bell = jnp.exp2((x * x) * (-0.5 * LOG2E))
    poly = t * (
        0.5 * 0.254829592
        + t
        * (
            0.5 * -0.284496736
            + t * (0.5 * 1.421413741 + t * (0.5 * -1.453152027 + t * (0.5 * 1.061405429)))
        )
    )
    tail = poly * bell
    act = jnp.maximum(x, 0.0) - size * tail
    slope = jnp.where(x > 0.0, 1.0 - tail, tail) + (x * bell) * (1.0 / math.sqrt(2.0 * math.pi))
    return act, slope


def dense_kernel(
    meta, plain, cotp, mixed, att_mine, att_other, ff_mine, ff_other, rowpar, upbias,
    outp, gmix, gplain, gff, gshort, small,
    wqs_scr, wout_scr, up_acc, down_acc, out_acc, short_acc, small_acc,
    att_scr, wff, att_sems, ff_sems,
):
    i = pl.program_id(0)

    @pl.when(i == 0)
    def _():
        ff_copies = fetch_shards(meta, ff_mine, ff_other, wff, ff_sems)
        for copy in fetch_shards(meta, att_mine, att_other, att_scr, att_sems):
            copy.wait()
        for j in range(PARTS):
            wout_scr[48 * j : 48 * j + 48, :] = att_scr[j, 0, 0:48, :]
            wqs_scr[48 * j : 48 * j + 48, :] = att_scr[j, 1, 16:64, 192:384]
        up_acc[...] = jnp.zeros_like(up_acc)
        down_acc[...] = jnp.zeros_like(down_acc)
        out_acc[...] = jnp.zeros_like(out_acc)
        short_acc[...] = jnp.zeros_like(short_acc)
        small_acc[...] = jnp.zeros_like(small_acc)
        for copy in ff_copies:
            copy.wait()

    @pl.when(i < meta[3, 3])
    def _():
        out_bias, ln_gain, ln_shift, down_bias = (rowpar[k : k + 1, :] for k in range(4))
        wout = wout_scr[...]
        wshort = wqs_scr[...]
        first = mm(plain[...], wshort, NT) + mm(mixed[...], wout, NT) + out_bias
        shifted, scale = norm_stats(first)
        hat = shifted * scale
        normed = (hat * ln_gain + ln_shift).astype(BF)
        normed_t = normed.T
        cot = cotp[...]
        cot_t = cot.T
        branch = jnp.zeros((CHUNK, D_OUT), F32)
        grad_normed = jnp.zeros((CHUNK, D_OUT), F32)
        one_rows = jnp.ones((8, CHUNK), BF)
        for j in range(4):
            wup = jnp.concatenate([wff[2 * j, 0], wff[2 * j + 1, 0]], axis=0)
            wdown = jnp.concatenate([wff[2 * j, 1], wff[2 * j + 1, 1]], axis=0)
            hidden = mm(normed, wup, NT) + upbias[0:1, 384 * j : 384 * j + 384]
            grad_act = mm(cot, wdown, NT)
            act, slope = gelu_both(hidden)
            act = act.astype(BF)
            grad_hidden = (grad_act * slope).astype(BF)
            branch += mm(act, wdown)
            grad_normed += mm(grad_hidden, wup)
            up_acc[:, 384 * j : 384 * j + 384] += mm(normed_t, grad_hidden)
            down_acc[:, 384 * j : 384 * j + 384] += mm(cot_t, act)
            small_acc[8 * (4 + j) : 8 * (5 + j), :] += mm(one_rows, grad_hidden)
        outp[...] = (first + branch + down_bias).astype(BF)
        grad_branch = cot.astype(F32)
        grad_hat = grad_normed * ln_gain
        center = jnp.mean(grad_hat, axis=-1, keepdims=True)
        along = jnp.mean(grad_hat * hat, axis=-1, keepdims=True)
        grad_first = grad_branch + scale * (grad_hat - center - hat * along)
        low = grad_first.astype(BF)
        low_t = low.T
        gmix[...] = mm(low, wout).astype(BF)
        gplain[...] = mm(low, wshort).astype(BF)
        out_acc[...] += mm(low_t, mixed[...])
        short_acc[...] += mm(low_t, plain[...])

        def fold(values):
            return jnp.sum(values.reshape(CHUNK // 8, 8, D_OUT), axis=0)

        small_acc[0:8, :] += fold(grad_first)
        small_acc[8:16, :] += fold(grad_normed * hat)
        small_acc[16:24, :] += fold(grad_normed)
        small_acc[24:32, :] += fold(grad_branch)

    @pl.when(i == meta[3, 3])
    def _():
        outp[...] = jnp.zeros_like(outp)
        gmix[...] = jnp.zeros_like(gmix)
        gplain[...] = jnp.zeros_like(gplain)

    @pl.when(i == meta[3, 3] - 1)
    def _():
        own, core = meta[3, 1], meta[3, 2]
        for j in range(PARTS):
            at = own ^ j
            gff[core, at, 0:192, :] = up_acc[:, 192 * j : 192 * j + 192].T.astype(BF)
            gff[1 - core, at, 0:192, :] = down_acc[:, 192 * j : 192 * j + 192].T.astype(BF)
            out_rows = out_acc[48 * j : 48 * j + 48, :].astype(BF)
            gff[core, at, 192:224, :] = out_rows[0:32]
            gff[1 - core, at, 192:208, :] = out_rows[32:48]
            gff[1 - core, at, 208:224, :] = jnp.zeros((16, D_OUT), BF)
        gshort[...] = short_acc[...].astype(BF)
        for k in range(8):
            total = small_acc[8 * k : 8 * k + 8, :]
            if k < 4:
                small[k : k + 1, :] = jnp.sum(total, axis=0, keepdims=True)
            else:
                small[k : k + 1, :] = total[0:1, :]


def attend_back_kernel(
    meta, hat, gains, att_mine, att_other, qkvt, probs, gmix, gplain, outp, gshort,
    grads, out, gqs, small,
    wqkv_scr, gqkv_scr, wqkv_acc, table_acc, small_acc, shift_scr, att_scr, sems,
):
    n = pl.program_id(0)
    high, wide, rows, cols, stride = geometry(meta, n)
    start = pl.multiple_of(meta[2, n], 16)
    used = stride * rows

    @pl.when(n == 0)
    def _():
        for copy in fetch_shards(meta, att_mine, att_other, att_scr, sems):
            copy.wait()
        unpack_qkv(att_scr, wqkv_scr)
        wqkv_acc[...] = jnp.zeros_like(wqkv_acc)
        table_acc[...] = jnp.zeros_like(table_acc)
        small_acc[...] = jnp.zeros_like(small_acc)

    def body(size, psize):
        pick = packing((psize, size), stride, rows, cols)
        gmt = mm(gmix[pl.ds(start, psize), :], pick, TN).astype(BF)
        for head in range(HEADS):
            at = HEAD_DIM * head
            query = qkvt[0, at : at + 32, :size]
            key = qkvt[0, 384 + at : 416 + at, :size]
            value = qkvt[0, 768 + at : 800 + at, :size]
            grad_mix = gmt[at : at + 32, :]
            share = probs[0, head, :size, :size]
            wide_share = share.astype(F32)
            grad_share = mm(value, grad_mix, TN)
            inner = jnp.sum(wide_share * grad_share, axis=0, keepdims=True)
            grad_scores = wide_share * (grad_share - inner)
            if size == SMALL:
                table_acc[0, pl.ds(table_row(head, stride), size), :] += grad_scores
            else:
                at_row = head * WIDE_ROWS
                table_acc[0, at_row : at_row + size, :] += grad_scores[:, :128]
                table_acc[1, at_row : at_row + size, : size - 128] += grad_scores[:, 128:]
            low = grad_scores.astype(BF)
            gqkv_scr[at : at + 32, :size] = (mm(key, low) * SCORE_SCALE).astype(BF)
            gqkv_scr[384 + at : 416 + at, :size] = (mm(query, low, NT) * SCORE_SCALE).astype(BF)
            gqkv_scr[768 + at : 800 + at, :size] = mm(grad_mix, share, NT).astype(BF)
        valid = slot_valid((size, 1), 0, stride, rows, cols)
        hat_rows = hat[0, :size, :]
        pooled = jnp.where(valid, hat_rows * gains[0:1, :] + gains[1:2, :], 0.0)
        gqkv = gqkv_scr[:, :size]
        wqkv_acc[...] += mm(gqkv, pooled.astype(BF))
        grad_pooled = jnp.where(valid, mm(gqkv, wqkv_scr[...], TN), 0.0)
        gain_rows = grad_pooled * hat_rows
        small_acc[0:8, :] += jnp.sum(gain_rows.reshape(size // 8, 8, D_IN), axis=0)
        small_acc[8:16, :] += jnp.sum(grad_pooled.reshape(size // 8, 8, D_IN), axis=0)
        row, col = cell_of(iota((size, 1), 0), stride)
        count = jnp.where(2 * row + 1 < high, 2.0, 1.0) * jnp.where(2 * col + 1 < wide, 2.0, 1.0)
        part = 1.0 / count
        grad_hat = grad_pooled * gains[0:1, :] * part
        grad_hat = grad_hat - jnp.mean(grad_hat, axis=-1, keepdims=True)
        spread = unpacking((size, psize), stride, rows, cols)
        grads[0, :size, 0:192] = grad_hat.astype(BF)
        grads[0, :size, 256:448] = (mm(spread, gplain[pl.ds(start, psize), :]) * part).astype(BF)
        spread = unpacking((TOK, psize), GRID, rows, cols)
        out[0] = mm(spread, outp[pl.ds(start, psize), :]).astype(BF)

    grads[...] = jnp.zeros_like(grads)
    pl.when(used <= SMALL)(functools.partial(body, SMALL, SMALL))
    pl.when(used > SMALL)(functools.partial(body, SLOT, SLOT))

    @pl.when(n == pl.num_programs(0) - 1)
    def _():
        own, core = meta[3, 1], meta[3, 2]
        for j in range(PARTS):
            at = own ^ j
            rows_j = [wqkv_acc[144 * j + 48 * k : 144 * j + 48 * k + 48, :] for k in range(3)]
            gqs[core, at, :, 0:192] = rows_j[0].astype(BF)
            gqs[1 - core, at, :, 0:192] = rows_j[1].astype(BF)
            gqs[core, at, :, 192:384] = rows_j[2].astype(BF)
            gqs[1 - core, at, :, 192:384] = gshort[48 * j : 48 * j + 48, :]
        by_shift = jnp.zeros((192, 384), F32)
        for cell in range(GRID):
            pick = shift_map(cell, GRID, 256)
            top, rest = split_two(
                jnp.concatenate(
                    [table_acc[k, pl.ds(cell, 192, stride=GRID), :] for k in range(2)], axis=1
                )
            )
            by_shift += mm(top, pick, NT) + mm(rest, pick, NT)
        for cell in range(8):
            pick = shift_map(cell, 8, 128)
            top, rest = split_two(
                table_acc[0, pl.ds(HEADS * WIDE_ROWS + cell, 192, stride=8), :]
            )
            by_shift += mm(top, pick, NT) + mm(rest, pick, NT)
        shift_scr[...] = jnp.zeros_like(shift_scr)
        for k in range(3):
            shift_scr[k, 0:192, :] = by_shift[:, 128 * k : 128 * k + 128]
        table = jnp.zeros((16, 768), F32)
        for r in range(GRID):
            rows_r = jnp.concatenate(
                [shift_scr[k, pl.ds(r, 16, stride=16), :] for k in range(6)], axis=1
            )
            table += pltpu.roll(rows_r, SIDE * (GRID - 1 - r), 1)
        small[...] = jnp.zeros_like(small)
        small[0:1, 0:192] = jnp.sum(small_acc[0:8, :], axis=0, keepdims=True)
        small[0:1, 192:384] = jnp.sum(small_acc[8:16, :], axis=0, keepdims=True)
        small[8:24, :] = table[:, 0:384]
        small[24:40, :] = table[:, 384:768]


def front_back_kernel(meta, img, grads, out):
    n = pl.program_id(0)
    high, wide, rows, cols, stride = geometry(meta, n)
    spot = iota((STRIP, 1), 0)
    prow = (spot >= 28).astype(jnp.int32) + (spot >= 56) + (spot >= 84)
    pcol = spot - 28 * prow
    token = jnp.where(pcol < wide, (prow >> 1) * stride + (pcol >> 1), -4096)

    def strip(i):
        pixels = img[0, STRIP * i : STRIP * (i + 1), :].astype(F32)
        shifted, scale = norm_stats(pixels)
        normed = shifted * scale
        goal = jnp.where(prow + 4 * i < high, token + 2 * stride * i, -1)
        pick = onehot(iota((STRIP, SLOT), 1) == goal)
        spread = mm(pick, grads[0, :SLOT, :])
        grad_hat = spread[:, 0:192]
        along = jnp.mean(grad_hat * normed, axis=-1, keepdims=True)
        full = scale * (grad_hat - normed * along) + spread[:, 256:448]
        out[0, STRIP * i : STRIP * (i + 1), :] = full.astype(BF)

    def blank(i):
        out[0, STRIP * i : STRIP * (i + 1), :] = jnp.zeros((STRIP, D_IN), BF)

    for i in range(7):
        if i < 2:
            strip(i)
        else:
            pl.when(4 * i < high)(functools.partial(strip, i))
            pl.when(4 * i >= high)(functools.partial(blank, i))


def per_image(*tail):
    return pl.BlockSpec((1,) + tail, lambda n, *_: (n,) + (0,) * len(tail))


def whole(*shape):
    return pl.BlockSpec(shape, lambda n, *_: (0,) * len(shape))


def call(kernel, grid, in_specs, out_specs, out_shape, scratch, name, *args):
    return pl.pallas_call(
        kernel,
        grid_spec=pltpu.PrefetchScalarGridSpec(
            num_scalar_prefetch=1,
            grid=grid,
            in_specs=in_specs,
            out_specs=out_specs,
            scratch_shapes=scratch,
        ),
        out_shape=out_shape,
        compiler_params=pltpu.CompilerParams(
            dimension_semantics=("arbitrary",), vmem_limit_bytes=56 * 2**20
        ),
        name=name,
    )(*args)


def shape_of(*dims, dtype=BF):
    return jax.ShapeDtypeStruct(dims, dtype)


def mask_meta(token_mask, own, core):
    count = token_mask.shape[0]
    cells = token_mask.reshape(count, 2 * GRID, 2 * GRID)
    high = jnp.sum(cells[:, :, 0], axis=1)
    wide = jnp.sum(cells[:, 0, :], axis=1)
    tokens = ((high + 1) >> 1) * ((wide + 1) >> 1)
    taken = ((tokens + 15) >> 4) << 4
    order = jnp.arange(count)
    start = jnp.sum(jnp.where(order[None, :] < order[:, None], taken[None, :], 0), axis=1)
    total = jnp.sum(taken)
    chunks = (total + CHUNK - 1) // CHUNK
    extra = jnp.select([order == 0, order == 1, order == 2], [total, own, core], chunks)
    return jnp.stack([high, wide, start, extra]).astype(jnp.int32)


def device_front(meta, images, rel_table, cotangent):
    count = images.shape[0]
    packed = count * SLOT + CHUNK
    table = jnp.pad(rel_table, ((0, 4), (0, 768 - SIDE * SIDE)))
    return call(
        front_kernel,
        (count,),
        [per_image(PIX, D_IN), per_image(TOK, D_OUT), whole(16, 768)],
        [
            per_image(SLOT, D_IN),
            whole(packed, D_IN),
            whole(packed, D_OUT),
            whole(2, BIAS_ROWS, 128),
        ],
        [
            shape_of(count, SLOT, D_IN, dtype=F32),
            shape_of(packed, D_IN),
            shape_of(packed, D_OUT),
            shape_of(2, BIAS_ROWS, 128, dtype=F32),
        ],
        [pltpu.VMEM((SLOT, D_IN), F32), pltpu.VMEM((3, 192, 128), F32)],
        "front",
        meta,
        images,
        cotangent,
        table,
    )


def device_attend(meta, hat, gains, att, bias):
    count = hat.shape[0]
    packed = count * SLOT + CHUNK
    return call(
        attend_kernel,
        (count,),
        [
            per_image(SLOT, D_IN),
            whole(2, D_IN),
            pl.BlockSpec(memory_space=pl.ANY),
            pl.BlockSpec(memory_space=pl.ANY),
            whole(2, BIAS_ROWS, 128),
        ],
        [per_image(3 * D_OUT, SLOT), per_image(HEADS, SLOT, SLOT), whole(packed, D_OUT)],
        [
            shape_of(count, 3 * D_OUT, SLOT),
            shape_of(count, HEADS, SLOT, SLOT),
            shape_of(packed, D_OUT),
        ],
        [
            pltpu.VMEM((3 * D_OUT, D_IN), BF),
            pltpu.VMEM((D_OUT, SLOT), BF),
            pltpu.VMEM((PARTS, 2, 80, 384), BF),
            pltpu.SemaphoreType.DMA((16,)),
        ],
        "attend",
        meta,
        hat,
        gains,
        *att,
        bias,
    )


def device_dense(meta, plain, cotp, mixed, att, ff, rowpar, upbias):
    packed = plain.shape[0]
    rows_of = lambda width: pl.BlockSpec(
        (CHUNK, width), lambda n, meta: (jnp.minimum(n, meta[3, 3]), 0)
    )
    return call(
        dense_kernel,
        (packed // CHUNK,),
        [
            rows_of(D_IN),
            rows_of(D_OUT),
            rows_of(D_OUT),
            pl.BlockSpec(memory_space=pl.ANY),
            pl.BlockSpec(memory_space=pl.ANY),
            pl.BlockSpec(memory_space=pl.ANY),
            pl.BlockSpec(memory_space=pl.ANY),
            whole(8, D_OUT),
            whole(1, FF),
        ],
        [
            rows_of(D_OUT),
            rows_of(D_OUT),
            rows_of(D_IN),
            whole(2, PARTS, 224, 384),
            whole(D_OUT, D_IN),
            whole(8, D_OUT),
        ],
        [
            shape_of(packed, D_OUT),
            shape_of(packed, D_OUT),
            shape_of(packed, D_IN),
            shape_of(2, PARTS, 224, 384),
            shape_of(D_OUT, D_IN),
            shape_of(8, D_OUT, dtype=F32),
        ],
        [
            pltpu.VMEM((D_OUT, D_IN), BF),
            pltpu.VMEM((D_OUT, D_OUT), BF),
            pltpu.VMEM((D_OUT, FF), F32),
            pltpu.VMEM((D_OUT, FF), F32),
            pltpu.VMEM((D_OUT, D_OUT), F32),
            pltpu.VMEM((D_OUT, D_IN), F32),
            pltpu.VMEM((64, D_OUT), F32),
            pltpu.VMEM((PARTS, 2, 80, 384), BF),
            pltpu.VMEM((PARTS, 2, 192, 384), BF),
            pltpu.SemaphoreType.DMA((16,)),
            pltpu.SemaphoreType.DMA((16,)),
        ],
        "dense",
        meta,
        plain,
        cotp,
        mixed,
        *att,
        *ff,
        rowpar,
        upbias,
    )


def device_attend_back(meta, hat, gains, att, qkvt, probs, gmix, gplain, outp, gshort):
    count = hat.shape[0]
    packed = gmix.shape[0]
    return call(
        attend_back_kernel,
        (count,),
        [
            per_image(SLOT, D_IN),
            whole(2, D_IN),
            pl.BlockSpec(memory_space=pl.ANY),
            pl.BlockSpec(memory_space=pl.ANY),
            per_image(3 * D_OUT, SLOT),
            per_image(HEADS, SLOT, SLOT),
            whole(packed, D_OUT),
            whole(packed, D_IN),
            whole(packed, D_OUT),
            whole(D_OUT, D_IN),
        ],
        [
            per_image(SLOT, 512),
            per_image(TOK, D_OUT),
            whole(2, PARTS, 48, 384),
            whole(40, 384),
        ],
        [
            shape_of(count, SLOT, 512),
            shape_of(count, TOK, D_OUT),
            shape_of(2, PARTS, 48, 384),
            shape_of(40, 384, dtype=F32),
        ],
        [
            pltpu.VMEM((3 * D_OUT, D_IN), BF),
            pltpu.VMEM((3 * D_OUT, SLOT), BF),
            pltpu.VMEM((3 * D_OUT, D_IN), F32),
            pltpu.VMEM((2, BIAS_ROWS, 128), F32),
            pltpu.VMEM((16, D_IN), F32),
            pltpu.VMEM((6, 256, 128), F32),
            pltpu.VMEM((PARTS, 2, 80, 384), BF),
            pltpu.SemaphoreType.DMA((16,)),
        ],
        "attend_back",
        meta,
        hat,
        gains,
        *att,
        qkvt,
        probs,
        gmix,
        gplain,
        outp,
        gshort,
    )


def device_front_back(meta, images, grads):
    count = images.shape[0]
    return call(
        front_back_kernel,
        (count,),
        [per_image(PIX, D_IN), per_image(SLOT, 512)],
        [per_image(PIX, D_IN)],
        [shape_of(count, PIX, D_IN)],
        [],
        "front_back",
        meta,
        images,
        grads,
    )[0]


def wire_weights(w_short, w_qkv, w_out, w_up, w_down):
    qs = jnp.concatenate([w_qkv.T, w_short.T], axis=0)
    half = qs.shape[0] // 2
    qs = jnp.concatenate([qs[:half], qs[half:]], axis=1)
    att = jnp.concatenate([w_out.T, qs, jnp.zeros((16, 384), F32)], axis=0)
    ff = jnp.stack([w_up.T, w_down])
    return att.reshape(2, 80, 384).astype(BF), ff.astype(BF)


def shard_grads(ff, qs):
    g_up, g_down = ff[0, :192].T, ff[1, :192]
    g_out = jnp.concatenate([ff[0, 192:224], ff[1, 192:208]], axis=0).T
    g_qkv = jnp.concatenate([qs[0, :, :192], qs[1, :, :192], qs[0, :, 192:]], axis=0).T
    g_short = qs[1, :, 192:].T
    return g_short, g_qkv, g_out, g_up, g_down


class FastLinks:
    def __init__(self):
        self.own = lax.axis_index("wide")
        self.core = lax.axis_index("narrow") % 2

    def across(self, value, bit):
        return lax.ppermute(value, "narrow", [(i, i ^ bit) for i in range(4)])

    def along(self, value, bits):
        return lax.ppermute(value, "wide", [(i, i ^ bits) for i in range(PARTS)])

    def pick(self, pair, which):
        return lax.dynamic_index_in_dim(pair, which, 0, keepdims=False)

    def gather(self, halves):
        own = self.pick(halves, self.core)
        mine = jnp.stack([own] + [self.along(own, d) for d in range(1, PARTS)])
        return mine, self.across(mine, 1)

    def both_halves(self, value):
        other = self.across(value, 1)
        return jnp.where(self.core == 0, jnp.stack([value, other]), jnp.stack([other, value]))

    def tree(self, parts):
        while len(parts) > 1:
            parts = [parts[k] + parts[k + 1] for k in range(0, len(parts), 2)]
        return parts[0]

    def reduce_shards(self, partial):
        got = self.across(partial[1], 1)
        terms = [
            (partial[0, d].astype(F32) + got[d].astype(F32)).astype(BF) for d in range(PARTS)
        ]
        terms = [terms[0]] + [self.along(terms[d], d) for d in range(1, PARTS)]
        total = self.tree([term.astype(F32) for term in terms]).astype(BF)
        total = total.astype(F32) + self.across(total, 2).astype(F32)
        return self.both_halves(total)

    def reduce_all(self, value):
        value = value + self.across(value, 1)
        value = self.tree([value] + [self.along(value, d) for d in range(1, PARTS)])
        return value + self.across(value, 2)


class PlainLinks:
    own = 0
    core = 0

    def gather_weights(self, w_short, w_qkv, w_out, w_up, w_down):
        full = [
            lax.all_gather(w.astype(BF), "wide", axis=axis, tiled=True)
            for w, axis in ((w_short, 1), (w_qkv, 1), (w_out, 1), (w_up, 1), (w_down, 0))
        ]

        def cut(w, j, axis):
            size = w.shape[axis] // PARTS
            return lax.slice_in_dim(w, j * size, (j + 1) * size, axis=axis)

        parts = [
            wire_weights(*(cut(w, j, axis) for w, axis in zip(full, (1, 1, 1, 1, 0))))
            for j in range(PARTS)
        ]
        return tuple(
            (jnp.stack([p[k][0] for p in parts]), jnp.stack([p[k][1] for p in parts]))
            for k in range(2)
        )

    def reduce_grads(self, gff, gqs):
        parts = [shard_grads(gff[:, j], gqs[:, j]) for j in range(PARTS)]
        out = []
        for k, axis in enumerate((1, 1, 1, 1, 0)):
            whole_grad = jnp.concatenate([p[k] for p in parts], axis=axis)
            shard = lax.psum_scatter(whole_grad, "wide", scatter_dimension=axis, tiled=True)
            out.append(lax.psum(shard, "narrow").astype(F32))
        return out


def shards(
    fast, images, token_mask, w_short, w_qkv, w_out, w_up, w_down, ln1_gain, ln1_shift, out_bias,
    ln2_gain, ln2_shift, up_bias, down_bias, rel_table, cotangent,
):
    links = FastLinks() if fast else PlainLinks()
    meta = mask_meta(token_mask, links.own, links.core)
    if fast:
        att, ff = wire_weights(w_short, w_qkv, w_out, w_up, w_down)
        att = links.gather(att)
        ff = links.gather(ff)
    else:
        att, ff = links.gather_weights(w_short, w_qkv, w_out, w_up, w_down)
    gains = jnp.stack([ln1_gain, ln1_shift])
    rowpar = jnp.stack([out_bias, ln2_gain, ln2_shift, down_bias] + [down_bias] * 4)
    hat, plain, cotp, bias = device_front(meta, images, rel_table, cotangent)
    qkvt, probs, mixed = device_attend(meta, hat, gains, att, bias)
    outp, gmix, gplain, gff, gshort, small_dense = device_dense(
        meta, plain, cotp, mixed, att, ff, rowpar, up_bias[None]
    )
    grads, output, gqs, small_attend = device_attend_back(
        meta, hat, gains, att, qkvt, probs, gmix, gplain, outp, gshort
    )
    grad_images = device_front_back(meta, images, grads)
    small = jnp.concatenate([small_dense, small_attend], axis=0)
    if fast:
        weights = shard_grads(links.reduce_shards(gff), links.reduce_shards(gqs))
        small = links.reduce_all(small)
    else:
        weights = links.reduce_grads(gff, gqs)
        small = lax.psum(small, ("wide", "narrow"))
    table = jnp.concatenate([small[16 : 16 + HEADS], small[32 : 32 + HEADS]], axis=1)
    return (
        output,
        grad_images,
        *weights,
        small[8, :192],
        small[8, 192:],
        small[0],
        small[1],
        small[2],
        small[4:8].reshape(FF),
        small[3],
        table[:, : SIDE * SIDE],
    )


def solution(mesh):
    data = ("wide", "narrow")
    rows = P(None, "wide")
    in_specs = (
        (P(data, None, None), P(data, None), rows, rows, rows, rows, P("wide", None))
        + (P(),) * 8
        + (P(data, None, None),)
    )
    out_specs = (
        (P(data, None, None), P(data, None, None), rows, rows, rows, rows, P("wide", None))
        + (P(),) * 8
    )
    fast = mesh.shape["wide"] == PARTS and mesh.shape["narrow"] == 4
    return jax.shard_map(
        functools.partial(shards, fast),
        mesh=mesh,
        in_specs=in_specs,
        out_specs=out_specs,
        check_vma=False,
    )
```

```python
import functools
import math

import jax
import jax.numpy as jnp
from jax import lax
from jax.experimental import pallas as pl
from jax.experimental.pallas import tpu as pltpu
from jax.sharding import PartitionSpec as P

D_IN = 192
D_OUT = 384
HEADS = 12
HEAD_DIM = 32
FF = 1536
GRID = 14
SIDE = 2 * GRID - 1
TOK = GRID * GRID
PIX = 4 * TOK
EPS = 1e-05
LOG2E = math.log2(math.e)
SCORE_SCALE = HEAD_DIM ** (-0.5)

SLOT = 208
SMALL = 128
LARGE = 256
WIDE_ROWS = 16 * GRID
NARROW_ROWS = 16 * 8
BIAS_ROWS = HEADS * (WIDE_ROWS + NARROW_ROWS)
CHUNK = 256
PARTS = 8
BF = jnp.bfloat16
F32 = jnp.float32
NN = (((1,), (0,)), ((), ()))
NT = (((1,), (1,)), ((), ()))
TN = (((0,), (0,)), ((), ()))


def mm(left, right, dims=NN):
    return lax.dot_general(left, right, dims, preferred_element_type=F32)


def iota(shape, dim):
    return lax.broadcasted_iota(jnp.int32, shape, dim)


def geometry(meta, n):
    high, wide = meta[n, 0], meta[n, 1]
    rows, cols = (high + 1) >> 1, (wide + 1) >> 1
    stride = jnp.where(cols <= 8, 8, GRID)
    return high, wide, rows, cols, stride


def cell_of(index, stride):
    row = jnp.where(stride == 8, index >> 3, (index * 4682) >> 16)
    return row, index - stride * row


def packed_index(index, stride, rows, cols):
    row, col = cell_of(index, stride)
    return jnp.where((col < cols) & (row < rows), row * cols + col, -1)


def onehot(mask):
    return jnp.where(mask, 1.0, 0.0).astype(BF)


def packing(shape, stride, rows, cols):
    return onehot(iota(shape, 0) == packed_index(iota((1, shape[1]), 1), stride, rows, cols))


def unpacking(shape, stride, rows, cols):
    return onehot(iota(shape, 1) == packed_index(iota((shape[0], 1), 0), stride, rows, cols))


def split_two(values):
    high = values.astype(BF)
    return high, (values - high.astype(F32)).astype(BF)


def shift_map(cell, stride, lanes):
    spot = iota((1, lanes), 1)
    row, col = cell_of(spot, stride)
    pick = jnp.where((row < GRID) & (col < GRID), SIDE * row + col - cell + GRID - 1, -1)
    return onehot(iota((384, lanes), 0) == pick)


def token_of_pixel(shape, dim, high, wide, stride):
    spot = iota(shape, dim)
    row = (spot * 2341) >> 16
    col = spot - 28 * row
    return jnp.where((row < high) & (col < wide), (row >> 1) * stride + (col >> 1), -1)


def window_share(shape, dim, high, wide, stride):
    row, col = cell_of(iota(shape, dim), stride)
    return jnp.where(2 * row + 1 < high, 0.5, 1.0) * jnp.where(2 * col + 1 < wide, 0.5, 1.0)


def norm_stats(values, axis=0):
    center = jnp.mean(values, axis=axis, keepdims=True)
    shifted = values - center
    spread = jnp.mean(shifted * shifted, axis=axis, keepdims=True)
    return shifted, lax.rsqrt(spread + EPS)


def prepare_kernel(place, mask, short_t, qkv_t, out_t, up_t, down, meta, att, ff):
    att[0:48, :] = out_t[...].astype(BF)
    att[48:144, 0:192] = qkv_t[0:96, :].astype(BF)
    att[48:96, 192:384] = qkv_t[96:144, :].astype(BF)
    att[96:144, 192:384] = short_t[...].astype(BF)
    att[144:160, :] = jnp.zeros((16, D_OUT), BF)
    ff[0:192, :] = up_t[...].astype(BF)
    ff[192:384, :] = down[...].astype(BF)
    meta_rows(place, mask, meta)


def meta_rows(place, mask, meta):
    count = mask.shape[0]
    ones = mask[...]
    spot = iota(ones.shape, 1)
    row = (spot * 2341) >> 16
    high = jnp.sum(jnp.where(spot == 28 * row, ones, 0).astype(F32), axis=1, keepdims=True)
    wide = jnp.sum(jnp.where(spot < 28, ones, 0).astype(F32), axis=1, keepdims=True)
    high, wide = high.astype(jnp.int32), wide.astype(jnp.int32)
    taken = ((((high + 1) >> 1) * ((wide + 1) >> 1) + 15) >> 4) << 4
    across = jnp.broadcast_to(taken.astype(F32), (count, 128)).T[:count]
    order = iota((count, count), 0)
    start = jnp.sum(
        jnp.where(iota((count, count), 1) < order, across, 0.0), axis=1, keepdims=True
    ).astype(jnp.int32)
    total = jnp.sum(across, axis=1, keepdims=True).astype(jnp.int32)
    chunks = (total + CHUNK - 1) >> 8
    order = iota((count, 1), 0)
    extra = jnp.where(order == 0, total, jnp.where(order == 3, chunks, 0))
    extra = jnp.where(order == 1, place[0], jnp.where(order == 2, place[1], extra))
    lane = iota((count, 128), 1)
    meta[...] = jnp.where(
        lane == 0, high, jnp.where(lane == 1, wide, jnp.where(lane == 2, start, extra))
    )


def front_kernel(meta, img, cot, hat, plain, cotp):
    n = pl.program_id(0)
    high, wide, rows, cols, stride = geometry(meta, n)
    start = pl.multiple_of(meta[n, 2], 16)

    def pack(size, lanes, values):
        pick = packing((size, lanes), stride, rows, cols)
        plain[pl.ds(start, size), :] = mm(pick, values, NT).astype(BF)
        pick = packing((size, TOK), GRID, rows, cols)
        cotp[pl.ds(start, size), :] = mm(pick, cot[0]).astype(BF)

    def body(pixels, size):
        values = img[0, :, :pixels]
        shifted, scale = norm_stats(values.astype(F32))
        normed = (shifted * scale).astype(BF)
        pick = onehot(iota((pixels, size), 1) == token_of_pixel((pixels, 1), 0, high, wide, stride))
        share = window_share((1, size), 1, high, wide, stride)
        sums = mm(jnp.concatenate([normed, values], axis=0), pick) * share
        hat[0, :, :size] = sums[:D_IN]
        pooled = sums[D_IN:].astype(BF)
        if size == SMALL:
            pack(SMALL, size, pooled)
        else:
            pl.when(rows * cols <= SMALL)(lambda: pack(SMALL, size, pooled))
            pl.when(rows * cols > SMALL)(lambda: pack(SLOT, size, pooled))

    short = high <= 18
    large = stride * rows > SMALL
    pl.when(short)(functools.partial(body, 512, SMALL))
    pl.when(jnp.logical_not(short | large))(functools.partial(body, PIX, SMALL))
    pl.when(large)(functools.partial(body, PIX, LARGE))

    @pl.when(n == pl.num_programs(0) - 1)
    def _():
        total = pl.multiple_of(meta[0, 3], 16)
        plain[pl.ds(total, CHUNK), :] = jnp.zeros((CHUNK, D_IN), BF)
        cotp[pl.ds(total, CHUNK), :] = jnp.zeros((CHUNK, D_OUT), BF)


def tables_kernel(tab, bias, shift_scr, table_scr):
    shift_scr[...] = jnp.zeros_like(shift_scr)
    table_scr[...] = jnp.zeros_like(table_scr)
    table_scr[:HEADS, : SIDE * SIDE] = tab[...] * LOG2E
    table = table_scr[...]
    for r in range(GRID):
        moved = pltpu.roll(table, (768 - SIDE * (GRID - 1 - r)) % 768, 1)
        for k in range(3):
            shift_scr[k, pl.ds(r, HEADS, stride=16), :] = moved[
                :HEADS, 128 * k : 128 * k + 128
            ]
    top, rest = split_two(jnp.concatenate([shift_scr[k] for k in range(3)], axis=1))
    for cell in range(GRID):
        pick = shift_map(cell, GRID, 256)
        spread = mm(top, pick) + mm(rest, pick)
        for k in range(2):
            bias[k, pl.ds(cell, 192, stride=GRID), :] = spread[:, 128 * k : 128 * k + 128]
    for cell in range(8):
        pick = shift_map(cell, 8, 128)
        bias[0, pl.ds(HEADS * WIDE_ROWS + cell, 192, stride=8), :] = mm(top, pick) + mm(
            rest, pick
        )


def fetch_shards(meta, mine, other, dest, sems):
    own, narrow = meta[1, 3], meta[2, 3]
    copies = []
    for e in range(PARTS):
        source = mine if e < 4 else other
        step = (2 if e & 2 else 0) ^ (5 if e & 1 else 0) ^ (1 if e >= 4 else 0)
        copies.append(
            pltpu.make_async_copy(source.at[e & 3], dest.at[own ^ narrow ^ step], sems.at[e])
        )
    for copy in copies:
        copy.start()
    return copies


def unpack_qkv(att, qkv_scr):
    for j in range(PARTS):
        qkv_scr[144 * j : 144 * j + 96, :] = att[j, 48:144, 0:192]
        qkv_scr[144 * j + 96 : 144 * j + 144, :] = att[j, 48:96, 192:384]


def slot_valid(shape, dim, stride, rows, cols):
    row, col = cell_of(iota(shape, dim), stride)
    return (col < cols) & (row < rows)


def columns_of(gain, shift, dest):
    rows = jnp.concatenate([gain[...], shift[...], jnp.zeros((6, D_IN), F32)], axis=0)
    dest[...] = rows.T


def spread_heads(block, tail=None):
    size = block.shape[1]
    parts = []
    for j in range(4):
        rows = [block[32 * j : 32 * j + 32]]
        if j > 0:
            rows.insert(0, jnp.zeros((32 * j, size), BF))
        if j < 3:
            rows.append(jnp.zeros((96 - 32 * j, size), BF))
        if tail is not None:
            rows.append(tail)
        parts.append(jnp.concatenate(rows, axis=0))
    return jnp.concatenate(parts, axis=1)


def table_row(head, stride):
    row = jnp.where(stride == 8, HEADS * WIDE_ROWS + head * NARROW_ROWS, head * WIDE_ROWS)
    return pl.multiple_of(row, 8)


def attend_kernel(
    meta, hat, gain, shift, att_mine, att_other, bias, qkvt, probs, mixed,
    wqkv_scr, mix_scr, score_scr, att_scr, gain_scr, sems,
):
    n = pl.program_id(0)
    high, wide, rows, cols, stride = geometry(meta, n)
    start = pl.multiple_of(meta[n, 2], 16)
    used = stride * rows

    @pl.when(n == 0)
    def _():
        for copy in fetch_shards(meta, att_mine, att_other, att_scr, sems):
            copy.wait()
        unpack_qkv(att_scr, wqkv_scr)
        columns_of(gain, shift, gain_scr)

    def body(size, keys):
        lane_ok = slot_valid((1, size), 1, stride, rows, cols)
        pooled = jnp.where(lane_ok, hat[0, :, :size] * gain_scr[:, 0:1] + gain_scr[:, 1:2], 0.0)
        qkvt[0, :, :size] = mm(wqkv_scr[...], pooled.astype(BF)).astype(BF)
        first_row = iota((16, size), 0) == 0
        closed = jnp.where(first_row & ~lane_ok, -1e30, 0.0).astype(BF)
        ones = onehot(first_row)
        for g in range(3):
            key = jnp.concatenate([qkvt[0, 384 + 128 * g : 512 + 128 * g, :size], closed], axis=0)
            query = spread_heads(qkvt[0, 128 * g : 128 * g + 128, :size], ones)
            score_scr[g, :keys, : 4 * size] = mm(key.T[:keys], query)
        for head in range(HEADS):
            at = size * (head % 4)
            scores = score_scr[head // 4, :keys, at : at + size] * (SCORE_SCALE * LOG2E)
            if size == SMALL:
                scores += bias[0, pl.ds(table_row(head, stride), keys), :]
            else:
                row = head * WIDE_ROWS
                scores += jnp.concatenate(
                    [bias[0, row : row + keys, :], bias[1, row : row + keys, :]], axis=1
                )
            expo = jnp.exp2(scores - jnp.max(scores, axis=0, keepdims=True))
            share = expo * (1.0 / jnp.sum(expo, axis=0, keepdims=True))
            probs[0, head, :keys, :size] = share.astype(BF)
        for head in range(HEADS):
            at = HEAD_DIM * head
            value = qkvt[0, 768 + at : 800 + at, :keys]
            mix_scr[at : at + 32, :size] = mm(value, probs[0, head, :keys, :size]).astype(BF)

        def pack(psize):
            pick = packing((psize, size), stride, rows, cols)
            mixed[pl.ds(start, psize), :] = mm(pick, mix_scr[:, :size], NT).astype(BF)

        if size == SMALL:
            pack(SMALL)
        else:
            pl.when(rows * cols <= SMALL)(functools.partial(pack, SMALL))
            pl.when(rows * cols > SMALL)(functools.partial(pack, SLOT))

    pl.when(used <= SMALL)(functools.partial(body, SMALL, SMALL))
    pl.when(used > SMALL)(functools.partial(body, LARGE, SLOT))

    @pl.when(n == pl.num_programs(0) - 1)
    def _():
        total = pl.multiple_of(meta[0, 3], 16)
        mixed[pl.ds(total, CHUNK), :] = jnp.zeros((CHUNK, D_OUT), BF)


def gelu_both(x):
    size = jnp.abs(x)
    t = pl.reciprocal(1.0 + (0.3275911 / math.sqrt(2.0)) * size, approx=True)
    bell = jnp.exp2((x * x) * (-0.5 * LOG2E))
    poly = t * (
        0.5 * 0.254829592
        + t
        * (
            0.5 * -0.284496736
            + t * (0.5 * 1.421413741 + t * (0.5 * -1.453152027 + t * (0.5 * 1.061405429)))
        )
    )
    tail = poly * bell
    act = jnp.maximum(x, 0.0) - size * tail
    slope = jnp.where(x > 0.0, 1.0 - tail, tail) + (x * bell) * (1.0 / math.sqrt(2.0 * math.pi))
    return act, slope


def dense_kernel(
    meta, plain, cotp, mixed, att_mine, att_other, ff_mine, ff_other,
    outbias, gain, shift, downbias, upbias,
    outp, gmix, gplain, gff, gshort, small,
    wqs_scr, wout_scr, up_acc, down_acc, out_acc, short_acc, small_acc,
    att_scr, wff, att_sems, ff_sems,
):
    i = pl.program_id(0)

    @pl.when(i == 0)
    def _():
        ff_copies = fetch_shards(meta, ff_mine, ff_other, wff, ff_sems)
        for copy in fetch_shards(meta, att_mine, att_other, att_scr, att_sems):
            copy.wait()
        for j in range(PARTS):
            wout_scr[48 * j : 48 * j + 48, :] = att_scr[j, 0:48, :]
            wqs_scr[48 * j : 48 * j + 48, :] = att_scr[j, 96:144, 192:384]
        up_acc[...] = jnp.zeros_like(up_acc)
        down_acc[...] = jnp.zeros_like(down_acc)
        out_acc[...] = jnp.zeros_like(out_acc)
        short_acc[...] = jnp.zeros_like(short_acc)
        small_acc[...] = jnp.zeros_like(small_acc)
        for copy in ff_copies:
            copy.wait()

    @pl.when(i < meta[3, 3])
    def _():
        out_bias, ln_gain, ln_shift, down_bias = outbias[...], gain[...], shift[...], downbias[...]
        wout = wout_scr[...]
        wshort = wqs_scr[...]
        first = mm(plain[...], wshort, NT) + mm(mixed[...], wout, NT) + out_bias
        shifted, scale = norm_stats(first, -1)
        hat = shifted * scale
        normed = (hat * ln_gain + ln_shift).astype(BF)
        normed_t = normed.T
        cot = cotp[...]
        cot_t = cot.T
        branch = jnp.zeros((CHUNK, D_OUT), F32)
        grad_normed = jnp.zeros((CHUNK, D_OUT), F32)
        one_rows = jnp.ones((8, CHUNK), BF)
        for j in range(4):
            wup = jnp.concatenate([wff[2 * j, 0:192], wff[2 * j + 1, 0:192]], axis=0)
            wdown = jnp.concatenate([wff[2 * j, 192:384], wff[2 * j + 1, 192:384]], axis=0)
            hidden = mm(normed, wup, NT) + upbias[0:1, 384 * j : 384 * j + 384]
            grad_act = mm(cot, wdown, NT)
            act, slope = gelu_both(hidden)
            act = act.astype(BF)
            grad_hidden = (grad_act * slope).astype(BF)
            branch += mm(act, wdown)
            grad_normed += mm(grad_hidden, wup)
            up_acc[:, 384 * j : 384 * j + 384] += mm(normed_t, grad_hidden)
            down_acc[:, 384 * j : 384 * j + 384] += mm(cot_t, act)
            small_acc[8 * (4 + j) : 8 * (5 + j), :] += mm(one_rows, grad_hidden)
        outp[...] = (first + branch + down_bias).astype(BF)
        grad_branch = cot.astype(F32)
        grad_hat = grad_normed * ln_gain
        center = jnp.mean(grad_hat, axis=-1, keepdims=True)
        along = jnp.mean(grad_hat * hat, axis=-1, keepdims=True)
        grad_first = grad_branch + scale * (grad_hat - center - hat * along)
        low = grad_first.astype(BF)
        low_t = low.T
        gmix[...] = mm(low, wout).astype(BF)
        gplain[...] = mm(low, wshort).astype(BF)
        out_acc[...] += mm(low_t, mixed[...])
        short_acc[...] += mm(low_t, plain[...])

        def fold(values):
            return jnp.sum(values.reshape(CHUNK // 8, 8, D_OUT), axis=0)

        small_acc[0:8, :] += fold(grad_first)
        small_acc[8:16, :] += fold(grad_normed * hat)
        small_acc[16:24, :] += fold(grad_normed)
        small_acc[24:32, :] += fold(grad_branch)

    @pl.when(i == meta[3, 3])
    def _():
        outp[...] = jnp.zeros_like(outp)
        gmix[...] = jnp.zeros_like(gmix)
        gplain[...] = jnp.zeros_like(gplain)

    @pl.when(i == meta[3, 3] - 1)
    def _():
        own, core = meta[1, 3], meta[2, 3] & 1
        for j in range(PARTS):
            at = own ^ j
            gff[core, at, 0:192, :] = up_acc[:, 192 * j : 192 * j + 192].T.astype(BF)
            gff[1 - core, at, 0:192, :] = down_acc[:, 192 * j : 192 * j + 192].T.astype(BF)
            out_rows = out_acc[48 * j : 48 * j + 48, :].astype(BF)
            gff[core, at, 192:224, :] = out_rows[0:32]
            gff[1 - core, at, 192:208, :] = out_rows[32:48]
            gff[1 - core, at, 208:224, :] = jnp.zeros((16, D_OUT), BF)
        gshort[...] = short_acc[...].astype(BF)
        for k in range(8):
            total = small_acc[8 * k : 8 * k + 8, :]
            if k < 4:
                small[k : k + 1, :] = jnp.sum(total, axis=0, keepdims=True)
            else:
                small[k : k + 1, :] = total[0:1, :]


def expand_kernel(meta, outp, out):
    n = pl.program_id(0)
    high, wide, rows, cols, stride = geometry(meta, n)
    start = pl.multiple_of(meta[n, 2], 16)

    def body(size):
        spread = unpacking((TOK, size), GRID, rows, cols)
        out[0] = mm(spread, outp[pl.ds(start, size), :]).astype(BF)

    pl.when(rows * cols <= SMALL)(functools.partial(body, SMALL))
    pl.when(rows * cols > SMALL)(functools.partial(body, SLOT))


def attend_back_kernel(
    meta, hat, gain, shift, att_mine, att_other, qkvt, probs, gmix, gplain, gshort,
    grads, gqs, small,
    wqkv_scr, wrow_scr, gm_scr, score_scr, gs_scr, gqkv_scr, wqkv_acc, table_acc, small_acc,
    shift_scr, att_scr, gain_scr, sems,
):
    n = pl.program_id(0)
    high, wide, rows, cols, stride = geometry(meta, n)
    start = pl.multiple_of(meta[n, 2], 16)
    used = stride * rows

    @pl.when(n == 0)
    def _():
        for copy in fetch_shards(meta, att_mine, att_other, att_scr, sems):
            copy.wait()
        unpack_qkv(att_scr, wqkv_scr)
        columns_of(gain, shift, gain_scr)
        wrow_scr[...] = wqkv_scr[...].T
        wqkv_acc[...] = jnp.zeros_like(wqkv_acc)
        table_acc[...] = jnp.zeros_like(table_acc)
        small_acc[...] = jnp.zeros_like(small_acc)

    def body(size, keys, psize):
        pick = packing((psize, size), stride, rows, cols)
        gm_scr[:, :size] = mm(gmix[pl.ds(start, psize), :], pick, TN).astype(BF)
        for g in range(3):
            value = qkvt[0, 768 + 128 * g : 896 + 128 * g, :size].T[:keys]
            grad_mix = spread_heads(gm_scr[128 * g : 128 * g + 128, :size])
            score_scr[g, :keys, : 4 * size] = mm(value, grad_mix)
        for head in range(HEADS):
            at = size * (head % 4)
            share = probs[0, head, :keys, :size].astype(F32)
            grad_share = score_scr[head // 4, :keys, at : at + size]
            inner = jnp.sum(share * grad_share, axis=0, keepdims=True)
            grad_scores = share * (grad_share - inner)
            if size == SMALL:
                table_acc[0, pl.ds(table_row(head, stride), keys), :] += grad_scores
            else:
                row = head * WIDE_ROWS
                table_acc[0, row : row + keys, :] += grad_scores[:, :128]
                table_acc[1, row : row + keys, :] += grad_scores[:, 128:]
            gs_scr[head, :keys, :size] = grad_scores.astype(BF)
        for head in range(HEADS):
            at = HEAD_DIM * head
            low = gs_scr[head, :keys, :size]
            key = qkvt[0, 384 + at : 416 + at, :keys]
            query = qkvt[0, at : at + 32, :size]
            gqkv_scr[at : at + 32, :size] = (mm(key, low) * SCORE_SCALE).astype(BF)
            gqkv_scr[384 + at : 416 + at, :keys] = (mm(query, low, NT) * SCORE_SCALE).astype(BF)
            gqkv_scr[768 + at : 800 + at, :keys] = mm(
                gm_scr[at : at + 32, :size], probs[0, head, :keys, :size], NT
            ).astype(BF)
        if keys < size:
            gqkv_scr[384:, keys:size] = jnp.zeros((768, size - keys), BF)
        lane_ok = slot_valid((1, size), 1, stride, rows, cols)
        hat_cols = hat[0, :, :size]
        pooled = jnp.where(lane_ok, hat_cols * gain_scr[:, 0:1] + gain_scr[:, 1:2], 0.0)
        gqkv = gqkv_scr[:, :size]
        wqkv_acc[...] += mm(gqkv, pooled.astype(BF), NT)
        grad_pooled = jnp.where(lane_ok, mm(wrow_scr[...], gqkv), 0.0)
        gain_terms = grad_pooled * hat_cols
        for k in range(size // 128):
            small_acc[0] += gain_terms[:, 128 * k : 128 * k + 128]
            small_acc[1] += grad_pooled[:, 128 * k : 128 * k + 128]
        part = window_share((1, size), 1, high, wide, stride)
        grad_hat = grad_pooled * gain_scr[:, 0:1] * part
        grad_hat = grad_hat - jnp.mean(grad_hat, axis=0, keepdims=True)
        grads[0, 0:192, :size] = grad_hat.astype(BF)
        grads[0, 192:384, :size] = (mm(gplain[pl.ds(start, psize), :], pick, TN) * part).astype(BF)

    pl.when(used <= SMALL)(functools.partial(body, SMALL, SMALL, SMALL))
    pl.when(used > SMALL)(functools.partial(body, LARGE, SLOT, SLOT))

    @pl.when(n == pl.num_programs(0) - 1)
    def _():
        own, narrow = meta[1, 3], meta[2, 3]
        for j in range(PARTS):
            d = own ^ j
            late = d >> 2
            keeper = (d ^ (5 * late)) ^ narrow
            core, far = keeper & 1, keeper >> 1
            rows_j = [wqkv_acc[144 * j + 48 * k : 144 * j + 48 * k + 48, :] for k in range(3)]
            gqs[core, far, late, 0:48, 0:192] = rows_j[0].astype(BF)
            gqs[core, far, late, 48:96, 0:192] = rows_j[1].astype(BF)
            gqs[core, far, late, 0:48, 192:384] = rows_j[2].astype(BF)
            gqs[core, far, late, 48:96, 192:384] = gshort[48 * j : 48 * j + 48, :]
        by_shift = jnp.zeros((192, 384), F32)
        for cell in range(GRID):
            pick = shift_map(cell, GRID, 256)
            top, rest = split_two(
                jnp.concatenate(
                    [table_acc[k, pl.ds(cell, 192, stride=GRID), :] for k in range(2)], axis=1
                )
            )
            by_shift += mm(top, pick, NT) + mm(rest, pick, NT)
        for cell in range(8):
            pick = shift_map(cell, 8, 128)
            top, rest = split_two(
                table_acc[0, pl.ds(HEADS * WIDE_ROWS + cell, 192, stride=8), :]
            )
            by_shift += mm(top, pick, NT) + mm(rest, pick, NT)
        shift_scr[...] = jnp.zeros_like(shift_scr)
        for k in range(3):
            shift_scr[k, 0:192, :] = by_shift[:, 128 * k : 128 * k + 128]
        table = jnp.zeros((16, 768), F32)
        for r in range(GRID):
            rows_r = jnp.concatenate(
                [shift_scr[k, pl.ds(r, 16, stride=16), :] for k in range(6)], axis=1
            )
            table += pltpu.roll(rows_r, SIDE * (GRID - 1 - r), 1)
        small[...] = jnp.zeros_like(small)
        small[0:1, 0:192] = jnp.sum(small_acc[0].T, axis=0, keepdims=True)
        small[0:1, 192:384] = jnp.sum(small_acc[1].T, axis=0, keepdims=True)
        small[8:24, :] = table[:, 0:384]
        small[24:40, :] = table[:, 384:768]


def front_back_kernel(first, meta, img, grads, out):
    n = pl.program_id(0) + first
    high, wide, rows, cols, stride = geometry(meta, n)

    def body(pixels, size):
        shifted, scale = norm_stats(img[0, :, :pixels].astype(F32))
        normed = shifted * scale
        token = token_of_pixel((1, pixels), 1, high, wide, stride)
        spread = mm(grads[0, :, :size], onehot(iota((size, pixels), 0) == token))
        grad_hat = spread[:D_IN]
        along = jnp.mean(grad_hat * normed, axis=0, keepdims=True)
        full = scale * (grad_hat - normed * along) + spread[D_IN:]
        out[0, :, :pixels] = full.astype(BF)
        if pixels < PIX:
            out[0, :, pixels:] = jnp.zeros((D_IN, PIX - pixels), BF)

    short = high <= 18
    large = stride * rows > SMALL
    pl.when(short)(functools.partial(body, 512, SMALL))
    pl.when(jnp.logical_not(short | large))(functools.partial(body, PIX, SMALL))
    pl.when(large)(functools.partial(body, PIX, LARGE))


def per_image(*tail):
    return pl.BlockSpec((1,) + tail, lambda n, *_: (n,) + (0,) * len(tail))


def whole(*shape):
    return pl.BlockSpec(shape, lambda n, *_: (0,) * len(shape))


def call(kernel, micros, grid, in_specs, out_specs, out_shape, scratch, name, *args):
    return pl.pallas_call(
        kernel,
        grid_spec=pltpu.PrefetchScalarGridSpec(
            num_scalar_prefetch=1,
            grid=grid,
            in_specs=in_specs,
            out_specs=out_specs,
            scratch_shapes=scratch,
        ),
        out_shape=out_shape,
        compiler_params=pltpu.CompilerParams(
            dimension_semantics=("arbitrary",), vmem_limit_bytes=56 * 2**20
        ),
        name=name,
        cost_estimate=pl.CostEstimate(
            flops=micros * 10**9, bytes_accessed=micros * 10**6, transcendentals=0
        ),
    )(*args)


def shape_of(*dims, dtype=BF):
    return jax.ShapeDtypeStruct(dims, dtype)


ANY = pl.BlockSpec(memory_space=pl.ANY)
GATHERED = [ANY, ANY]


def device_prepare(place, token_mask, w_short, w_qkv, w_out, w_up, w_down):
    count = token_mask.shape[0]
    return call(
        prepare_kernel,
        3,
        (1,),
        [
            whole(count, PIX),
            whole(48, D_IN),
            whole(144, D_IN),
            whole(48, D_OUT),
            whole(192, D_OUT),
            whole(192, D_OUT),
        ],
        [whole(count, 128), whole(160, D_OUT), whole(384, D_OUT)],
        [shape_of(count, 128, dtype=jnp.int32), shape_of(160, D_OUT), shape_of(384, D_OUT)],
        [],
        "prepare",
        place,
        token_mask,
        w_short.T,
        w_qkv.T,
        w_out.T,
        w_up.T,
        w_down,
    )


def device_meta(place, token_mask):
    count = token_mask.shape[0]
    return call(
        meta_rows,
        2,
        (1,),
        [whole(count, PIX)],
        [whole(count, 128)],
        [shape_of(count, 128, dtype=jnp.int32)],
        [],
        "meta",
        place,
        token_mask,
    )[0]


def device_front(meta, images, cotangent):
    count = images.shape[0]
    packed = count * SLOT + CHUNK
    return call(
        front_kernel,
        15,
        (count,),
        [per_image(D_IN, PIX), per_image(TOK, D_OUT)],
        [per_image(D_IN, LARGE), whole(packed, D_IN), whole(packed, D_OUT)],
        [
            shape_of(count, D_IN, LARGE, dtype=F32),
            shape_of(packed, D_IN),
            shape_of(packed, D_OUT),
        ],
        [],
        "front",
        meta,
        images,
        cotangent,
    )


def device_tables(rel_table):
    return pl.pallas_call(
        tables_kernel,
        out_shape=shape_of(2, BIAS_ROWS, 128, dtype=F32),
        scratch_shapes=[pltpu.VMEM((3, 192, 128), F32), pltpu.VMEM((16, 768), F32)],
        compiler_params=pltpu.CompilerParams(vmem_limit_bytes=40 * 2**20),
        name="tables",
        cost_estimate=pl.CostEstimate(
            flops=8 * 10**9, bytes_accessed=8 * 10**6, transcendentals=0
        ),
    )(rel_table)


def device_attend(meta, hat, gain, shift, att, bias):
    count = hat.shape[0]
    packed = count * SLOT + CHUNK
    return call(
        attend_kernel,
        30,
        (count,),
        [per_image(D_IN, LARGE), whole(1, D_IN), whole(1, D_IN)]
        + GATHERED
        + [whole(2, BIAS_ROWS, 128)],
        [per_image(3 * D_OUT, LARGE), per_image(HEADS, SLOT, LARGE), whole(packed, D_OUT)],
        [
            shape_of(count, 3 * D_OUT, LARGE),
            shape_of(count, HEADS, SLOT, LARGE),
            shape_of(packed, D_OUT),
        ],
        [
            pltpu.VMEM((3 * D_OUT, D_IN), BF),
            pltpu.VMEM((D_OUT, LARGE), BF),
            pltpu.VMEM((3, SLOT, 4 * LARGE), F32),
            pltpu.VMEM((PARTS, 160, 384), BF),
            pltpu.VMEM((D_IN, 8), F32),
            pltpu.SemaphoreType.DMA((PARTS,)),
        ],
        "attend",
        meta,
        hat,
        gain,
        shift,
        *att,
        bias,
    )


def device_dense(meta, plain, cotp, mixed, att, ff, params):
    packed = plain.shape[0]
    rows_of = lambda width: pl.BlockSpec(
        (CHUNK, width), lambda n, meta: (jnp.minimum(n, meta[3, 3]), 0)
    )
    return call(
        dense_kernel,
        40,
        (packed // CHUNK,),
        [rows_of(D_IN), rows_of(D_OUT), rows_of(D_OUT)]
        + GATHERED
        + GATHERED
        + [whole(1, D_OUT)] * 4
        + [whole(1, FF)],
        [
            rows_of(D_OUT),
            rows_of(D_OUT),
            rows_of(D_IN),
            whole(2, PARTS, 224, 384),
            whole(D_OUT, D_IN),
            whole(8, D_OUT),
        ],
        [
            shape_of(packed, D_OUT),
            shape_of(packed, D_OUT),
            shape_of(packed, D_IN),
            shape_of(2, PARTS, 224, 384),
            shape_of(D_OUT, D_IN),
            shape_of(8, D_OUT, dtype=F32),
        ],
        [
            pltpu.VMEM((D_OUT, D_IN), BF),
            pltpu.VMEM((D_OUT, D_OUT), BF),
            pltpu.VMEM((D_OUT, FF), F32),
            pltpu.VMEM((D_OUT, FF), F32),
            pltpu.VMEM((D_OUT, D_OUT), F32),
            pltpu.VMEM((D_OUT, D_IN), F32),
            pltpu.VMEM((64, D_OUT), F32),
            pltpu.VMEM((PARTS, 160, 384), BF),
            pltpu.VMEM((PARTS, 384, 384), BF),
            pltpu.SemaphoreType.DMA((PARTS,)),
            pltpu.SemaphoreType.DMA((PARTS,)),
        ],
        "dense",
        meta,
        plain,
        cotp,
        mixed,
        *att,
        *ff,
        *params,
    )


def device_expand(meta, outp, count):
    return call(
        expand_kernel,
        5,
        (count,),
        [whole(*outp.shape)],
        [per_image(TOK, D_OUT)],
        [shape_of(count, TOK, D_OUT)],
        [],
        "expand",
        meta,
        outp,
    )[0]


def device_attend_back(meta, hat, gain, shift, att, qkvt, probs, gmix, gplain, gshort):
    count = hat.shape[0]
    packed = gmix.shape[0]
    return call(
        attend_back_kernel,
        40,
        (count,),
        [per_image(D_IN, LARGE), whole(1, D_IN), whole(1, D_IN)]
        + GATHERED
        + [
            per_image(3 * D_OUT, LARGE),
            per_image(HEADS, SLOT, LARGE),
            whole(packed, D_OUT),
            whole(packed, D_IN),
            whole(D_OUT, D_IN),
        ],
        [per_image(2 * D_IN, LARGE), whole(2, 2, 2, 96, 384), whole(40, 384)],
        [
            shape_of(count, 2 * D_IN, LARGE),
            shape_of(2, 2, 2, 96, 384),
            shape_of(40, 384, dtype=F32),
        ],
        [
            pltpu.VMEM((3 * D_OUT, D_IN), BF),
            pltpu.VMEM((D_IN, 3 * D_OUT), BF),
            pltpu.VMEM((D_OUT, LARGE), BF),
            pltpu.VMEM((3, SLOT, 4 * LARGE), F32),
            pltpu.VMEM((HEADS, SLOT, LARGE), BF),
            pltpu.VMEM((3 * D_OUT, LARGE), BF),
            pltpu.VMEM((3 * D_OUT, D_IN), F32),
            pltpu.VMEM((2, BIAS_ROWS, 128), F32),
            pltpu.VMEM((2, D_IN, 128), F32),
            pltpu.VMEM((6, 256, 128), F32),
            pltpu.VMEM((PARTS, 160, 384), BF),
            pltpu.VMEM((D_IN, 8), F32),
            pltpu.SemaphoreType.DMA((PARTS,)),
        ],
        "attend_back",
        meta,
        hat,
        gain,
        shift,
        *att,
        qkvt,
        probs,
        gmix,
        gplain,
        gshort,
    )


def device_front_back(meta, images, grads, first, count):
    some = lambda *tail: pl.BlockSpec(
        (1,) + tail, lambda n, *_: (n + first,) + (0,) * len(tail)
    )
    return call(
        functools.partial(front_back_kernel, first),
        count,
        (count,),
        [some(D_IN, PIX), some(2 * D_IN, LARGE)],
        [per_image(D_IN, PIX)],
        [shape_of(count, D_IN, PIX)],
        [],
        "front_back",
        meta,
        images,
        grads,
    )[0]


def shard_grads(ff, qs):
    g_up, g_down = ff[0, :192].T, ff[1, :192]
    g_out = jnp.concatenate([ff[0, 192:224], ff[1, 192:208]], axis=0).T
    g_qkv = jnp.concatenate([qs[:, :192], qs[:48, 192:]], axis=0).T
    g_short = qs[48:, 192:].T
    return g_short, g_qkv, g_out, g_up, g_down


def tied(*values):
    return lax.optimization_barrier(values)


class FastLinks:
    def __init__(self):
        self.own = lax.axis_index("wide")
        self.narrow = lax.axis_index("narrow")

    def across(self, value, bit):
        return lax.ppermute(value, "narrow", [(i, i ^ bit) for i in range(4)])

    def along(self, value, bits):
        return lax.ppermute(value, "wide", [(i, i ^ bits) for i in range(PARTS)])

    def spread(self, value, bits):
        pairs = [
            (4 * w + k, 4 * (w ^ k ^ bits) + k) for w in range(PARTS) for k in range(4)
        ]
        return lax.ppermute(value, ("wide", "narrow"), pairs)

    def fetch_two(self, value):
        return jnp.stack([self.spread(value, 0), self.spread(value, 5)])

    def both_halves(self, value):
        other = self.across(value, 1)
        first = self.narrow % 2 == 0
        return jnp.where(first, jnp.stack([value, other]), jnp.stack([other, value]))


def low_sum(left, right):
    return (left.astype(F32) + right.astype(F32)).astype(BF)


def high_sum(left, right):
    return left.astype(F32) + right.astype(F32)


def tree(parts):
    while len(parts) > 1:
        parts = [high_sum(parts[k], parts[k + 1]) for k in range(0, len(parts), 2)]
    return parts[0]


class PlainLinks:
    own = 0
    narrow = 0

    def gather_weights(self, w_short, w_qkv, w_out, w_up, w_down):
        full = [
            lax.all_gather(w.astype(BF), "wide", axis=axis, tiled=True)
            for w, axis in ((w_short, 1), (w_qkv, 1), (w_out, 1), (w_up, 1), (w_down, 0))
        ]

        def shard(j):
            short, qkv, out, up, down = (
                lax.slice_in_dim(w, j * size, (j + 1) * size, axis=axis)
                for w, size, axis in zip(full, (48, 144, 48, 192, 192), (1, 1, 1, 1, 0))
            )
            qs = jnp.concatenate([qkv.T, short.T], axis=0)
            qs = jnp.concatenate([qs[:96], qs[96:]], axis=1)
            att = jnp.concatenate([out.T, qs, jnp.zeros((16, 384), BF)], axis=0)
            return att, jnp.concatenate([up.T, down], axis=0)

        parts = [shard(j) for j in (0, 5, 2, 7, 1, 4, 3, 6)]
        return tuple(
            (jnp.stack([p[k] for p in parts[:4]]), jnp.stack([p[k] for p in parts[4:]]))
            for k in range(2)
        )

    def reduce_grads(self, gff, gqs):
        place = {0: (0, 0, 0), 5: (0, 0, 1), 1: (1, 0, 0), 4: (1, 0, 1)}
        place.update({2: (0, 1, 0), 7: (0, 1, 1), 3: (1, 1, 0), 6: (1, 1, 1)})
        parts = [shard_grads(gff[:, j], gqs[place[j]]) for j in range(PARTS)]
        out = []
        for k, axis in enumerate((1, 1, 1, 1, 0)):
            whole_grad = jnp.concatenate([p[k] for p in parts], axis=axis)
            shard = lax.psum_scatter(whole_grad, "wide", scatter_dimension=axis, tiled=True)
            out.append(lax.psum(shard, "narrow").astype(F32))
        return out


def outputs(output, grad_images, weights, small):
    table = jnp.concatenate([small[16 : 16 + HEADS], small[32 : 32 + HEADS]], axis=1)
    return (
        output,
        jnp.swapaxes(grad_images, 1, 2),
        *weights,
        small[8, :192],
        small[8, 192:],
        small[0],
        small[1],
        small[2],
        small[4:8].reshape(FF),
        small[3],
        table[:, : SIDE * SIDE],
    )


def shards_plain(
    images, token_mask, w_short, w_qkv, w_out, w_up, w_down, ln1_gain, ln1_shift, out_bias,
    ln2_gain, ln2_shift, up_bias, down_bias, rel_table, cotangent,
):
    links = PlainLinks()
    count = images.shape[0]
    images = jnp.swapaxes(images, 1, 2)
    ln1 = (ln1_gain[None], ln1_shift[None])
    params = [p[None] for p in (out_bias, ln2_gain, ln2_shift, down_bias, up_bias)]
    meta = device_meta(jnp.zeros((2,), jnp.int32), token_mask)
    att, ff = links.gather_weights(w_short, w_qkv, w_out, w_up, w_down)
    hat, plain, cotp = device_front(meta, images, cotangent)
    bias = device_tables(rel_table)
    qkvt, probs, mixed = device_attend(meta, hat, *ln1, att, bias)
    outp, gmix, gplain, gff, gshort, small_dense = device_dense(
        meta, plain, cotp, mixed, att, ff, params
    )
    output = device_expand(meta, outp, count)
    grads, gqs, small_attend = device_attend_back(
        meta, hat, *ln1, att, qkvt, probs, gmix, gplain, gshort
    )
    grad_images = device_front_back(meta, images, grads, 0, count)
    small = jnp.concatenate([small_dense, small_attend], axis=0)
    small = lax.psum(small, ("wide", "narrow"))
    return outputs(output, grad_images, links.reduce_grads(gff, gqs), small)


def shards_fast(
    images, token_mask, w_short, w_qkv, w_out, w_up, w_down, ln1_gain, ln1_shift, out_bias,
    ln2_gain, ln2_shift, up_bias, down_bias, rel_table, cotangent,
):
    links = FastLinks()
    count = images.shape[0]
    images = jnp.swapaxes(images, 1, 2)
    ln1 = (ln1_gain[None], ln1_shift[None])
    params = [p[None] for p in (out_bias, ln2_gain, ln2_shift, down_bias, up_bias)]
    place = jnp.stack([links.own, links.narrow]).astype(jnp.int32)
    meta, att, ff = device_prepare(place, token_mask, w_short, w_qkv, w_out, w_up, w_down)

    att, ff = links.fetch_two(att), links.fetch_two(ff)
    hat, plain, cotp = device_front(meta, images, cotangent)
    att, hat, rel_table = tied(att, hat, rel_table)
    att = jnp.concatenate([att, links.across(att, 2)])
    bias = device_tables(rel_table)
    att, bias, ff = tied(att, bias, ff)
    att = (att, links.across(att, 1))
    ff_more = links.across(ff, 2)
    qkvt, probs, mixed = device_attend(meta, hat, *ln1, att, bias)
    ff_more, mixed = tied(ff_more, mixed)
    ff = jnp.concatenate([ff, ff_more])
    ff = (ff, links.across(ff, 1))
    outp, gmix, gplain, gff, gshort, small_dense = device_dense(
        meta, plain, cotp, mixed, att, ff, params
    )

    got = links.across(gff[1], 1)
    output = device_expand(meta, outp, count)
    got, output, gmix = tied(got, output, gmix)
    terms = [low_sum(gff[0, d], got[d]) for d in range(PARTS)]
    far = (7, 6, 5, 4, 3)
    moved = {d: links.along(terms[d], d) for d in far}
    grads, gqs, small_attend = device_attend_back(
        meta, hat, *ln1, att, qkvt, probs, gmix, gplain, gshort
    )
    tie = tied(grads, gqs, small_attend, terms[1], terms[2], *(moved[d] for d in far))
    grads, gqs, small_attend = tie[:3]
    terms[1:] = [
        links.along(tie[3], 1), links.along(tie[4], 2), *reversed(tie[5:])
    ]
    small = jnp.concatenate([small_dense, small_attend], axis=0)
    cuts = [0, 6 * count // 16, 11 * count // 16, count]
    pieces = []

    def piece(k, source):
        pieces.append(device_front_back(meta, images, source, cuts[k], cuts[k + 1] - cuts[k]))

    got, small_got = links.across(gqs[1], 1), links.across(small, 1)
    held, small = low_sum(gqs[0], got), small + small_got
    got, small_got = links.across(held[1], 2), links.across(small, 2)
    piece(0, grads)
    got, small_got, pieces[0], grads = tied(got, small_got, pieces[0], grads)
    held, small = low_sum(held[0], got), small + small_got
    got = links.spread(held[0], 0), links.spread(held[1], 5)
    small_got = links.spread(small, 0), links.spread(small, 5)
    piece(1, grads)
    *got, pieces[1], grads = tied(*got, *small_got, pieces[1], grads)
    held, small = low_sum(got[0], got[1]), got[2] + got[3]
    ff_sum = tree(terms).astype(BF)
    got, small_got, ff_got = links.across(held, 2), links.across(small, 2), links.across(ff_sum, 2)
    piece(2, grads)
    got, small_got, ff_got, pieces[2] = tied(got, small_got, ff_got, pieces[2])
    held, small, ff_sum = high_sum(held, got), small + small_got, high_sum(ff_sum, ff_got)
    held, small = held + links.across(held, 1), small + links.across(small, 1)
    weights = shard_grads(links.both_halves(ff_sum), held)
    return outputs(output, jnp.concatenate(pieces), weights, small)


def solution(mesh):
    data = ("wide", "narrow")
    rows = P(None, "wide")
    in_specs = (
        (P(data, None, None), P(data, None), rows, rows, rows, rows, P("wide", None))
        + (P(),) * 8
        + (P(data, None, None),)
    )
    out_specs = (
        (P(data, None, None), P(data, None, None), rows, rows, rows, rows, P("wide", None))
        + (P(),) * 8
    )
    fast = mesh.shape["wide"] == PARTS and mesh.shape["narrow"] == 4
    return jax.shard_map(
        shards_fast if fast else shards_plain,
        mesh=mesh,
        in_specs=in_specs,
        out_specs=out_specs,
        check_vma=False,
    )
```

```python
import functools
import math

import jax
import jax.numpy as jnp
from jax import lax
from jax.experimental import pallas as pl
from jax.experimental.pallas import tpu as pltpu
from jax.sharding import PartitionSpec as P

D_IN = 192
D_OUT = 384
HEADS = 12
HEAD_DIM = 32
FF = 1536
GRID = 14
SIDE = 2 * GRID - 1
TOK = GRID * GRID
PIX = 4 * TOK
EPS = 1e-05
LOG2E = math.log2(math.e)
SCORE_SCALE = HEAD_DIM ** (-0.5)

SLOT = 208
SMALL = 128
LARGE = 256
WIDE_ROWS = 16 * GRID
NARROW_ROWS = 16 * 8
BIAS_ROWS = HEADS * (WIDE_ROWS + NARROW_ROWS)
CHUNK = 512
WIDTH = 512
PARTS = 8
BF = jnp.bfloat16
F32 = jnp.float32
NN = (((1,), (0,)), ((), ()))
NT = (((1,), (1,)), ((), ()))
TN = (((0,), (0,)), ((), ()))


def mm(left, right, dims=NN):
    return lax.dot_general(left, right, dims, preferred_element_type=F32)


def iota(shape, dim):
    return lax.broadcasted_iota(jnp.int32, shape, dim)


def geometry(meta, n):
    high, wide = meta[n, 0], meta[n, 1]
    rows, cols = (high + 1) >> 1, (wide + 1) >> 1
    return high, wide, rows, cols, meta[n, 6]


def cell_of(index, stride):
    row = jnp.where(stride == 8, index >> 3, (index * 4682) >> 16)
    return row, index - stride * row


def packed_index(index, stride, rows, cols):
    row, col = cell_of(index, stride)
    return jnp.where((col < cols) & (row < rows), row * cols + col, -1)


def onehot(mask):
    return jnp.where(mask, 1.0, 0.0).astype(BF)


def packing(shape, stride, rows, cols):
    return onehot(iota(shape, 0) == packed_index(iota((1, shape[1]), 1), stride, rows, cols))


def unpacking(shape, stride, rows, cols):
    return onehot(iota(shape, 1) == packed_index(iota((shape[0], 1), 0), stride, rows, cols))


def split_two(values):
    high = values.astype(BF)
    return high, (values - high.astype(F32)).astype(BF)


def shift_map(cell, stride, lanes):
    spot = iota((1, lanes), 1)
    row, col = cell_of(spot, stride)
    pick = jnp.where((row < GRID) & (col < GRID), SIDE * row + col - cell + GRID - 1, -1)
    return onehot(iota((384, lanes), 0) == pick)


def token_of_pixel(shape, dim, high, wide, stride):
    spot = iota(shape, dim)
    row = (spot * 2341) >> 16
    col = spot - 28 * row
    return jnp.where((row < high) & (col < wide), (row >> 1) * stride + (col >> 1), -1)


def window_share(shape, dim, high, wide, stride):
    row, col = cell_of(iota(shape, dim), stride)
    return jnp.where(2 * row + 1 < high, 0.5, 1.0) * jnp.where(2 * col + 1 < wide, 0.5, 1.0)


def norm_stats(values, axis=0):
    center = jnp.mean(values, axis=axis, keepdims=True)
    shifted = values - center
    spread = jnp.mean(shifted * shifted, axis=axis, keepdims=True)
    return shifted, lax.rsqrt(spread + EPS)


def prepare_kernel(place, mask, short_t, qkv_t, out_t, up_t, down, meta, att, ff):
    att[0:96, 0:192] = qkv_t[0:96, :].astype(BF)
    att[0:48, 192:384] = qkv_t[96:144, :].astype(BF)
    att[48:96, 192:384] = short_t[...].astype(BF)
    ff[0:192, :] = up_t[...].astype(BF)
    ff[192:384, :] = down[...].astype(BF)
    ff[384:432, :] = out_t[...].astype(BF)
    meta_rows(place, mask, meta)


def meta_rows(place, mask, meta):
    count = mask.shape[0]
    ones = mask[...]
    spot = iota(ones.shape, 1)
    row = (spot * 2341) >> 16
    high = jnp.sum(jnp.where(spot == 28 * row, ones, 0).astype(F32), axis=1, keepdims=True)
    wide = jnp.sum(jnp.where(spot < 28, ones, 0).astype(F32), axis=1, keepdims=True)

    def along(column):
        return jnp.broadcast_to(column, (count, 128)).T[:count]

    def total(values):
        return jnp.sum(values, axis=1, keepdims=True)

    rows = (high.astype(jnp.int32) + 1) >> 1
    cols = (wide.astype(jnp.int32) + 1) >> 1
    image = iota((count, 1), 0)
    stride = jnp.where(cols <= 8, 8, GRID)
    key = (stride * rows * count + image).astype(F32)
    rank = total(jnp.where(along(key) < key, 1.0, 0.0))
    chosen = along(rank) == image.astype(F32)

    def sort(column):
        return total(jnp.where(chosen, along(column), 0.0))

    taken = sort(((((rows * cols) + 15) >> 4) << 4).astype(F32))
    small = total(jnp.where(along(key) < SMALL * count + count, 1.0, 0.0)).astype(jnp.int32)
    start = total(jnp.where(iota((count, count), 1) < image, along(taken), 0.0))
    packed = total(along(taken)).astype(jnp.int32)
    chunks = (packed + CHUNK - 1) >> 9
    extra = jnp.where(image == 0, packed, jnp.where(image == 3, chunks, small >> 1))
    extra = jnp.where(image == 1, place[0], jnp.where(image == 2, place[1], extra))
    lane = iota((count, 128), 1)
    result = jnp.zeros((count, 128), jnp.int32)
    stride = jnp.where(image < (small >> 1) * 2, sort(stride.astype(F32)), float(GRID))
    columns = (sort(high), sort(wide), start, extra, sort(image.astype(F32)), rank, stride)
    for k, column in enumerate(columns):
        result = jnp.where(lane == k, column.astype(jnp.int32), result)
    meta[...] = result


def front_kernel(meta, img_a, img_b, cot_a, cot_b, hat, plain, cotp):
    n = pl.program_id(0)
    geo = [geometry(meta, 2 * n), geometry(meta, 2 * n + 1)]
    starts = [pl.multiple_of(meta[2 * n + k, 2], 16) for k in range(2)]

    def body(pixels, size, psize):
        sums = []
        for k, img in enumerate((img_a, img_b)):
            high, wide, rows, cols, stride = geo[k]
            values = img[0, :, :pixels]
            shifted, scale = norm_stats(values.astype(F32))
            normed = (shifted * scale).astype(BF)
            token = token_of_pixel((pixels, 1), 0, high, wide, stride)
            pick = onehot(iota((pixels, size), 1) == token)
            share = window_share((1, size), 1, high, wide, stride)
            sums.append(mm(jnp.concatenate([normed, values], axis=0), pick) * share)
        packed = []
        for k, cot in enumerate((cot_a, cot_b)):
            high, wide, rows, cols, stride = geo[k]
            hat[k, :, :size] = sums[k][:D_IN]
            pick = packing((psize, size), stride, rows, cols)
            first = mm(pick, sums[k][D_IN:].astype(BF), NT).astype(BF)
            pick = packing((psize, TOK), GRID, rows, cols)
            packed.append((first, mm(pick, cot[0]).astype(BF)))
        for k in range(2):
            plain[pl.ds(starts[k], psize), :] = packed[k][0]
            cotp[pl.ds(starts[k], psize), :] = packed[k][1]

    short = (geo[0][0] <= 18) & (geo[1][0] <= 18)
    large = geo[1][4] * geo[1][2] > SMALL
    pl.when(short & jnp.logical_not(large))(functools.partial(body, 512, SMALL, SMALL))
    pl.when(jnp.logical_not(short | large))(functools.partial(body, PIX, SMALL, SMALL))
    pl.when(large)(functools.partial(body, PIX, LARGE, SLOT))

    @pl.when(n == pl.num_programs(0) - 1)
    def _():
        total = pl.multiple_of(meta[0, 3], 16)
        plain[pl.ds(total, CHUNK), :] = jnp.zeros((CHUNK, D_IN), BF)
        cotp[pl.ds(total, CHUNK), :] = jnp.zeros((CHUNK, D_OUT), BF)


def tables_kernel(tab, bias, shift_scr, table_scr):
    shift_scr[...] = jnp.zeros_like(shift_scr)
    table_scr[...] = jnp.zeros_like(table_scr)
    table_scr[:HEADS, : SIDE * SIDE] = tab[...] * LOG2E
    table = table_scr[...]
    for r in range(GRID):
        moved = pltpu.roll(table, (768 - SIDE * (GRID - 1 - r)) % 768, 1)
        for k in range(3):
            shift_scr[k, pl.ds(r, HEADS, stride=16), :] = moved[
                :HEADS, 128 * k : 128 * k + 128
            ]
    top, rest = split_two(jnp.concatenate([shift_scr[k] for k in range(3)], axis=1))
    for cell in range(GRID):
        pick = shift_map(cell, GRID, 256)
        spread = mm(top, pick) + mm(rest, pick)
        for k in range(2):
            bias[k, pl.ds(cell, 192, stride=GRID), :] = spread[:, 128 * k : 128 * k + 128]
    for cell in range(8):
        pick = shift_map(cell, 8, 128)
        bias[0, pl.ds(HEADS * WIDE_ROWS + cell, 192, stride=8), :] = mm(top, pick) + mm(
            rest, pick
        )


def shard_at(meta, e):
    step = (2 if e & 2 else 0) ^ (5 if e & 1 else 0) ^ (1 if e >= 4 else 0)
    return meta[1, 3] ^ meta[2, 3] ^ step


def fetch_shards(meta, mine, other, dest, sems):
    copies = []
    for e in range(PARTS):
        source = mine if e < 4 else other
        copies.append(
            pltpu.make_async_copy(source.at[e & 3], dest.at[shard_at(meta, e)], sems.at[e])
        )
    for copy in copies:
        copy.start()
    return copies


def unpack_qkv(att, qkv_scr):
    for j in range(PARTS):
        qkv_scr[144 * j : 144 * j + 96, :] = att[j, 0:96, 0:192]
        qkv_scr[144 * j + 96 : 144 * j + 144, :] = att[j, 0:48, 192:384]


def slot_valid(shape, dim, stride, rows, cols):
    row, col = cell_of(iota(shape, dim), stride)
    return (col < cols) & (row < rows)


def row_of(vector):
    return vector[...].reshape(1, vector.shape[0])


def columns_of(gain, shift, dest):
    rows = jnp.concatenate(
        [row_of(gain), row_of(shift), jnp.zeros((6, D_IN), F32)], axis=0
    )
    dest[...] = rows.T


def spread_heads(block, tail=None):
    size = block.shape[1]
    parts = []
    for j in range(4):
        rows = [block[32 * j : 32 * j + 32]]
        if j > 0:
            rows.insert(0, jnp.zeros((32 * j, size), BF))
        if j < 3:
            rows.append(jnp.zeros((96 - 32 * j, size), BF))
        if tail is not None:
            rows.append(tail)
        parts.append(jnp.concatenate(rows, axis=0))
    return jnp.concatenate(parts, axis=1)


def table_row(head, stride):
    row = jnp.where(stride == 8, HEADS * WIDE_ROWS + head * NARROW_ROWS, head * WIDE_ROWS)
    return pl.multiple_of(row, 8)


def pooled_pair(geo, size, hat, gain_scr):
    lane_ok = [slot_valid((1, size), 1, g[4], g[2], g[3]) for g in geo]
    pooled = [
        jnp.where(lane_ok[k], hat[k, :, :size] * gain_scr[:, 0:1] + gain_scr[:, 1:2], 0.0)
        for k in range(2)
    ]
    return lane_ok, jnp.concatenate(pooled, axis=1).astype(BF)


def attend_kernel(
    meta, hat, gain, shift, att_mine, att_other, bias,
    qkvt_small, probs_small, qkvt_large, probs_large, mixed,
    wqkv_scr, mix_scr, score_scr, att_scr, gain_scr, bias_scr, rows_scr, sems, bias_sems, rows_sem,
):
    n = pl.program_id(0)
    fetch_bias = [
        pltpu.make_async_copy(bias.at[0], bias_scr.at[0], bias_sems.at[0]),
        pltpu.make_async_copy(
            bias.at[1, pl.ds(0, HEADS * WIDE_ROWS)],
            bias_scr.at[1, pl.ds(0, HEADS * WIDE_ROWS)],
            bias_sems.at[1],
        ),
    ]

    def put_rows(pair, size):
        first = pl.multiple_of(meta[2 * pair, 2], 16)
        return pltpu.make_async_copy(
            rows_scr.at[pair & 1, pl.ds(0, size)], mixed.at[pl.ds(first, size)], rows_sem
        )

    def wait_rows(pair):
        pl.when(pair < meta[4, 3])(lambda: put_rows(pair, 2 * SMALL).wait())
        pl.when(pair >= meta[4, 3])(lambda: put_rows(pair, 2 * SLOT).wait())

    geo = [geometry(meta, 2 * n), geometry(meta, 2 * n + 1)]
    starts = [pl.multiple_of(meta[2 * n + k, 2], 16) for k in range(2)]

    @pl.when(n == 0)
    def _():
        for copy in fetch_bias:
            copy.start()
        copies = fetch_shards(meta, att_mine, att_other, att_scr, sems)
        columns_of(gain, shift, gain_scr)
        for copy in copies:
            copy.wait()
        unpack_qkv(att_scr, wqkv_scr)
        for copy in fetch_bias:
            copy.wait()

    def body(size, keys, psize, qkvt, probs):
        lane_ok, pooled = pooled_pair(geo, size, hat, gain_scr)
        qkv = mm(wqkv_scr[...], pooled).astype(BF)
        first_row = iota((16, size), 0) == 0
        ones = onehot(first_row)
        for k in range(2):
            qkvt[k] = qkv[:, size * k : size * k + size]
        for k in range(2):
            closed = jnp.where(first_row & ~lane_ok[k], -1e30, 0.0).astype(BF)
            for g in range(3):
                key = jnp.concatenate([qkvt[k, 384 + 128 * g : 512 + 128 * g, :], closed], axis=0)
                query = spread_heads(qkvt[k, 128 * g : 128 * g + 128, :], ones)
                score_scr[k, g, :keys, : 4 * size] = mm(key.T[:keys], query)
        for head in range(HEADS):
            at = size * (head % 4)
            for k in range(2):
                scores = score_scr[k, head // 4, :keys, at : at + size] * (SCORE_SCALE * LOG2E)
                if size == SMALL:
                    scores += bias_scr[0, pl.ds(table_row(head, geo[k][4]), keys), :]
                else:
                    scores += jnp.concatenate(
                        [
                            bias_scr[j, pl.ds(table_row(head, geo[k][4]), keys), :]
                            for j in range(2)
                        ],
                        axis=1,
                    )
                expo = jnp.exp2(scores - jnp.max(scores, axis=0, keepdims=True))
                share = expo * (1.0 / jnp.sum(expo, axis=0, keepdims=True))
                probs[k, head] = share.astype(BF)
        for head in range(HEADS):
            at = HEAD_DIM * head
            for k in range(2):
                value = qkvt[k, 768 + at : 800 + at, :keys]
                mix_scr[k, at : at + 32, :size] = mm(value, probs[k, head]).astype(BF)
        packed = []
        for k in range(2):
            pick = packing((psize, size), geo[k][4], geo[k][2], geo[k][3])
            packed.append(mm(pick, mix_scr[k, :, :size], NT).astype(BF))
        slot = n & 1
        rows_scr[slot, 0:psize, :] = packed[0]
        second = pl.multiple_of(starts[1] - starts[0], 16)
        rows_scr[slot, pl.ds(second, psize), :] = packed[1]
        pl.when(n > 0)(lambda: wait_rows(n - 1))
        put_rows(n, 2 * psize).start()

    pl.when(n < meta[4, 3])(
        functools.partial(body, SMALL, SMALL, SMALL, qkvt_small, probs_small)
    )
    pl.when(n >= meta[4, 3])(functools.partial(body, LARGE, SLOT, SLOT, qkvt_large, probs_large))

    @pl.when(n == pl.num_programs(0) - 1)
    def _():
        wait_rows(n)
        total = pl.multiple_of(meta[0, 3], 16)
        rows_scr[0, 0:CHUNK, :] = jnp.zeros((CHUNK, D_OUT), BF)
        blank = pltpu.make_async_copy(
            rows_scr.at[0, pl.ds(0, CHUNK)], mixed.at[pl.ds(total, CHUNK)], rows_sem
        )
        blank.start()
        blank.wait()


def gelu_both(x):
    bell = jnp.exp2((x * x) * (-0.5 * LOG2E))
    half = 0.5 + 0.5 * lax.erf(x * math.sqrt(0.5))
    return x * half, half + (x * bell) * (1.0 / math.sqrt(2.0 * math.pi))


def dense_kernel(
    meta, plain, cotp, mixed, att_mine, att_other, ff_mine, ff_other,
    outbias, gain, shift, downbias, upbias,
    outp, gmix, gplain, gff_kept, gff_sent, gshort, small,
    wshort_scr, wout_scr, wup_scr, wdown_scr, up_acc, down_acc, out_acc, short_acc, small_acc,
    up_small, att_scr, att_sems, ff_sems,
):
    i = pl.program_id(0)

    @pl.when(i == 0)
    def _():
        ff_copies = []
        for e in range(PARTS):
            source = (ff_mine if e < 4 else ff_other).at[e & 3]
            shard = shard_at(meta, e)
            for k, (dest, low, size) in enumerate(
                ((wup_scr, 0, 192), (wdown_scr, 192, 192), (wout_scr, 384, 48))
            ):
                ff_copies.append(
                    pltpu.make_async_copy(
                        source.at[pl.ds(low, size)],
                        dest.at[pl.ds(pl.multiple_of(shard * size, 16), size)],
                        ff_sems.at[3 * e + k],
                    )
                )
        for copy in ff_copies:
            copy.start()
        for copy in fetch_shards(meta, att_mine, att_other, att_scr, att_sems):
            copy.wait()
        for j in range(PARTS):
            wshort_scr[48 * j : 48 * j + 48, :] = att_scr[j, 48:96, 192:384]
        up_acc[...] = jnp.zeros_like(up_acc)
        down_acc[...] = jnp.zeros_like(down_acc)
        out_acc[...] = jnp.zeros_like(out_acc)
        short_acc[...] = jnp.zeros_like(short_acc)
        small_acc[...] = jnp.zeros_like(small_acc)
        up_small[...] = jnp.zeros_like(up_small)
        for copy in ff_copies:
            copy.wait()

    @pl.when(i < meta[3, 3])
    def _():
        out_bias, ln_gain, ln_shift, down_bias = map(row_of, (outbias, gain, shift, downbias))
        up_bias = row_of(upbias)
        wout = wout_scr[...]
        wshort = wshort_scr[...]
        first = mm(plain[...], wshort, NT) + mm(mixed[...], wout, NT) + out_bias
        shifted, scale = norm_stats(first, -1)
        hat = shifted * scale
        normed = (hat * ln_gain + ln_shift).astype(BF)
        normed_t = normed.T
        cot = cotp[...]
        cot_t = cot.T
        branch = jnp.zeros((CHUNK, D_OUT), F32)
        grad_normed = jnp.zeros((CHUNK, D_OUT), F32)
        one_rows = jnp.ones((8, CHUNK), BF)
        for j in range(FF // WIDTH):
            some = slice(WIDTH * j, WIDTH * j + WIDTH)
            hidden = mm(normed, wup_scr[some, :], NT) + up_bias[:, some]
            grad_act = mm(cot, wdown_scr[some, :], NT)
            act, slope = gelu_both(hidden)
            act = act.astype(BF)
            grad_hidden = (grad_act * slope).astype(BF)
            branch += mm(act, wdown_scr[some, :])
            grad_normed += mm(grad_hidden, wup_scr[some, :])
            up_acc[:, some] += mm(normed_t, grad_hidden)
            down_acc[:, some] += mm(cot_t, act)
            up_small[:, some] += mm(one_rows, grad_hidden)
        outp[...] = (first + branch + down_bias).astype(BF)
        grad_branch = cot.astype(F32)
        grad_hat = grad_normed * ln_gain
        center = jnp.mean(grad_hat, axis=-1, keepdims=True)
        along = jnp.mean(grad_hat * hat, axis=-1, keepdims=True)
        grad_first = grad_branch + scale * (grad_hat - center - hat * along)
        low = grad_first.astype(BF)
        low_t = low.T
        gmix[...] = mm(low, wout).astype(BF)
        gplain[...] = mm(low, wshort).astype(BF)
        out_acc[...] += mm(low_t, mixed[...])
        short_acc[...] += mm(low_t, plain[...])

        def fold(values):
            return jnp.sum(values.reshape(CHUNK // 8, 8, D_OUT), axis=0)

        small_acc[0:8, :] += fold(grad_first)
        small_acc[8:16, :] += fold(grad_normed * hat)
        small_acc[16:24, :] += fold(grad_normed)
        small_acc[24:32, :] += fold(grad_branch)

    @pl.when(i == meta[3, 3])
    def _():
        for ref in (outp, gmix, gplain):
            ref[...] = jnp.zeros_like(ref)

    @pl.when(i == meta[3, 3] - 1)
    def _():
        own, core = meta[1, 3], meta[2, 3] & 1

        def emit(kept, sent):
            for j in range(PARTS):
                at = own ^ j
                kept[at, 0:192, :] = up_acc[:, 192 * j : 192 * j + 192].astype(BF).T
                sent[at, 0:192, :] = down_acc[:, 192 * j : 192 * j + 192].astype(BF).T
                out_rows = out_acc[48 * j : 48 * j + 48, :].astype(BF)
                kept[at, 192:224, :] = out_rows[0:32]
                sent[at, 192:208, :] = out_rows[32:48]
                sent[at, 208:224, :] = jnp.zeros((16, D_OUT), BF)

        pl.when(core == 0)(functools.partial(emit, gff_kept, gff_sent))
        pl.when(core == 1)(functools.partial(emit, gff_sent, gff_kept))
        gshort[...] = short_acc[...].astype(BF)
        for k in range(4):
            total = small_acc[8 * k : 8 * k + 8, :]
            small[k : k + 1, :] = jnp.sum(total, axis=0, keepdims=True)
            small[4 + k : 5 + k, :] = up_small[0:1, 384 * k : 384 * k + 384]


def expand_kernel(meta, outp, out):
    n = pl.program_id(0)
    at = [meta[2 * n + k, 5] for k in range(2)]
    geo = [geometry(meta, p) for p in at]

    def body(size):
        for k in range(2):
            start = pl.multiple_of(meta[at[k], 2], 16)
            spread = unpacking((TOK, size), GRID, geo[k][2], geo[k][3])
            out[k] = mm(spread, outp[pl.ds(start, size), :]).astype(BF)

    most = jnp.maximum(geo[0][2] * geo[0][3], geo[1][2] * geo[1][3])
    pl.when(most <= SMALL)(functools.partial(body, SMALL))
    pl.when(most > SMALL)(functools.partial(body, SLOT))


def attend_back_kernel(
    meta, hat, gain, shift, att_mine, att_other,
    qkvt_small, probs_small, qkvt_large, probs_large, gmix, gplain, gshort, small_dense,
    grads, gqs, small,
    wqkv_scr, wrow_scr, gm_scr, score_scr, gs_scr, gqkv_scr, wqkv_acc, table_acc, small_acc,
    shift_scr, att_scr, gain_scr, gmix_scr, gplain_scr, sems, row_sems,
):
    n = pl.program_id(0)
    slot = n & 1

    def get_rows(pair, size):
        first = pl.multiple_of(meta[2 * pair, 2], 16)
        return [
            pltpu.make_async_copy(
                source.at[pl.ds(first, size)],
                dest.at[pair & 1, pl.ds(0, size)],
                row_sems.at[pair & 1, k],
            )
            for k, (source, dest) in enumerate(((gmix, gmix_scr), (gplain, gplain_scr)))
        ]

    def start_rows(pair):
        def start(size):
            for copy in get_rows(pair, size):
                copy.start()

        pl.when(pair < meta[4, 3])(lambda: start(2 * SMALL))
        pl.when(pair >= meta[4, 3])(lambda: start(2 * SLOT))

    pl.when(n == 0)(lambda: start_rows(n))
    pl.when(n + 1 < pl.num_programs(0))(lambda: start_rows(n + 1))
    geo = [geometry(meta, 2 * n), geometry(meta, 2 * n + 1)]
    starts = [pl.multiple_of(meta[2 * n + k, 2], 16) for k in range(2)]

    @pl.when(n == 0)
    def _():
        for copy in fetch_shards(meta, att_mine, att_other, att_scr, sems):
            copy.wait()
        unpack_qkv(att_scr, wqkv_scr)
        columns_of(gain, shift, gain_scr)
        wrow_scr[...] = wqkv_scr[...].T
        wqkv_acc[...] = jnp.zeros_like(wqkv_acc)
        table_acc[...] = jnp.zeros_like(table_acc)
        small_acc[...] = jnp.zeros_like(small_acc)

    def body(size, keys, psize, qkvt, probs):
        picks = [packing((psize, size), g[4], g[2], g[3]) for g in geo]
        second = pl.multiple_of(starts[1] - starts[0], 16)
        spans = [pl.ds(0, psize), pl.ds(second, psize)]
        for copy in get_rows(n, 2 * psize):
            copy.wait()
        for k in range(2):
            gm_scr[k, :, :size] = mm(gmix_scr[slot, spans[k], :], picks[k], TN).astype(BF)
        for k in range(2):
            for g in range(3):
                value = qkvt[k, 768 + 128 * g : 896 + 128 * g, :].T[:keys]
                grad_mix = spread_heads(gm_scr[k, 128 * g : 128 * g + 128, :size])
                score_scr[k, g, :keys, : 4 * size] = mm(value, grad_mix)
        for head in range(HEADS):
            at = size * (head % 4)
            for k in range(2):
                share = probs[k, head].astype(F32)
                grad_share = score_scr[k, head // 4, :keys, at : at + size]
                inner = jnp.sum(share * grad_share, axis=0, keepdims=True)
                grad_scores = share * (grad_share - inner)
                row = table_row(head, geo[k][4])
                for j in range(size // 128):
                    table_acc[j, pl.ds(row, keys), :] += grad_scores[:, 128 * j : 128 * j + 128]
                gs_scr[k, head, :keys, :size] = grad_scores.astype(BF)
        for head in range(HEADS):
            at = HEAD_DIM * head
            for k in range(2):
                low = gs_scr[k, head, :keys, :size]
                key = qkvt[k, 384 + at : 416 + at, :keys]
                query = qkvt[k, at : at + 32, :]
                left, right = size * k, size * k + keys
                gqkv_scr[at : at + 32, left : left + size] = (mm(key, low) * SCORE_SCALE).astype(BF)
                gqkv_scr[384 + at : 416 + at, left:right] = (
                    mm(query, low, NT) * SCORE_SCALE
                ).astype(BF)
                gqkv_scr[768 + at : 800 + at, left:right] = mm(
                    gm_scr[k, at : at + 32, :size], probs[k, head], NT
                ).astype(BF)
        if keys < size:
            for k in range(2):
                gqkv_scr[384:, size * k + keys : size * k + size] = jnp.zeros(
                    (768, size - keys), BF
                )
        lane_ok, pooled = pooled_pair(geo, size, hat, gain_scr)
        gqkv = gqkv_scr[:, : 2 * size]
        wqkv_acc[...] += mm(gqkv, pooled, NT)
        grad_pooled_both = mm(wrow_scr[...], gqkv)
        for k in range(2):
            high, wide = geo[k][:2]
            if size < LARGE:
                grads[k, :, size:] = jnp.zeros((2 * D_IN, LARGE - size), BF)
            grad_pooled = jnp.where(
                lane_ok[k], grad_pooled_both[:, size * k : size * k + size], 0.0
            )
            gain_terms = grad_pooled * hat[k, :, :size]
            for j in range(size // 128):
                small_acc[0] += gain_terms[:, 128 * j : 128 * j + 128]
                small_acc[1] += grad_pooled[:, 128 * j : 128 * j + 128]
            part = window_share((1, size), 1, high, wide, geo[k][4])
            grad_hat = grad_pooled * gain_scr[:, 0:1] * part
            grad_hat = grad_hat - jnp.mean(grad_hat, axis=0, keepdims=True)
            grads[k, 0:192, :size] = grad_hat.astype(BF)
            grads[k, 192:384, :size] = (
                mm(gplain_scr[slot, spans[k], :], picks[k], TN) * part
            ).astype(BF)

    pl.when(n < meta[4, 3])(
        functools.partial(body, SMALL, SMALL, SMALL, qkvt_small, probs_small)
    )
    pl.when(n >= meta[4, 3])(functools.partial(body, LARGE, SLOT, SLOT, qkvt_large, probs_large))

    @pl.when(n == pl.num_programs(0) - 1)
    def _():
        own, narrow = meta[1, 3], meta[2, 3]
        for j in range(PARTS):
            d = own ^ j
            late = d >> 2
            keeper = (d ^ (5 * late)) ^ narrow
            core, far = keeper & 1, keeper >> 1
            rows_j = [wqkv_acc[144 * j + 48 * k : 144 * j + 48 * k + 48, :] for k in range(3)]
            at = pl.multiple_of(192 * far + 96 * late, 32)
            gqs[core, pl.ds(at, 48), 0:192] = rows_j[0].astype(BF)
            gqs[core, pl.ds(at + 48, 48), 0:192] = rows_j[1].astype(BF)
            gqs[core, pl.ds(at, 48), 192:384] = rows_j[2].astype(BF)
            gqs[core, pl.ds(at + 48, 48), 192:384] = gshort[48 * j : 48 * j + 48, :]
        by_shift = jnp.zeros((192, 384), F32)
        for cell in range(GRID):
            pick = shift_map(cell, GRID, 256)
            top, rest = split_two(
                jnp.concatenate(
                    [table_acc[k, pl.ds(cell, 192, stride=GRID), :] for k in range(2)], axis=1
                )
            )
            by_shift += mm(top, pick, NT) + mm(rest, pick, NT)
        for cell in range(8):
            pick = shift_map(cell, 8, 128)
            top, rest = split_two(
                table_acc[0, pl.ds(HEADS * WIDE_ROWS + cell, 192, stride=8), :]
            )
            by_shift += mm(top, pick, NT) + mm(rest, pick, NT)
        shift_scr[...] = jnp.zeros_like(shift_scr)
        for k in range(3):
            shift_scr[k, 0:192, :] = by_shift[:, 128 * k : 128 * k + 128]
        table = jnp.zeros((16, 768), F32)
        for r in range(GRID):
            rows_r = jnp.concatenate(
                [shift_scr[k, pl.ds(r, 16, stride=16), :] for k in range(6)], axis=1
            )
            table += pltpu.roll(rows_r, SIDE * (GRID - 1 - r), 1)
        small[0:8, :] = small_dense[...]
        small[8:16, :] = jnp.zeros((8, 384), F32)
        small[8:9, 0:192] = jnp.sum(small_acc[0].T, axis=0, keepdims=True)
        small[8:9, 192:384] = jnp.sum(small_acc[1].T, axis=0, keepdims=True)
        small[16:32, :] = table[:, 0:384]
        small[32:48, :] = table[:, 384:768]
        high, low = split_two(small[...])
        for core in range(2):
            gqs[core, 384:432, :] = high
            gqs[core, 432:480, :] = low


def front_back_kernel(first, chained, meta, img, grads_a, grads_b, *rest):
    out = rest[1] if chained else rest[0]
    n = pl.program_id(0) + first
    geo = [geometry(meta, meta[2 * n + k, 5]) for k in range(2)]

    def body(pixels, size):
        for k, grads in enumerate((grads_a, grads_b)):
            high, wide, rows, cols, stride = geo[k]
            shifted, scale = norm_stats(img[k, :, :pixels].astype(F32))
            normed = shifted * scale
            token = token_of_pixel((1, pixels), 1, high, wide, stride)
            spread = mm(grads[0, :, :size], onehot(iota((size, pixels), 0) == token))
            grad_hat = spread[:D_IN]
            along = jnp.mean(grad_hat * normed, axis=0, keepdims=True)
            full = scale * (grad_hat - normed * along) + spread[D_IN:]
            out[k, :, :pixels] = full.astype(BF)
            if pixels < PIX:
                out[k, :, pixels:] = jnp.zeros((D_IN, PIX - pixels), BF)

    short = (geo[0][0] <= 18) & (geo[1][0] <= 18)
    large = jnp.maximum(geo[0][4] * geo[0][2], geo[1][4] * geo[1][2]) > SMALL
    pl.when(short & jnp.logical_not(large))(functools.partial(body, 512, SMALL))
    pl.when(jnp.logical_not(short | large))(functools.partial(body, PIX, SMALL))
    pl.when(large)(functools.partial(body, PIX, LARGE))


def finish_kernel(
    place, mine, got, short_t, qkv_t, out_t, up_t, down,
    ln1_gain, ln1_shift, out_bias, ln2_gain, ln2_shift, up_bias, down_bias, table,
):
    both = mine[0:144, :] + got[0:144, :]
    qkv_t[0:96, :] = both[0:96, 0:192]
    qkv_t[96:144, :] = both[0:48, 192:384]
    short_t[...] = both[48:96, 192:384]
    small = both[96:144, :]
    for k, dest in enumerate((out_bias, ln2_gain, ln2_shift, down_bias)):
        dest[...] = small[k]
    up_bias[...] = jnp.concatenate([small[4 + k : 5 + k] for k in range(4)], axis=1).reshape(FF)
    ln1_gain[...] = small[8, 0:192]
    ln1_shift[...] = small[8, 192:384]
    table[:, 0:384] = small[16 : 16 + HEADS]
    table[:, 384:] = small[32 : 32 + HEADS, 0 : SIDE * SIDE - 384]

    def emit(first, second):
        up_t[...] = first[144:336, :]
        out_t[0:32, :] = first[336:368, :]
        down[...] = second[144:336, :]
        out_t[32:48, :] = second[336:352, :]

    core = place[1] & 1
    pl.when(core == 0)(functools.partial(emit, mine, got))
    pl.when(core == 1)(functools.partial(emit, got, mine))


def per_image(*tail):
    return pl.BlockSpec((1,) + tail, lambda n, *_: (n,) + (0,) * len(tail))


def pair(*tail):
    return pl.BlockSpec((2,) + tail, lambda n, *_: (n,) + (0,) * len(tail))


def pair_member(lane, k, *tail):
    return pl.BlockSpec((1,) + tail, lambda n, meta: (meta[2 * n + k, lane],) + (0,) * len(tail))


def small_pair(*tail):
    return pl.BlockSpec(
        (2,) + tail,
        lambda n, meta: (jnp.minimum(n, jnp.maximum(meta[4, 3] - 1, 0)),) + (0,) * len(tail),
    )


def large_pair(*tail):
    return pl.BlockSpec(
        (2,) + tail, lambda n, meta: (jnp.maximum(n - meta[4, 3], 0),) + (0,) * len(tail)
    )


def attention_pairs():
    return [
        small_pair(3 * D_OUT, SMALL),
        small_pair(HEADS, SMALL, SMALL),
        large_pair(3 * D_OUT, LARGE),
        large_pair(HEADS, SLOT, LARGE),
    ]


def whole(*shape):
    return pl.BlockSpec(shape, lambda n, *_: (0,) * len(shape))


def call(
    kernel, micros, grid, in_specs, out_specs, out_shape, scratch, name, *args, aliases=()
):
    return pl.pallas_call(
        kernel,
        grid_spec=pltpu.PrefetchScalarGridSpec(
            num_scalar_prefetch=1,
            grid=grid,
            in_specs=in_specs,
            out_specs=out_specs,
            scratch_shapes=scratch,
        ),
        out_shape=out_shape,
        input_output_aliases=dict(aliases),
        compiler_params=pltpu.CompilerParams(
            dimension_semantics=("arbitrary",), vmem_limit_bytes=56 * 2**20
        ),
        name=name,
        cost_estimate=pl.CostEstimate(
            flops=micros * 10**9, bytes_accessed=micros * 10**6, transcendentals=0
        ),
    )(*args)


def shape_of(*dims, dtype=BF):
    return jax.ShapeDtypeStruct(dims, dtype)


def packed_rows(count):
    return (count * SLOT + CHUNK - 1) // CHUNK * CHUNK + CHUNK


ANY = pl.BlockSpec(memory_space=pl.ANY)
GATHERED = [ANY, ANY]


def device_prepare(place, token_mask, w_short, w_qkv, w_out, w_up, w_down):
    count = token_mask.shape[0]
    return call(
        prepare_kernel,
        3,
        (1,),
        [
            whole(count, PIX),
            whole(48, D_IN),
            whole(144, D_IN),
            whole(48, D_OUT),
            whole(192, D_OUT),
            whole(192, D_OUT),
        ],
        [whole(count, 128), whole(96, D_OUT), whole(432, D_OUT)],
        [shape_of(count, 128, dtype=jnp.int32), shape_of(96, D_OUT), shape_of(432, D_OUT)],
        [],
        "prepare",
        place,
        token_mask,
        w_short.T,
        w_qkv.T,
        w_out.T,
        w_up.T,
        w_down,
    )


def device_meta(place, token_mask):
    count = token_mask.shape[0]
    return call(
        meta_rows,
        2,
        (1,),
        [whole(count, PIX)],
        [whole(count, 128)],
        [shape_of(count, 128, dtype=jnp.int32)],
        [],
        "meta",
        place,
        token_mask,
    )[0]


def device_front(meta, images, cotangent):
    count = images.shape[0]
    packed = packed_rows(count)
    return call(
        front_kernel,
        15,
        (count // 2,),
        [pair_member(4, k, D_IN, PIX) for k in range(2)]
        + [pair_member(4, k, TOK, D_OUT) for k in range(2)],
        [pair(D_IN, LARGE), whole(packed, D_IN), whole(packed, D_OUT)],
        [
            shape_of(count, D_IN, LARGE, dtype=F32),
            shape_of(packed, D_IN),
            shape_of(packed, D_OUT),
        ],
        [],
        "front",
        meta,
        images,
        images,
        cotangent,
        cotangent,
    )


SMALL_OUTPUTS = [(D_IN,)] * 2 + [(D_OUT,)] * 3 + [(FF,), (D_OUT,), (HEADS, SIDE * SIDE)]


def device_finish(place, mine, got):
    return call(
        finish_kernel,
        2,
        (1,),
        [whole(368, D_OUT), whole(368, D_OUT)],
        [
            whole(48, D_IN),
            whole(144, D_IN),
            whole(48, D_OUT),
            whole(192, D_OUT),
            whole(192, D_OUT),
        ]
        + [whole(*dims) for dims in SMALL_OUTPUTS],
        [
            shape_of(48, D_IN, dtype=F32),
            shape_of(144, D_IN, dtype=F32),
            shape_of(48, D_OUT, dtype=F32),
            shape_of(192, D_OUT, dtype=F32),
            shape_of(192, D_OUT, dtype=F32),
        ]
        + [shape_of(*dims, dtype=F32) for dims in SMALL_OUTPUTS],
        [],
        "finish",
        place,
        mine,
        got,
    )


def device_tables(rel_table):
    return pl.pallas_call(
        tables_kernel,
        out_shape=shape_of(2, BIAS_ROWS, 128, dtype=F32),
        scratch_shapes=[pltpu.VMEM((3, 192, 128), F32), pltpu.VMEM((16, 768), F32)],
        compiler_params=pltpu.CompilerParams(vmem_limit_bytes=40 * 2**20),
        name="tables",
        cost_estimate=pl.CostEstimate(
            flops=8 * 10**9, bytes_accessed=8 * 10**6, transcendentals=0
        ),
    )(rel_table)


def device_attend(meta, hat, gain, shift, att, bias):
    count = hat.shape[0]
    packed = packed_rows(count)
    return call(
        attend_kernel,
        30,
        (count // 2,),
        [pair(D_IN, LARGE), whole(D_IN), whole(D_IN)]
        + GATHERED
        + [ANY],
        attention_pairs() + [ANY],
        [
            shape_of(count, 3 * D_OUT, SMALL),
            shape_of(count, HEADS, SMALL, SMALL),
            shape_of(count, 3 * D_OUT, LARGE),
            shape_of(count, HEADS, SLOT, LARGE),
            shape_of(packed, D_OUT),
        ],
        [
            pltpu.VMEM((3 * D_OUT, D_IN), BF),
            pltpu.VMEM((2, D_OUT, LARGE), BF),
            pltpu.VMEM((2, 3, SLOT, 4 * LARGE), F32),
            pltpu.VMEM((PARTS, 96, 384), BF),
            pltpu.VMEM((D_IN, 8), F32),
            pltpu.VMEM((2, BIAS_ROWS, 128), F32),
            pltpu.VMEM((2, CHUNK, D_OUT), BF),
            pltpu.SemaphoreType.DMA((PARTS,)),
            pltpu.SemaphoreType.DMA((2,)),
            pltpu.SemaphoreType.DMA,
        ],
        "attend",
        meta,
        hat,
        gain,
        shift,
        *att,
        bias,
    )


def device_dense(meta, plain, cotp, mixed, att, ff, params):
    packed = plain.shape[0]
    rows_of = lambda width: pl.BlockSpec(
        (CHUNK, width), lambda n, meta: (jnp.minimum(n, meta[3, 3]), 0)
    )
    return call(
        dense_kernel,
        40,
        (packed // CHUNK,),
        [rows_of(D_IN), rows_of(D_OUT), rows_of(D_OUT)]
        + GATHERED
        + GATHERED
        + [whole(D_OUT)] * 4
        + [whole(FF)],
        [
            rows_of(D_OUT),
            rows_of(D_OUT),
            rows_of(D_IN),
            whole(PARTS, 224, 384),
            whole(PARTS, 224, 384),
            whole(D_OUT, D_IN),
            whole(8, D_OUT),
        ],
        [
            shape_of(packed, D_OUT),
            shape_of(packed, D_OUT),
            shape_of(packed, D_IN),
            shape_of(PARTS, 224, 384),
            shape_of(PARTS, 224, 384),
            shape_of(D_OUT, D_IN),
            shape_of(8, D_OUT, dtype=F32),
        ],
        [
            pltpu.VMEM((D_OUT, D_IN), BF),
            pltpu.VMEM((D_OUT, D_OUT), BF),
            pltpu.VMEM((FF, D_OUT), BF),
            pltpu.VMEM((FF, D_OUT), BF),
            pltpu.VMEM((D_OUT, FF), F32),
            pltpu.VMEM((D_OUT, FF), F32),
            pltpu.VMEM((D_OUT, D_OUT), F32),
            pltpu.VMEM((D_OUT, D_IN), F32),
            pltpu.VMEM((32, D_OUT), F32),
            pltpu.VMEM((8, FF), F32),
            pltpu.VMEM((PARTS, 96, 384), BF),
            pltpu.SemaphoreType.DMA((PARTS,)),
            pltpu.SemaphoreType.DMA((3 * PARTS,)),
        ],
        "dense",
        meta,
        plain,
        cotp,
        mixed,
        *att,
        *ff,
        *params,
    )


def device_expand(meta, outp, count):
    return call(
        expand_kernel,
        5,
        (count // 2,),
        [whole(*outp.shape)],
        [pair(TOK, D_OUT)],
        [shape_of(count, TOK, D_OUT)],
        [],
        "expand",
        meta,
        outp,
    )[0]


def device_attend_back(meta, hat, gain, shift, att, kept, gmix, gplain, gshort, small):
    count = hat.shape[0]
    packed = gmix.shape[0]
    return call(
        attend_back_kernel,
        40,
        (count // 2,),
        [pair(D_IN, LARGE), whole(D_IN), whole(D_IN)]
        + GATHERED
        + attention_pairs()
        + [
            ANY,
            ANY,
            whole(D_OUT, D_IN),
            whole(8, 384),
        ],
        [pair(2 * D_IN, LARGE), whole(2, 480, 384), whole(48, 384)],
        [
            shape_of(count, 2 * D_IN, LARGE),
            shape_of(2, 480, 384),
            shape_of(48, 384, dtype=F32),
        ],
        [
            pltpu.VMEM((3 * D_OUT, D_IN), BF),
            pltpu.VMEM((D_IN, 3 * D_OUT), BF),
            pltpu.VMEM((2, D_OUT, LARGE), BF),
            pltpu.VMEM((2, 3, SLOT, 4 * LARGE), F32),
            pltpu.VMEM((2, HEADS, SLOT, LARGE), BF),
            pltpu.VMEM((3 * D_OUT, 2 * LARGE), BF),
            pltpu.VMEM((3 * D_OUT, D_IN), F32),
            pltpu.VMEM((2, BIAS_ROWS, 128), F32),
            pltpu.VMEM((2, D_IN, 128), F32),
            pltpu.VMEM((6, 256, 128), F32),
            pltpu.VMEM((PARTS, 96, 384), BF),
            pltpu.VMEM((D_IN, 8), F32),
            pltpu.VMEM((2, 2 * SLOT, D_OUT), BF),
            pltpu.VMEM((2, 2 * SLOT, D_IN), BF),
            pltpu.SemaphoreType.DMA((PARTS,)),
            pltpu.SemaphoreType.DMA((2, 2)),
        ],
        "attend_back",
        meta,
        hat,
        gain,
        shift,
        *att,
        *kept,
        gmix,
        gplain,
        gshort,
        small,
    )


def device_front_back(meta, images, grads, first, count, before=None):
    some = lambda *tail: pl.BlockSpec(
        (2,) + tail, lambda n, *_: (n + first,) + (0,) * len(tail)
    )
    member = lambda k, *tail: pl.BlockSpec(
        (1,) + tail, lambda n, meta: (meta[2 * (n + first) + k, 5],) + (0,) * len(tail)
    )
    chained = before is not None
    return call(
        functools.partial(front_back_kernel, first, chained),
        1,
        (count,),
        [some(D_IN, PIX)]
        + [member(k, 2 * D_IN, LARGE) for k in range(2)]
        + ([ANY] if chained else []),
        [some(D_IN, PIX)],
        [shape_of(*images.shape)],
        [],
        "front_back",
        meta,
        images,
        grads,
        grads,
        *([before] if chained else []),
        aliases={4: 0} if chained else {},
    )[0]


def shard_grads(ff, qs):
    g_up, g_down = ff[0][:192].T, ff[1][:192]
    g_out = jnp.concatenate([ff[0][192:224], ff[1][192:208]], axis=0).T
    g_qkv = jnp.concatenate([qs[:, :192], qs[:48, 192:]], axis=0).T
    g_short = qs[48:, 192:].T
    return g_short, g_qkv, g_out, g_up, g_down


def tied(*values):
    return lax.optimization_barrier(values)


class FastLinks:
    def __init__(self):
        self.own = lax.axis_index("wide")
        self.narrow = lax.axis_index("narrow")

    def across(self, value, bit):
        return lax.ppermute(value, "narrow", [(i, i ^ bit) for i in range(4)])

    def along(self, value, bits):
        return lax.ppermute(value, "wide", [(i, i ^ bits) for i in range(PARTS)])

    def spread(self, value, bits):
        pairs = [
            (4 * w + k, 4 * (w ^ k ^ bits) + k) for w in range(PARTS) for k in range(4)
        ]
        return lax.ppermute(value, ("wide", "narrow"), pairs)

    def fetch_two(self, value):
        return jnp.stack([self.spread(value, 0), self.spread(value, 5)])


def rounded(value):
    return lax.reduce_precision(value, 8, 7)


def low_sum(left, right):
    return rounded(left.astype(F32) + right.astype(F32)).astype(BF)


def high_sum(left, right):
    return left.astype(F32) + right.astype(F32)


def two_rows(value):
    high = rounded(value)
    return jnp.concatenate([high, rounded(value - high)], axis=0).astype(BF)


def one_row(pair):
    half = pair.shape[0] // 2
    return high_sum(pair[:half], pair[half:])


def tree(parts):
    while len(parts) > 1:
        parts = [high_sum(parts[k], parts[k + 1]) for k in range(0, len(parts), 2)]
    return parts[0]


class PlainLinks:
    own = 0
    narrow = 0

    def gather_weights(self, w_short, w_qkv, w_out, w_up, w_down):
        full = [
            lax.all_gather(w.astype(BF), "wide", axis=axis, tiled=True)
            for w, axis in ((w_short, 1), (w_qkv, 1), (w_out, 1), (w_up, 1), (w_down, 0))
        ]

        def shard(j):
            short, qkv, out, up, down = (
                lax.slice_in_dim(w, j * size, (j + 1) * size, axis=axis)
                for w, size, axis in zip(full, (48, 144, 48, 192, 192), (1, 1, 1, 1, 0))
            )
            qs = jnp.concatenate([qkv.T, short.T], axis=0)
            qs = jnp.concatenate([qs[:96], qs[96:]], axis=1)
            return qs, jnp.concatenate([up.T, down, out.T], axis=0)

        parts = [shard(j) for j in (0, 5, 2, 7, 1, 4, 3, 6)]
        return tuple(
            (jnp.stack([p[k] for p in parts[:4]]), jnp.stack([p[k] for p in parts[4:]]))
            for k in range(2)
        )

    def reduce_grads(self, gff, gqs):
        order = [0, 5, 2, 7, 1, 4, 3, 6]
        gqs = gqs[:, :384].reshape(PARTS, 96, 384)
        parts = [shard_grads([g[j] for g in gff], gqs[order.index(j)]) for j in range(PARTS)]
        out = []
        for k, axis in enumerate((1, 1, 1, 1, 0)):
            whole_grad = jnp.concatenate([p[k] for p in parts], axis=axis)
            shard = lax.psum_scatter(whole_grad, "wide", scatter_dimension=axis, tiled=True)
            out.append(lax.psum(shard, "narrow").astype(F32))
        return out


def outputs(output, grad_images, weights, small):
    table = jnp.concatenate([small[16 : 16 + HEADS], small[32 : 32 + HEADS]], axis=1)
    return (
        output,
        jnp.swapaxes(grad_images, 1, 2),
        *weights,
        small[8, :192],
        small[8, 192:],
        small[0],
        small[1],
        small[2],
        small[4:8].reshape(FF),
        small[3],
        table[:, : SIDE * SIDE],
    )


def shards_plain(
    images, token_mask, w_short, w_qkv, w_out, w_up, w_down, ln1_gain, ln1_shift, out_bias,
    ln2_gain, ln2_shift, up_bias, down_bias, rel_table, cotangent,
):
    links = PlainLinks()
    count = images.shape[0]
    images = jnp.swapaxes(images, 1, 2)
    ln1 = (ln1_gain, ln1_shift)
    params = (out_bias, ln2_gain, ln2_shift, down_bias, up_bias)
    meta = device_meta(jnp.zeros((2,), jnp.int32), token_mask)
    att, ff = links.gather_weights(w_short, w_qkv, w_out, w_up, w_down)
    hat, plain, cotp = device_front(meta, images, cotangent)
    bias = device_tables(rel_table)
    *kept, mixed = device_attend(meta, hat, *ln1, att, bias)
    outp, gmix, gplain, *gff, gshort, small = device_dense(
        meta, plain, cotp, mixed, att, ff, params
    )
    output = device_expand(meta, outp, count)
    grads, gqs, small = device_attend_back(
        meta, hat, *ln1, att, kept, gmix, gplain, gshort, small
    )
    grad_images = device_front_back(meta, images, grads, 0, count // 2)
    small = lax.psum(small, ("wide", "narrow"))
    return outputs(output, grad_images, links.reduce_grads(gff, gqs), small)


def shards_fast(
    images, token_mask, w_short, w_qkv, w_out, w_up, w_down, ln1_gain, ln1_shift, out_bias,
    ln2_gain, ln2_shift, up_bias, down_bias, rel_table, cotangent,
):
    links = FastLinks()
    count = images.shape[0]
    images = jnp.swapaxes(images, 1, 2)
    ln1 = (ln1_gain, ln1_shift)
    params = (out_bias, ln2_gain, ln2_shift, down_bias, up_bias)
    place = jnp.stack([links.own, links.narrow]).astype(jnp.int32)
    meta, att, ff = device_prepare(place, token_mask, w_short, w_qkv, w_out, w_up, w_down)

    att, ff = links.fetch_two(att), links.fetch_two(ff)
    hat, plain, cotp = device_front(meta, images, cotangent)
    att, hat, rel_table = tied(att, hat, rel_table)
    att = jnp.concatenate([att, links.across(att, 2)])
    bias = device_tables(rel_table)
    att, bias, ff = tied(att, bias, ff)
    att = (att, links.across(att, 1))
    ff_more = links.across(ff, 2)
    *kept, mixed = device_attend(meta, hat, *ln1, att, bias)
    ff_more, mixed = tied(ff_more, mixed)
    ff = jnp.concatenate([ff, ff_more])
    ff_other = links.across(ff, 1)
    outp, gmix, gplain, gff_kept, gff_sent, gshort, small = device_dense(
        meta, plain, cotp, mixed, att, (ff, ff_other), params
    )

    got = links.across(gff_sent, 1)
    output = device_expand(meta, outp, count)
    got, output, gmix = tied(got, output, gmix)
    terms = [low_sum(gff_kept[d], got[d]) for d in range(PARTS)]
    far = (7, 6, 5, 4, 3)
    moved = {d: links.along(terms[d], d) for d in far}
    grads, gqs, small = device_attend_back(
        meta, hat, *ln1, att, kept, gmix, gplain, gshort, small
    )
    tie = tied(grads, gqs, terms[1], terms[2], *(moved[d] for d in far))
    grads, gqs = tie[:2]
    pairs = count // 2
    cuts = [k * pairs // 8 for k in (0, 2, 5, 7, 8)]
    done = None

    def beside(k, *got):
        piece = device_front_back(meta, images, grads, cuts[k], cuts[k + 1] - cuts[k], done)
        return tied(piece, *got)

    got = links.across(gqs[1], 1)
    near = links.along(tie[2], 1), links.along(tie[3], 2)
    done, got, *near = beside(0, got, *near)
    terms[1:] = [*near, *reversed(tie[4:])]
    held = low_sum(gqs[0, :384], got[:384])
    small = one_row(gqs[0, 384:]) + one_row(got[384:])
    small = two_rows(small)
    sent, done = tied(jnp.concatenate([held[192:], small]), done)
    got = links.across(sent, 2)
    done, got, *terms = beside(1, got, *terms)
    held = low_sum(held[:192], got[:192])
    small = two_rows(one_row(small) + one_row(got[192:]))
    ff_sum = rounded(tree(terms)).astype(BF)
    *sent, ff_sum, done = tied(
        jnp.concatenate([held[:96], small]), jnp.concatenate([held[96:], small]), ff_sum, done
    )
    got = links.spread(sent[0], 0), links.spread(sent[1], 5)
    ff_got = links.across(ff_sum, 2)
    done, ff_got, *got = beside(2, ff_got, *got)
    held = low_sum(got[0][:96], got[1][:96])
    small = two_rows(one_row(got[0][96:]) + one_row(got[1][96:]))
    mine, done = tied(jnp.concatenate([held, small]), done)
    got = links.across(mine, 2)
    done, got, ff_sum, ff_got = beside(3, got, ff_sum, ff_got)
    mine = jnp.concatenate(
        [
            high_sum(mine[:96], got[:96]),
            one_row(mine[96:]) + one_row(got[96:]),
            high_sum(ff_sum, ff_got),
        ]
    )
    last = device_finish(place, mine, links.across(mine, 1))
    return (output, jnp.swapaxes(done, 1, 2), *(w.T for w in last[:4]), *last[4:])


def solution(mesh):
    data = ("wide", "narrow")
    rows = P(None, "wide")
    in_specs = (
        (P(data, None, None), P(data, None), rows, rows, rows, rows, P("wide", None))
        + (P(),) * 8
        + (P(data, None, None),)
    )
    out_specs = (
        (P(data, None, None), P(data, None, None), rows, rows, rows, rows, P("wide", None))
        + (P(),) * 8
    )
    fast = mesh.shape["wide"] == PARTS and mesh.shape["narrow"] == 4
    return jax.shard_map(
        shards_fast if fast else shards_plain,
        mesh=mesh,
        in_specs=in_specs,
        out_specs=out_specs,
        check_vma=False,
    )
```

```python
import functools
import math

import jax
import jax.numpy as jnp
from jax import lax
from jax.experimental import pallas as pl
from jax.experimental.pallas import tpu as pltpu
from jax.sharding import PartitionSpec as P

D_IN = 192
D_OUT = 384
HEADS = 12
HEAD_DIM = 32
FF = 1536
GRID = 14
SIDE = 2 * GRID - 1
TOK = GRID * GRID
PIX = 4 * TOK
EPS = 1e-05
LOG2E = math.log2(math.e)
SCORE_SCALE = HEAD_DIM ** (-0.5)

SLOT = 208
SMALL = 128
LARGE = 256
WIDE_ROWS = 16 * GRID
NARROW_ROWS = 16 * 8
BIAS_ROWS = HEADS * (WIDE_ROWS + NARROW_ROWS)
CHUNK = 512
WIDTH = 768
PARTS = 8
BF = jnp.bfloat16
F32 = jnp.float32
NN = (((1,), (0,)), ((), ()))
NT = (((1,), (1,)), ((), ()))
TN = (((0,), (0,)), ((), ()))


def mm(left, right, dims=NN):
    return lax.dot_general(left, right, dims, preferred_element_type=F32)


def iota(shape, dim):
    return lax.broadcasted_iota(jnp.int32, shape, dim)


def geometry(meta, n):
    high, wide = meta[n, 0], meta[n, 1]
    rows, cols = (high + 1) >> 1, (wide + 1) >> 1
    return high, wide, rows, cols, meta[n, 6]


def cell_of(index, stride):
    row = jnp.where(stride == 8, index >> 3, (index * 4682) >> 16)
    return row, index - stride * row


def packed_index(index, stride, rows, cols):
    row, col = cell_of(index, stride)
    return jnp.where((col < cols) & (row < rows), row * cols + col, -1)


def onehot(mask):
    return jnp.where(mask, 1.0, 0.0).astype(BF)


def packing(shape, stride, rows, cols):
    return onehot(iota(shape, 0) == packed_index(iota((1, shape[1]), 1), stride, rows, cols))


def unpacking(shape, stride, rows, cols):
    return onehot(iota(shape, 1) == packed_index(iota((shape[0], 1), 0), stride, rows, cols))


def split_two(values):
    high = values.astype(BF)
    return high, (values - high.astype(F32)).astype(BF)


def shift_map(cell, stride, lanes):
    spot = iota((1, lanes), 1)
    row, col = cell_of(spot, stride)
    pick = jnp.where((row < GRID) & (col < GRID), SIDE * row + col - cell + GRID - 1, -1)
    return onehot(iota((384, lanes), 0) == pick)


def token_of_pixel(shape, dim, high, wide, stride):
    spot = iota(shape, dim)
    row = (spot * 2341) >> 16
    col = spot - 28 * row
    return jnp.where((row < high) & (col < wide), (row >> 1) * stride + (col >> 1), -1)


def window_share(shape, dim, high, wide, stride):
    row, col = cell_of(iota(shape, dim), stride)
    return jnp.where(2 * row + 1 < high, 0.5, 1.0) * jnp.where(2 * col + 1 < wide, 0.5, 1.0)


def norm_stats(values, axis=0):
    center = jnp.mean(values, axis=axis, keepdims=True)
    shifted = values - center
    spread = jnp.mean(shifted * shifted, axis=axis, keepdims=True)
    return shifted, lax.rsqrt(spread + EPS)


def prepare_kernel(place, mask, short_t, qkv_t, out_t, up_t, down, meta, att, ff):
    att[0:96, 0:192] = qkv_t[0:96, :].astype(BF)
    att[0:48, 192:384] = qkv_t[96:144, :].astype(BF)
    att[48:96, 192:384] = short_t[...].astype(BF)
    ff[0:192, :] = up_t[...].astype(BF)
    ff[192:384, :] = down[...].astype(BF)
    ff[384:432, :] = out_t[...].astype(BF)
    meta_rows(place, mask, meta)


def meta_rows(place, mask, meta):
    count = mask.shape[0]
    ones = mask[...]
    spot = iota(ones.shape, 1)
    row = (spot * 2341) >> 16
    high = jnp.sum(jnp.where(spot == 28 * row, ones, 0).astype(F32), axis=1, keepdims=True)
    wide = jnp.sum(jnp.where(spot < 28, ones, 0).astype(F32), axis=1, keepdims=True)

    def along(column):
        return jnp.broadcast_to(column, (count, 128)).T[:count]

    def total(values):
        return jnp.sum(values, axis=1, keepdims=True)

    rows = (high.astype(jnp.int32) + 1) >> 1
    cols = (wide.astype(jnp.int32) + 1) >> 1
    image = iota((count, 1), 0)
    stride = jnp.where(cols <= 8, 8, GRID)
    key = (stride * rows * count + image).astype(F32)
    rank = total(jnp.where(along(key) < key, 1.0, 0.0))
    chosen = along(rank) == image.astype(F32)

    def sort(column):
        return total(jnp.where(chosen, along(column), 0.0))

    taken = sort(((((rows * cols) + 15) >> 4) << 4).astype(F32))
    small = total(jnp.where(along(key) < SMALL * count + count, 1.0, 0.0)).astype(jnp.int32)
    start = total(jnp.where(iota((count, count), 1) < image, along(taken), 0.0))
    packed = total(along(taken)).astype(jnp.int32)
    chunks = (packed + CHUNK - 1) >> 9
    extra = jnp.where(image == 0, packed, jnp.where(image == 3, chunks, small >> 1))
    extra = jnp.where(image == 1, place[0], jnp.where(image == 2, place[1], extra))
    lane = iota((count, 128), 1)
    result = jnp.zeros((count, 128), jnp.int32)
    stride = jnp.where(image < (small >> 1) * 2, sort(stride.astype(F32)), float(GRID))
    columns = (sort(high), sort(wide), start, extra, sort(image.astype(F32)), rank, stride)
    for k, column in enumerate(columns):
        result = jnp.where(lane == k, column.astype(jnp.int32), result)
    meta[...] = result


def front_kernel(meta, img_a, img_b, cot_a, cot_b, hat, plain, cotp):
    n = pl.program_id(0)
    geo = [geometry(meta, 2 * n), geometry(meta, 2 * n + 1)]
    starts = [pl.multiple_of(meta[2 * n + k, 2], 16) for k in range(2)]

    def body(pixels, size, psize):
        sums = []
        for k, img in enumerate((img_a, img_b)):
            high, wide, rows, cols, stride = geo[k]
            values = img[0, :, :pixels]
            shifted, scale = norm_stats(values.astype(F32))
            normed = (shifted * scale).astype(BF)
            token = token_of_pixel((pixels, 1), 0, high, wide, stride)
            pick = onehot(iota((pixels, size), 1) == token)
            share = window_share((1, size), 1, high, wide, stride)
            sums.append(mm(jnp.concatenate([normed, values], axis=0), pick) * share)
        packed = []
        for k, cot in enumerate((cot_a, cot_b)):
            high, wide, rows, cols, stride = geo[k]
            hat[k, :, :size] = sums[k][:D_IN]
            pick = packing((psize, size), stride, rows, cols)
            first = mm(pick, sums[k][D_IN:].astype(BF), NT).astype(BF)
            pick = packing((psize, TOK), GRID, rows, cols)
            packed.append((first, mm(pick, cot[0]).astype(BF)))
        for k in range(2):
            plain[pl.ds(starts[k], psize), :] = packed[k][0]
            cotp[pl.ds(starts[k], psize), :] = packed[k][1]

    short = (geo[0][0] <= 18) & (geo[1][0] <= 18)
    large = geo[1][4] * geo[1][2] > SMALL
    pl.when(short & jnp.logical_not(large))(functools.partial(body, 512, SMALL, SMALL))
    pl.when(jnp.logical_not(short | large))(functools.partial(body, PIX, SMALL, SMALL))
    pl.when(large)(functools.partial(body, PIX, LARGE, SLOT))

    @pl.when(n == pl.num_programs(0) - 1)
    def _():
        total = pl.multiple_of(meta[0, 3], 16)
        plain[pl.ds(total, CHUNK), :] = jnp.zeros((CHUNK, D_IN), BF)
        cotp[pl.ds(total, CHUNK), :] = jnp.zeros((CHUNK, D_OUT), BF)


def tables_kernel(tab, bias, shift_scr, table_scr):
    shift_scr[...] = jnp.zeros_like(shift_scr)
    table_scr[...] = jnp.zeros_like(table_scr)
    table_scr[:HEADS, : SIDE * SIDE] = tab[...] * LOG2E
    table = table_scr[...]
    for r in range(GRID):
        moved = pltpu.roll(table, (768 - SIDE * (GRID - 1 - r)) % 768, 1)
        for k in range(3):
            shift_scr[k, pl.ds(r, HEADS, stride=16), :] = moved[
                :HEADS, 128 * k : 128 * k + 128
            ]
    top, rest = split_two(jnp.concatenate([shift_scr[k] for k in range(3)], axis=1))
    for cell in range(GRID):
        pick = shift_map(cell, GRID, 256)
        spread = mm(top, pick) + mm(rest, pick)
        for k in range(2):
            bias[k, pl.ds(cell, 192, stride=GRID), :] = spread[:, 128 * k : 128 * k + 128]
    for cell in range(8):
        pick = shift_map(cell, 8, 128)
        bias[0, pl.ds(HEADS * WIDE_ROWS + cell, 192, stride=8), :] = mm(top, pick) + mm(
            rest, pick
        )


def shard_at(meta, e):
    step = (2 if e & 2 else 0) ^ (5 if e & 1 else 0) ^ (1 if e >= 4 else 0)
    return meta[1, 3] ^ meta[2, 3] ^ step


def fetch_shards(meta, mine, other, dest, sems):
    copies = []
    for e in range(PARTS):
        source = mine if e < 4 else other
        copies.append(
            pltpu.make_async_copy(source.at[e & 3], dest.at[shard_at(meta, e)], sems.at[e])
        )
    for copy in copies:
        copy.start()
    return copies


def unpack_qkv(att, qkv_scr):
    for j in range(PARTS):
        qkv_scr[144 * j : 144 * j + 96, :] = att[j, 0:96, 0:192]
        qkv_scr[144 * j + 96 : 144 * j + 144, :] = att[j, 0:48, 192:384]


def slot_valid(shape, dim, stride, rows, cols):
    row, col = cell_of(iota(shape, dim), stride)
    return (col < cols) & (row < rows)


def row_of(vector):
    return vector[...].reshape(1, vector.shape[0])


def columns_of(gain, shift, dest):
    rows = jnp.concatenate(
        [row_of(gain), row_of(shift), jnp.zeros((6, D_IN), F32)], axis=0
    )
    dest[...] = rows.T


def spread_heads(block, tail=None):
    size = block.shape[1]
    parts = []
    for j in range(4):
        rows = [block[32 * j : 32 * j + 32]]
        if j > 0:
            rows.insert(0, jnp.zeros((32 * j, size), BF))
        if j < 3:
            rows.append(jnp.zeros((96 - 32 * j, size), BF))
        if tail is not None:
            rows.append(tail)
        parts.append(jnp.concatenate(rows, axis=0))
    return jnp.concatenate(parts, axis=1)


def table_row(head, stride):
    row = jnp.where(stride == 8, HEADS * WIDE_ROWS + head * NARROW_ROWS, head * WIDE_ROWS)
    return pl.multiple_of(row, 8)


def pooled_pair(geo, size, hat, gain_scr):
    lane_ok = [slot_valid((1, size), 1, g[4], g[2], g[3]) for g in geo]
    pooled = [
        jnp.where(lane_ok[k], hat[k, :, :size] * gain_scr[:, 0:1] + gain_scr[:, 1:2], 0.0)
        for k in range(2)
    ]
    return lane_ok, jnp.concatenate(pooled, axis=1).astype(BF)


def attend_kernel(
    meta, hat, gain, shift, att_mine, att_other, bias,
    qkvt_small, probs_small, qkvt_large, probs_large, mixed,
    wqkv_scr, mix_scr, score_scr, att_scr, gain_scr, bias_scr, rows_scr, sems, bias_sems, rows_sem,
):
    n = pl.program_id(0)
    fetch_bias = [
        pltpu.make_async_copy(bias.at[0], bias_scr.at[0], bias_sems.at[0]),
        pltpu.make_async_copy(
            bias.at[1, pl.ds(0, HEADS * WIDE_ROWS)],
            bias_scr.at[1, pl.ds(0, HEADS * WIDE_ROWS)],
            bias_sems.at[1],
        ),
    ]

    def put_rows(pair, size):
        first = pl.multiple_of(meta[2 * pair, 2], 16)
        return pltpu.make_async_copy(
            rows_scr.at[pair & 1, pl.ds(0, size)], mixed.at[pl.ds(first, size)], rows_sem
        )

    def wait_rows(pair):
        pl.when(pair < meta[4, 3])(lambda: put_rows(pair, 2 * SMALL).wait())
        pl.when(pair >= meta[4, 3])(lambda: put_rows(pair, 2 * SLOT).wait())

    geo = [geometry(meta, 2 * n), geometry(meta, 2 * n + 1)]
    starts = [pl.multiple_of(meta[2 * n + k, 2], 16) for k in range(2)]

    @pl.when(n == 0)
    def _():
        for copy in fetch_bias:
            copy.start()
        copies = fetch_shards(meta, att_mine, att_other, att_scr, sems)
        columns_of(gain, shift, gain_scr)
        for copy in copies:
            copy.wait()
        unpack_qkv(att_scr, wqkv_scr)
        for copy in fetch_bias:
            copy.wait()

    def body(size, keys, psize, qkvt, probs):
        lane_ok, pooled = pooled_pair(geo, size, hat, gain_scr)
        qkv = mm(wqkv_scr[...], pooled).astype(BF)
        first_row = iota((16, size), 0) == 0
        ones = onehot(first_row)
        for k in range(2):
            qkvt[k] = qkv[:, size * k : size * k + size]
        for k in range(2):
            closed = jnp.where(first_row & ~lane_ok[k], -1e30, 0.0).astype(BF)
            for g in range(3):
                key = jnp.concatenate([qkvt[k, 384 + 128 * g : 512 + 128 * g, :], closed], axis=0)
                query = spread_heads(qkvt[k, 128 * g : 128 * g + 128, :], ones)
                score_scr[k, g, :keys, : 4 * size] = mm(key.T[:keys], query)
        for head in range(HEADS):
            at = size * (head % 4)
            for k in range(2):
                scores = score_scr[k, head // 4, :keys, at : at + size] * (SCORE_SCALE * LOG2E)
                if size == SMALL:
                    scores += bias_scr[0, pl.ds(table_row(head, geo[k][4]), keys), :]
                else:
                    scores += jnp.concatenate(
                        [
                            bias_scr[j, pl.ds(table_row(head, geo[k][4]), keys), :]
                            for j in range(2)
                        ],
                        axis=1,
                    )
                expo = jnp.exp2(scores - jnp.max(scores, axis=0, keepdims=True))
                share = expo * (1.0 / jnp.sum(expo, axis=0, keepdims=True))
                probs[k, head] = share.astype(BF)
        for head in range(HEADS):
            at = HEAD_DIM * head
            for k in range(2):
                value = qkvt[k, 768 + at : 800 + at, :keys]
                mix_scr[k, at : at + 32, :size] = mm(value, probs[k, head]).astype(BF)
        packed = []
        for k in range(2):
            pick = packing((psize, size), geo[k][4], geo[k][2], geo[k][3])
            packed.append(mm(pick, mix_scr[k, :, :size], NT).astype(BF))
        slot = n & 1
        rows_scr[slot, 0:psize, :] = packed[0]
        second = pl.multiple_of(starts[1] - starts[0], 16)
        rows_scr[slot, pl.ds(second, psize), :] = packed[1]
        pl.when(n > 0)(lambda: wait_rows(n - 1))
        put_rows(n, 2 * psize).start()

    pl.when(n < meta[4, 3])(
        functools.partial(body, SMALL, SMALL, SMALL, qkvt_small, probs_small)
    )
    pl.when(n >= meta[4, 3])(functools.partial(body, LARGE, SLOT, SLOT, qkvt_large, probs_large))

    @pl.when(n == pl.num_programs(0) - 1)
    def _():
        wait_rows(n)
        total = pl.multiple_of(meta[0, 3], 16)
        rows_scr[0, 0:CHUNK, :] = jnp.zeros((CHUNK, D_OUT), BF)
        blank = pltpu.make_async_copy(
            rows_scr.at[0, pl.ds(0, CHUNK)], mixed.at[pl.ds(total, CHUNK)], rows_sem
        )
        blank.start()
        blank.wait()


def gelu_both(x):
    bell = jnp.exp2((x * x) * (-0.5 * LOG2E))
    half = 0.5 + 0.5 * lax.erf(x * math.sqrt(0.5))
    return x * half, half + (x * bell) * (1.0 / math.sqrt(2.0 * math.pi))


def dense_kernel(
    meta, plain, cotp, mixed, att_mine, att_other, ff_mine, ff_other,
    outbias, gain, shift, downbias, upbias,
    outp, gmix, gplain, gff_kept, gff_sent, gshort, small,
    wshort_scr, wout_scr, wup_scr, wdown_scr, up_acc, down_acc, out_acc, short_acc, small_acc,
    up_small, att_scr, att_sems, ff_sems,
):
    i = pl.program_id(0)

    @pl.when(i == 0)
    def _():
        ff_copies = []
        for e in range(PARTS):
            source = (ff_mine if e < 4 else ff_other).at[e & 3]
            shard = shard_at(meta, e)
            for k, (dest, low, size) in enumerate(
                ((wup_scr, 0, 192), (wdown_scr, 192, 192), (wout_scr, 384, 48))
            ):
                ff_copies.append(
                    pltpu.make_async_copy(
                        source.at[pl.ds(low, size)],
                        dest.at[pl.ds(pl.multiple_of(shard * size, 16), size)],
                        ff_sems.at[3 * e + k],
                    )
                )
        for copy in ff_copies:
            copy.start()
        for copy in fetch_shards(meta, att_mine, att_other, att_scr, att_sems):
            copy.wait()
        for j in range(PARTS):
            wshort_scr[48 * j : 48 * j + 48, :] = att_scr[j, 48:96, 192:384]
        up_acc[...] = jnp.zeros_like(up_acc)
        down_acc[...] = jnp.zeros_like(down_acc)
        out_acc[...] = jnp.zeros_like(out_acc)
        short_acc[...] = jnp.zeros_like(short_acc)
        small_acc[...] = jnp.zeros_like(small_acc)
        up_small[...] = jnp.zeros_like(up_small)
        for copy in ff_copies:
            copy.wait()

    @pl.when(i < meta[3, 3])
    def _():
        out_bias, ln_gain, ln_shift, down_bias = map(row_of, (outbias, gain, shift, downbias))
        up_bias = row_of(upbias)
        wout = wout_scr[...]
        wshort = wshort_scr[...]
        first = mm(plain[...], wshort, NT) + mm(mixed[...], wout, NT) + out_bias
        shifted, scale = norm_stats(first, -1)
        hat = shifted * scale
        normed = (hat * ln_gain + ln_shift).astype(BF)
        normed_t = normed.T
        cot = cotp[...]
        cot_t = cot.T
        branch = jnp.zeros((CHUNK, D_OUT), F32)
        grad_normed = jnp.zeros((CHUNK, D_OUT), F32)
        one_rows = jnp.ones((8, CHUNK), BF)
        for j in range(FF // WIDTH):
            some = slice(WIDTH * j, WIDTH * j + WIDTH)
            hidden = mm(normed, wup_scr[some, :], NT) + up_bias[:, some]
            grad_act = mm(cot, wdown_scr[some, :], NT)
            act, slope = gelu_both(hidden)
            act = act.astype(BF)
            grad_hidden = (grad_act * slope).astype(BF)
            branch += mm(act, wdown_scr[some, :])
            grad_normed += mm(grad_hidden, wup_scr[some, :])
            up_acc[:, some] += mm(normed_t, grad_hidden)
            down_acc[:, some] += mm(cot_t, act)
            up_small[:, some] += mm(one_rows, grad_hidden)
        outp[...] = (first + branch + down_bias).astype(BF)
        grad_branch = cot.astype(F32)
        grad_hat = grad_normed * ln_gain
        center = jnp.mean(grad_hat, axis=-1, keepdims=True)
        along = jnp.mean(grad_hat * hat, axis=-1, keepdims=True)
        grad_first = grad_branch + scale * (grad_hat - center - hat * along)
        low = grad_first.astype(BF)
        low_t = low.T
        gmix[...] = mm(low, wout).astype(BF)
        gplain[...] = mm(low, wshort).astype(BF)
        out_acc[...] += mm(low_t, mixed[...])
        short_acc[...] += mm(low_t, plain[...])

        def fold(values):
            return jnp.sum(values.reshape(CHUNK // 8, 8, D_OUT), axis=0)

        small_acc[0:8, :] += fold(grad_first)
        small_acc[8:16, :] += fold(grad_normed * hat)
        small_acc[16:24, :] += fold(grad_normed)
        small_acc[24:32, :] += fold(grad_branch)

    @pl.when(i == meta[3, 3])
    def _():
        for ref in (outp, gmix, gplain):
            ref[...] = jnp.zeros_like(ref)

    @pl.when(i == meta[3, 3] - 1)
    def _():
        own, core = meta[1, 3], meta[2, 3] & 1

        def emit(kept, sent):
            for j in range(PARTS):
                at = own ^ j
                kept[at, 0:192, :] = up_acc[:, 192 * j : 192 * j + 192].astype(BF).T
                sent[at, 0:192, :] = down_acc[:, 192 * j : 192 * j + 192].astype(BF).T
                out_rows = out_acc[48 * j : 48 * j + 48, :].astype(BF)
                kept[at, 192:224, :] = out_rows[0:32]
                sent[at, 192:208, :] = out_rows[32:48]
                sent[at, 208:224, :] = jnp.zeros((16, D_OUT), BF)

        pl.when(core == 0)(functools.partial(emit, gff_kept, gff_sent))
        pl.when(core == 1)(functools.partial(emit, gff_sent, gff_kept))
        gshort[...] = short_acc[...].astype(BF)
        for k in range(4):
            total = small_acc[8 * k : 8 * k + 8, :]
            small[k : k + 1, :] = jnp.sum(total, axis=0, keepdims=True)
            small[4 + k : 5 + k, :] = up_small[0:1, 384 * k : 384 * k + 384]


def expand_kernel(meta, outp, out):
    n = pl.program_id(0)
    at = [meta[4 * n + k, 5] for k in range(4)]
    geo = [geometry(meta, p) for p in at]

    def body(size):
        for k in range(4):
            start = pl.multiple_of(meta[at[k], 2], 16)
            spread = unpacking((TOK, size), GRID, geo[k][2], geo[k][3])
            out[k] = mm(spread, outp[pl.ds(start, size), :]).astype(BF)

    most = functools.reduce(jnp.maximum, [g[2] * g[3] for g in geo])
    pl.when(most <= SMALL)(functools.partial(body, SMALL))
    pl.when(most > SMALL)(functools.partial(body, SLOT))


def attend_back_kernel(
    meta, hat, gain, shift, att_mine, att_other,
    qkvt_small, probs_small, qkvt_large, probs_large, gmix, gplain, gshort, small_dense,
    grads, gqs_kept, gqs_sent, small,
    wqkv_scr, wrow_scr, gm_scr, score_scr, gs_scr, gqkv_scr, wqkv_acc, table_acc, small_acc,
    shift_scr, att_scr, gain_scr, gmix_scr, gplain_scr, gqs_scr, sems, row_sems,
):
    n = pl.program_id(0)
    slot = n & 1

    def get_rows(pair, size):
        first = pl.multiple_of(meta[2 * pair, 2], 16)
        return [
            pltpu.make_async_copy(
                source.at[pl.ds(first, size)],
                dest.at[pair & 1, pl.ds(0, size)],
                row_sems.at[pair & 1, k],
            )
            for k, (source, dest) in enumerate(((gmix, gmix_scr), (gplain, gplain_scr)))
        ]

    def start_rows(pair):
        def start(size):
            for copy in get_rows(pair, size):
                copy.start()

        pl.when(pair < meta[4, 3])(lambda: start(2 * SMALL))
        pl.when(pair >= meta[4, 3])(lambda: start(2 * SLOT))

    pl.when(n == 0)(lambda: start_rows(n))
    pl.when(n + 1 < pl.num_programs(0))(lambda: start_rows(n + 1))
    geo = [geometry(meta, 2 * n), geometry(meta, 2 * n + 1)]
    starts = [pl.multiple_of(meta[2 * n + k, 2], 16) for k in range(2)]

    @pl.when(n == 0)
    def _():
        for copy in fetch_shards(meta, att_mine, att_other, att_scr, sems):
            copy.wait()
        unpack_qkv(att_scr, wqkv_scr)
        columns_of(gain, shift, gain_scr)
        wrow_scr[...] = wqkv_scr[...].T
        wqkv_acc[...] = jnp.zeros_like(wqkv_acc)
        table_acc[...] = jnp.zeros_like(table_acc)
        small_acc[...] = jnp.zeros_like(small_acc)

    def body(size, keys, psize, qkvt, probs):
        picks = [packing((psize, size), g[4], g[2], g[3]) for g in geo]
        second = pl.multiple_of(starts[1] - starts[0], 16)
        spans = [pl.ds(0, psize), pl.ds(second, psize)]
        for copy in get_rows(n, 2 * psize):
            copy.wait()
        for k in range(2):
            gm_scr[k, :, :size] = mm(gmix_scr[slot, spans[k], :], picks[k], TN).astype(BF)
        for k in range(2):
            for g in range(3):
                value = qkvt[k, 768 + 128 * g : 896 + 128 * g, :].T[:keys]
                grad_mix = spread_heads(gm_scr[k, 128 * g : 128 * g + 128, :size])
                score_scr[k, g, :keys, : 4 * size] = mm(value, grad_mix)
        for head in range(HEADS):
            at = size * (head % 4)
            for k in range(2):
                share = probs[k, head].astype(F32)
                grad_share = score_scr[k, head // 4, :keys, at : at + size]
                inner = jnp.sum(share * grad_share, axis=0, keepdims=True)
                grad_scores = share * (grad_share - inner)
                row = table_row(head, geo[k][4])
                for j in range(size // 128):
                    table_acc[j, pl.ds(row, keys), :] += grad_scores[:, 128 * j : 128 * j + 128]
                gs_scr[k, head, :keys, :size] = grad_scores.astype(BF)
        for head in range(HEADS):
            at = HEAD_DIM * head
            for k in range(2):
                low = gs_scr[k, head, :keys, :size]
                key = qkvt[k, 384 + at : 416 + at, :keys]
                query = qkvt[k, at : at + 32, :]
                left, right = size * k, size * k + keys
                gqkv_scr[at : at + 32, left : left + size] = (mm(key, low) * SCORE_SCALE).astype(BF)
                gqkv_scr[384 + at : 416 + at, left:right] = (
                    mm(query, low, NT) * SCORE_SCALE
                ).astype(BF)
                gqkv_scr[768 + at : 800 + at, left:right] = mm(
                    gm_scr[k, at : at + 32, :size], probs[k, head], NT
                ).astype(BF)
        if keys < size:
            for k in range(2):
                gqkv_scr[384:, size * k + keys : size * k + size] = jnp.zeros(
                    (768, size - keys), BF
                )
        lane_ok, pooled = pooled_pair(geo, size, hat, gain_scr)
        gqkv = gqkv_scr[:, : 2 * size]
        wqkv_acc[...] += mm(gqkv, pooled, NT)
        grad_pooled_both = mm(wrow_scr[...], gqkv)
        for k in range(2):
            high, wide = geo[k][:2]
            if size < LARGE:
                grads[k, :, size:] = jnp.zeros((2 * D_IN, LARGE - size), BF)
            grad_pooled = jnp.where(
                lane_ok[k], grad_pooled_both[:, size * k : size * k + size], 0.0
            )
            gain_terms = grad_pooled * hat[k, :, :size]
            for j in range(size // 128):
                small_acc[0] += gain_terms[:, 128 * j : 128 * j + 128]
                small_acc[1] += grad_pooled[:, 128 * j : 128 * j + 128]
            part = window_share((1, size), 1, high, wide, geo[k][4])
            grad_hat = grad_pooled * gain_scr[:, 0:1] * part
            grad_hat = grad_hat - jnp.mean(grad_hat, axis=0, keepdims=True)
            grads[k, 0:192, :size] = grad_hat.astype(BF)
            grads[k, 192:384, :size] = (
                mm(gplain_scr[slot, spans[k], :], picks[k], TN) * part
            ).astype(BF)

    pl.when(n < meta[4, 3])(
        functools.partial(body, SMALL, SMALL, SMALL, qkvt_small, probs_small)
    )
    pl.when(n >= meta[4, 3])(functools.partial(body, LARGE, SLOT, SLOT, qkvt_large, probs_large))

    @pl.when(n == pl.num_programs(0) - 1)
    def _():
        own, narrow = meta[1, 3], meta[2, 3]
        for j in range(PARTS):
            d = own ^ j
            late = d >> 2
            keeper = (d ^ (5 * late)) ^ narrow
            core = keeper & 1
            at = pl.multiple_of(192 * (keeper >> 1) + 96 * late, 32)
            rows_j = [wqkv_acc[144 * j + 48 * k : 144 * j + 48 * k + 48, :] for k in range(3)]
            gqs_scr[core, pl.ds(at, 48), 0:192] = rows_j[0].astype(BF)
            gqs_scr[core, pl.ds(at + 48, 48), 0:192] = rows_j[1].astype(BF)
            gqs_scr[core, pl.ds(at, 48), 192:384] = rows_j[2].astype(BF)
            gqs_scr[core, pl.ds(at + 48, 48), 192:384] = gshort[48 * j : 48 * j + 48, :]
        by_shift = jnp.zeros((192, 384), F32)
        for cell in range(GRID):
            pick = shift_map(cell, GRID, 256)
            top, rest = split_two(
                jnp.concatenate(
                    [table_acc[k, pl.ds(cell, 192, stride=GRID), :] for k in range(2)], axis=1
                )
            )
            by_shift += mm(top, pick, NT) + mm(rest, pick, NT)
        for cell in range(8):
            pick = shift_map(cell, 8, 128)
            top, rest = split_two(
                table_acc[0, pl.ds(HEADS * WIDE_ROWS + cell, 192, stride=8), :]
            )
            by_shift += mm(top, pick, NT) + mm(rest, pick, NT)
        shift_scr[...] = jnp.zeros_like(shift_scr)
        for k in range(3):
            shift_scr[k, 0:192, :] = by_shift[:, 128 * k : 128 * k + 128]
        table = jnp.zeros((16, 768), F32)
        for r in range(GRID):
            rows_r = jnp.concatenate(
                [shift_scr[k, pl.ds(r, 16, stride=16), :] for k in range(6)], axis=1
            )
            table += pltpu.roll(rows_r, SIDE * (GRID - 1 - r), 1)
        small[0:8, :] = small_dense[...]
        small[8:16, :] = jnp.zeros((8, 384), F32)
        small[8:9, 0:192] = jnp.sum(small_acc[0].T, axis=0, keepdims=True)
        small[8:9, 192:384] = jnp.sum(small_acc[1].T, axis=0, keepdims=True)
        small[16:32, :] = table[:, 0:384]
        small[32:48, :] = table[:, 384:768]
        high, low = split_two(small[...])
        for core, dest in enumerate((gqs_kept, gqs_sent)):
            dest[0:384, :] = gqs_scr[core]
            dest[384:432, :] = high
            dest[432:480, :] = low


def front_back_kernel(first, chained, meta, img, grads_a, grads_b, *rest):
    out = rest[1] if chained else rest[0]
    n = pl.program_id(0) + first
    geo = [geometry(meta, meta[2 * n + k, 5]) for k in range(2)]

    def body(pixels, size):
        for k, grads in enumerate((grads_a, grads_b)):
            high, wide, rows, cols, stride = geo[k]
            shifted, scale = norm_stats(img[k, :, :pixels].astype(F32))
            normed = shifted * scale
            token = token_of_pixel((1, pixels), 1, high, wide, stride)
            spread = mm(grads[0, :, :size], onehot(iota((size, pixels), 0) == token))
            grad_hat = spread[:D_IN]
            along = jnp.mean(grad_hat * normed, axis=0, keepdims=True)
            full = scale * (grad_hat - normed * along) + spread[D_IN:]
            out[k, :, :pixels] = full.astype(BF)
            if pixels < PIX:
                out[k, :, pixels:] = jnp.zeros((D_IN, PIX - pixels), BF)

    short = (geo[0][0] <= 18) & (geo[1][0] <= 18)
    large = jnp.maximum(geo[0][4] * geo[0][2], geo[1][4] * geo[1][2]) > SMALL
    pl.when(short & jnp.logical_not(large))(functools.partial(body, 512, SMALL))
    pl.when(jnp.logical_not(short | large))(functools.partial(body, PIX, SMALL))
    pl.when(large)(functools.partial(body, PIX, LARGE))


def finish_kernel(
    place, mine, got, short_t, qkv_t, out_t, up_t, down,
    ln1_gain, ln1_shift, out_bias, ln2_gain, ln2_shift, up_bias, down_bias, table,
):
    both = mine[0:144, :] + got[0:144, :]
    qkv_t[0:96, :] = both[0:96, 0:192]
    qkv_t[96:144, :] = both[0:48, 192:384]
    short_t[...] = both[48:96, 192:384]
    small = both[96:144, :]
    for k, dest in enumerate((out_bias, ln2_gain, ln2_shift, down_bias)):
        dest[...] = small[k]
    up_bias[...] = jnp.concatenate([small[4 + k : 5 + k] for k in range(4)], axis=1).reshape(FF)
    ln1_gain[...] = small[8, 0:192]
    ln1_shift[...] = small[8, 192:384]
    table[:, 0:384] = small[16 : 16 + HEADS]
    table[:, 384:] = small[32 : 32 + HEADS, 0 : SIDE * SIDE - 384]

    def emit(first, second):
        up_t[...] = first[144:336, :]
        out_t[0:32, :] = first[336:368, :]
        down[...] = second[144:336, :]
        out_t[32:48, :] = second[336:352, :]

    core = place[1] & 1
    pl.when(core == 0)(functools.partial(emit, mine, got))
    pl.when(core == 1)(functools.partial(emit, got, mine))


def per_image(*tail):
    return pl.BlockSpec((1,) + tail, lambda n, *_: (n,) + (0,) * len(tail))


def pair(*tail):
    return pl.BlockSpec((2,) + tail, lambda n, *_: (n,) + (0,) * len(tail))


def pair_member(lane, k, *tail):
    return pl.BlockSpec((1,) + tail, lambda n, meta: (meta[2 * n + k, lane],) + (0,) * len(tail))


def small_pair(*tail):
    return pl.BlockSpec(
        (2,) + tail,
        lambda n, meta: (jnp.minimum(n, jnp.maximum(meta[4, 3] - 1, 0)),) + (0,) * len(tail),
    )


def large_pair(*tail):
    return pl.BlockSpec(
        (2,) + tail, lambda n, meta: (jnp.maximum(n - meta[4, 3], 0),) + (0,) * len(tail)
    )


def attention_pairs():
    return [
        small_pair(3 * D_OUT, SMALL),
        small_pair(HEADS, SMALL, SMALL),
        large_pair(3 * D_OUT, LARGE),
        large_pair(HEADS, SLOT, LARGE),
    ]


def whole(*shape):
    return pl.BlockSpec(shape, lambda n, *_: (0,) * len(shape))


def call(
    kernel, micros, grid, in_specs, out_specs, out_shape, scratch, name, *args, aliases=(), vmem=56
):
    return pl.pallas_call(
        kernel,
        grid_spec=pltpu.PrefetchScalarGridSpec(
            num_scalar_prefetch=1,
            grid=grid,
            in_specs=in_specs,
            out_specs=out_specs,
            scratch_shapes=scratch,
        ),
        out_shape=out_shape,
        input_output_aliases=dict(aliases),
        compiler_params=pltpu.CompilerParams(
            dimension_semantics=("arbitrary",), vmem_limit_bytes=vmem * 2**20
        ),
        name=name,
        cost_estimate=pl.CostEstimate(
            flops=micros * 10**9, bytes_accessed=micros * 10**6, transcendentals=0
        ),
    )(*args)


def shape_of(*dims, dtype=BF):
    return jax.ShapeDtypeStruct(dims, dtype)


def packed_rows(count):
    return (count * SLOT + CHUNK - 1) // CHUNK * CHUNK + CHUNK


ANY = pl.BlockSpec(memory_space=pl.ANY)
GATHERED = [ANY, ANY]


def device_prepare(place, token_mask, w_short, w_qkv, w_out, w_up, w_down):
    count = token_mask.shape[0]
    return call(
        prepare_kernel,
        3,
        (1,),
        [
            whole(count, PIX),
            whole(48, D_IN),
            whole(144, D_IN),
            whole(48, D_OUT),
            whole(192, D_OUT),
            whole(192, D_OUT),
        ],
        [whole(count, 128), whole(96, D_OUT), whole(432, D_OUT)],
        [shape_of(count, 128, dtype=jnp.int32), shape_of(96, D_OUT), shape_of(432, D_OUT)],
        [],
        "prepare",
        place,
        token_mask,
        w_short.T,
        w_qkv.T,
        w_out.T,
        w_up.T,
        w_down,
    )


def device_meta(place, token_mask):
    count = token_mask.shape[0]
    return call(
        meta_rows,
        2,
        (1,),
        [whole(count, PIX)],
        [whole(count, 128)],
        [shape_of(count, 128, dtype=jnp.int32)],
        [],
        "meta",
        place,
        token_mask,
    )[0]


def device_front(meta, images, cotangent):
    count = images.shape[0]
    packed = packed_rows(count)
    return call(
        front_kernel,
        15,
        (count // 2,),
        [pair_member(4, k, D_IN, PIX) for k in range(2)]
        + [pair_member(4, k, TOK, D_OUT) for k in range(2)],
        [pair(D_IN, LARGE), whole(packed, D_IN), whole(packed, D_OUT)],
        [
            shape_of(count, D_IN, LARGE, dtype=F32),
            shape_of(packed, D_IN),
            shape_of(packed, D_OUT),
        ],
        [],
        "front",
        meta,
        images,
        images,
        cotangent,
        cotangent,
        vmem=28,
    )


SMALL_OUTPUTS = [(D_IN,)] * 2 + [(D_OUT,)] * 3 + [(FF,), (D_OUT,), (HEADS, SIDE * SIDE)]


def device_finish(place, mine, got):
    return call(
        finish_kernel,
        2,
        (1,),
        [whole(368, D_OUT), whole(368, D_OUT)],
        [
            whole(48, D_IN),
            whole(144, D_IN),
            whole(48, D_OUT),
            whole(192, D_OUT),
            whole(192, D_OUT),
        ]
        + [whole(*dims) for dims in SMALL_OUTPUTS],
        [
            shape_of(48, D_IN, dtype=F32),
            shape_of(144, D_IN, dtype=F32),
            shape_of(48, D_OUT, dtype=F32),
            shape_of(192, D_OUT, dtype=F32),
            shape_of(192, D_OUT, dtype=F32),
        ]
        + [shape_of(*dims, dtype=F32) for dims in SMALL_OUTPUTS],
        [],
        "finish",
        place,
        mine,
        got,
        vmem=12,
    )


def device_tables(rel_table):
    return pl.pallas_call(
        tables_kernel,
        out_shape=shape_of(2, BIAS_ROWS, 128, dtype=F32),
        scratch_shapes=[pltpu.VMEM((3, 192, 128), F32), pltpu.VMEM((16, 768), F32)],
        compiler_params=pltpu.CompilerParams(vmem_limit_bytes=16 * 2**20),
        name="tables",
        cost_estimate=pl.CostEstimate(
            flops=8 * 10**9, bytes_accessed=8 * 10**6, transcendentals=0
        ),
    )(rel_table)


def device_attend(meta, hat, gain, shift, att, bias):
    count = hat.shape[0]
    packed = packed_rows(count)
    return call(
        attend_kernel,
        30,
        (count // 2,),
        [pair(D_IN, LARGE), whole(D_IN), whole(D_IN)]
        + GATHERED
        + [ANY],
        attention_pairs() + [ANY],
        [
            shape_of(count, 3 * D_OUT, SMALL),
            shape_of(count, HEADS, SMALL, SMALL),
            shape_of(count, 3 * D_OUT, LARGE),
            shape_of(count, HEADS, SLOT, LARGE),
            shape_of(packed, D_OUT),
        ],
        [
            pltpu.VMEM((3 * D_OUT, D_IN), BF),
            pltpu.VMEM((2, D_OUT, LARGE), BF),
            pltpu.VMEM((2, 3, SLOT, 4 * LARGE), F32),
            pltpu.VMEM((PARTS, 96, 384), BF),
            pltpu.VMEM((D_IN, 8), F32),
            pltpu.VMEM((2, BIAS_ROWS, 128), F32),
            pltpu.VMEM((2, CHUNK, D_OUT), BF),
            pltpu.SemaphoreType.DMA((PARTS,)),
            pltpu.SemaphoreType.DMA((2,)),
            pltpu.SemaphoreType.DMA,
        ],
        "attend",
        meta,
        hat,
        gain,
        shift,
        *att,
        bias,
        vmem=36,
    )


def device_dense(meta, plain, cotp, mixed, att, ff, params):
    packed = plain.shape[0]
    rows_of = lambda width: pl.BlockSpec(
        (CHUNK, width), lambda n, meta: (jnp.minimum(n, meta[3, 3]), 0)
    )
    return call(
        dense_kernel,
        40,
        (packed // CHUNK,),
        [rows_of(D_IN), rows_of(D_OUT), rows_of(D_OUT)]
        + GATHERED
        + GATHERED
        + [whole(D_OUT)] * 4
        + [whole(FF)],
        [
            rows_of(D_OUT),
            rows_of(D_OUT),
            rows_of(D_IN),
            whole(PARTS, 224, 384),
            whole(PARTS, 224, 384),
            whole(D_OUT, D_IN),
            whole(8, D_OUT),
        ],
        [
            shape_of(packed, D_OUT),
            shape_of(packed, D_OUT),
            shape_of(packed, D_IN),
            shape_of(PARTS, 224, 384),
            shape_of(PARTS, 224, 384),
            shape_of(D_OUT, D_IN),
            shape_of(8, D_OUT, dtype=F32),
        ],
        [
            pltpu.VMEM((D_OUT, D_IN), BF),
            pltpu.VMEM((D_OUT, D_OUT), BF),
            pltpu.VMEM((FF, D_OUT), BF),
            pltpu.VMEM((FF, D_OUT), BF),
            pltpu.VMEM((D_OUT, FF), F32),
            pltpu.VMEM((D_OUT, FF), F32),
            pltpu.VMEM((D_OUT, D_OUT), F32),
            pltpu.VMEM((D_OUT, D_IN), F32),
            pltpu.VMEM((32, D_OUT), F32),
            pltpu.VMEM((8, FF), F32),
            pltpu.VMEM((PARTS, 96, 384), BF),
            pltpu.SemaphoreType.DMA((PARTS,)),
            pltpu.SemaphoreType.DMA((3 * PARTS,)),
        ],
        "dense",
        meta,
        plain,
        cotp,
        mixed,
        *att,
        *ff,
        *params,
        vmem=40,
    )


def device_expand(meta, outp, count):
    return call(
        expand_kernel,
        5,
        (count // 4,),
        [whole(*outp.shape)],
        [pl.BlockSpec((4, TOK, D_OUT), lambda n, *_: (n, 0, 0))],
        [shape_of(count, TOK, D_OUT)],
        [],
        "expand",
        meta,
        outp,
        vmem=24,
    )[0]


def device_attend_back(meta, hat, gain, shift, att, kept, gmix, gplain, gshort, small):
    count = hat.shape[0]
    packed = gmix.shape[0]
    return call(
        attend_back_kernel,
        40,
        (count // 2,),
        [pair(D_IN, LARGE), whole(D_IN), whole(D_IN)]
        + GATHERED
        + attention_pairs()
        + [
            ANY,
            ANY,
            whole(D_OUT, D_IN),
            whole(8, 384),
        ],
        [pair(2 * D_IN, LARGE), whole(480, 384), whole(480, 384), whole(48, 384)],
        [
            shape_of(count, 2 * D_IN, LARGE),
            shape_of(480, 384),
            shape_of(480, 384),
            shape_of(48, 384, dtype=F32),
        ],
        [
            pltpu.VMEM((3 * D_OUT, D_IN), BF),
            pltpu.VMEM((D_IN, 3 * D_OUT), BF),
            pltpu.VMEM((2, D_OUT, LARGE), BF),
            pltpu.VMEM((2, 3, SLOT, 4 * LARGE), F32),
            pltpu.VMEM((2, HEADS, SLOT, LARGE), BF),
            pltpu.VMEM((3 * D_OUT, 2 * LARGE), BF),
            pltpu.VMEM((3 * D_OUT, D_IN), F32),
            pltpu.VMEM((2, BIAS_ROWS, 128), F32),
            pltpu.VMEM((2, D_IN, 128), F32),
            pltpu.VMEM((6, 256, 128), F32),
            pltpu.VMEM((PARTS, 96, 384), BF),
            pltpu.VMEM((D_IN, 8), F32),
            pltpu.VMEM((2, 2 * SLOT, D_OUT), BF),
            pltpu.VMEM((2, 2 * SLOT, D_IN), BF),
            pltpu.VMEM((2, 384, 384), BF),
            pltpu.SemaphoreType.DMA((PARTS,)),
            pltpu.SemaphoreType.DMA((2, 2)),
        ],
        "attend_back",
        meta,
        hat,
        gain,
        shift,
        *att,
        *kept,
        gmix,
        gplain,
        gshort,
        small,
        vmem=52,
    )


def device_front_back(meta, images, grads, first, count, before=None):
    some = lambda *tail: pl.BlockSpec(
        (2,) + tail, lambda n, *_: (n + first,) + (0,) * len(tail)
    )
    member = lambda k, *tail: pl.BlockSpec(
        (1,) + tail, lambda n, meta: (meta[2 * (n + first) + k, 5],) + (0,) * len(tail)
    )
    chained = before is not None
    return call(
        functools.partial(front_back_kernel, first, chained),
        1,
        (count,),
        [some(D_IN, PIX)]
        + [member(k, 2 * D_IN, LARGE) for k in range(2)]
        + ([ANY] if chained else []),
        [some(D_IN, PIX)],
        [shape_of(*images.shape)],
        [],
        "front_back",
        meta,
        images,
        grads,
        grads,
        *([before] if chained else []),
        aliases={4: 0} if chained else {},
        vmem=24,
    )[0]


def shard_grads(ff, qs):
    g_up, g_down = ff[0][:192].T, ff[1][:192]
    g_out = jnp.concatenate([ff[0][192:224], ff[1][192:208]], axis=0).T
    g_qkv = jnp.concatenate([qs[:, :192], qs[:48, 192:]], axis=0).T
    g_short = qs[48:, 192:].T
    return g_short, g_qkv, g_out, g_up, g_down


def tied(*values):
    return lax.optimization_barrier(values)


class FastLinks:
    def __init__(self):
        self.own = lax.axis_index("wide")
        self.narrow = lax.axis_index("narrow")

    def across(self, value, bit):
        return lax.ppermute(value, "narrow", [(i, i ^ bit) for i in range(4)])

    def along(self, value, bits):
        return lax.ppermute(value, "wide", [(i, i ^ bits) for i in range(PARTS)])

    def spread(self, value, bits):
        pairs = [
            (4 * w + k, 4 * (w ^ k ^ bits) + k) for w in range(PARTS) for k in range(4)
        ]
        return lax.ppermute(value, ("wide", "narrow"), pairs)

    def fetch_two(self, value):
        return jnp.stack([self.spread(value, 0), self.spread(value, 5)])


def rounded(value):
    return lax.reduce_precision(value, 8, 7)


def low_sum(left, right):
    return rounded(left.astype(F32) + right.astype(F32)).astype(BF)


def high_sum(left, right):
    return left.astype(F32) + right.astype(F32)


def two_rows(value):
    high = rounded(value)
    return jnp.concatenate([high, rounded(value - high)], axis=0).astype(BF)


def one_row(pair):
    half = pair.shape[0] // 2
    return high_sum(pair[:half], pair[half:])


def tree(parts):
    while len(parts) > 1:
        parts = [high_sum(parts[k], parts[k + 1]) for k in range(0, len(parts), 2)]
    return parts[0]


class PlainLinks:
    own = 0
    narrow = 0

    def gather_weights(self, w_short, w_qkv, w_out, w_up, w_down):
        full = [
            lax.all_gather(w.astype(BF), "wide", axis=axis, tiled=True)
            for w, axis in ((w_short, 1), (w_qkv, 1), (w_out, 1), (w_up, 1), (w_down, 0))
        ]

        def shard(j):
            short, qkv, out, up, down = (
                lax.slice_in_dim(w, j * size, (j + 1) * size, axis=axis)
                for w, size, axis in zip(full, (48, 144, 48, 192, 192), (1, 1, 1, 1, 0))
            )
            qs = jnp.concatenate([qkv.T, short.T], axis=0)
            qs = jnp.concatenate([qs[:96], qs[96:]], axis=1)
            return qs, jnp.concatenate([up.T, down, out.T], axis=0)

        parts = [shard(j) for j in (0, 5, 2, 7, 1, 4, 3, 6)]
        return tuple(
            (jnp.stack([p[k] for p in parts[:4]]), jnp.stack([p[k] for p in parts[4:]]))
            for k in range(2)
        )

    def reduce_grads(self, gff, gqs):
        order = [0, 5, 2, 7, 1, 4, 3, 6]
        gqs = jnp.concatenate([half[:384].reshape(4, 96, 384) for half in gqs])
        parts = [shard_grads([g[j] for g in gff], gqs[order.index(j)]) for j in range(PARTS)]
        out = []
        for k, axis in enumerate((1, 1, 1, 1, 0)):
            whole_grad = jnp.concatenate([p[k] for p in parts], axis=axis)
            shard = lax.psum_scatter(whole_grad, "wide", scatter_dimension=axis, tiled=True)
            out.append(lax.psum(shard, "narrow").astype(F32))
        return out


def outputs(output, grad_images, weights, small):
    table = jnp.concatenate([small[16 : 16 + HEADS], small[32 : 32 + HEADS]], axis=1)
    return (
        output,
        jnp.swapaxes(grad_images, 1, 2),
        *weights,
        small[8, :192],
        small[8, 192:],
        small[0],
        small[1],
        small[2],
        small[4:8].reshape(FF),
        small[3],
        table[:, : SIDE * SIDE],
    )


def shards_plain(
    images, token_mask, w_short, w_qkv, w_out, w_up, w_down, ln1_gain, ln1_shift, out_bias,
    ln2_gain, ln2_shift, up_bias, down_bias, rel_table, cotangent,
):
    links = PlainLinks()
    count = images.shape[0]
    images = jnp.swapaxes(images, 1, 2)
    ln1 = (ln1_gain, ln1_shift)
    params = (out_bias, ln2_gain, ln2_shift, down_bias, up_bias)
    meta = device_meta(jnp.zeros((2,), jnp.int32), token_mask)
    att, ff = links.gather_weights(w_short, w_qkv, w_out, w_up, w_down)
    hat, plain, cotp = device_front(meta, images, cotangent)
    bias = device_tables(rel_table)
    *kept, mixed = device_attend(meta, hat, *ln1, att, bias)
    outp, gmix, gplain, *gff, gshort, small = device_dense(
        meta, plain, cotp, mixed, att, ff, params
    )
    output = device_expand(meta, outp, count)
    grads, *gqs, small = device_attend_back(
        meta, hat, *ln1, att, kept, gmix, gplain, gshort, small
    )
    grad_images = device_front_back(meta, images, grads, 0, count // 2)
    small = lax.psum(small, ("wide", "narrow"))
    return outputs(output, grad_images, links.reduce_grads(gff, gqs), small)


def shards_fast(
    images, token_mask, w_short, w_qkv, w_out, w_up, w_down, ln1_gain, ln1_shift, out_bias,
    ln2_gain, ln2_shift, up_bias, down_bias, rel_table, cotangent,
):
    links = FastLinks()
    count = images.shape[0]
    images = jnp.swapaxes(images, 1, 2)
    ln1 = (ln1_gain, ln1_shift)
    params = (out_bias, ln2_gain, ln2_shift, down_bias, up_bias)
    place = jnp.stack([links.own, links.narrow]).astype(jnp.int32)
    meta, att, ff = device_prepare(place, token_mask, w_short, w_qkv, w_out, w_up, w_down)

    att, ff = links.fetch_two(att), links.fetch_two(ff)
    hat, plain, cotp = device_front(meta, images, cotangent)
    att, hat, rel_table = tied(att, hat, rel_table)
    att = jnp.concatenate([att, links.across(att, 2)])
    bias = device_tables(rel_table)
    att, bias, ff = tied(att, bias, ff)
    att = (att, links.across(att, 1))
    ff_more = links.across(ff, 2)
    *kept, mixed = device_attend(meta, hat, *ln1, att, bias)
    ff_more, mixed = tied(ff_more, mixed)
    ff = jnp.concatenate([ff, ff_more])
    ff_other = links.across(ff, 1)
    outp, gmix, gplain, gff_kept, gff_sent, gshort, small = device_dense(
        meta, plain, cotp, mixed, att, (ff, ff_other), params
    )

    got = links.across(gff_sent, 1)
    output = device_expand(meta, outp, count)
    got, output, gmix = tied(got, output, gmix)
    terms = [low_sum(gff_kept[d], got[d]) for d in range(PARTS)]
    far = (7, 6, 5, 4, 3)
    moved = {d: links.along(terms[d], d) for d in far}
    grads, gqs_kept, gqs_sent, small = device_attend_back(
        meta, hat, *ln1, att, kept, gmix, gplain, gshort, small
    )
    tie = tied(grads, gqs_kept, gqs_sent, *terms[1:3], *(moved[d] for d in far))
    grads, gqs_kept, gqs_sent = tie[:3]
    pairs = count // 2
    cuts = [k * pairs // 8 for k in (0, 2, 5, 7, 8)]
    done = None

    def beside(k, *got):
        piece = device_front_back(meta, images, grads, cuts[k], cuts[k + 1] - cuts[k], done)
        return tied(piece, *got)

    got = links.across(gqs_sent, 1)
    near = [links.along(tie[2 + d], d) for d in (1, 2)]
    done, got, *near = beside(0, got, *near)
    terms[1:] = [*near, *reversed(tie[5:])]
    held = low_sum(gqs_kept[:384], got[:384])
    small = one_row(gqs_kept[384:]) + one_row(got[384:])
    small = two_rows(small)
    sent, done = tied(jnp.concatenate([held[192:], small]), done)
    got = links.across(sent, 2)
    done, got, *terms = beside(1, got, *terms)
    held = low_sum(held[:192], got[:192])
    small = two_rows(one_row(small) + one_row(got[192:]))
    ff_sum = rounded(tree(terms)).astype(BF)
    *sent, ff_sum, done = tied(
        jnp.concatenate([held[:96], small]), jnp.concatenate([held[96:], small]), ff_sum, done
    )
    got = links.spread(sent[0], 0), links.spread(sent[1], 5)
    ff_got = links.across(ff_sum, 2)
    done, ff_got, *got = beside(2, ff_got, *got)
    held = low_sum(got[0][:96], got[1][:96])
    small = two_rows(one_row(got[0][96:]) + one_row(got[1][96:]))
    mine, done = tied(jnp.concatenate([held, small]), done)
    got = links.across(mine, 2)
    done, got, ff_sum, ff_got = beside(3, got, ff_sum, ff_got)
    mine = jnp.concatenate(
        [
            high_sum(mine[:96], got[:96]),
            one_row(mine[96:]) + one_row(got[96:]),
            high_sum(ff_sum, ff_got),
        ]
    )
    last = device_finish(place, mine, links.across(mine, 1))
    return (output, jnp.swapaxes(done, 1, 2), *(w.T for w in last[:4]), *last[4:])


def solution(mesh):
    data = ("wide", "narrow")
    rows = P(None, "wide")
    in_specs = (
        (P(data, None, None), P(data, None), rows, rows, rows, rows, P("wide", None))
        + (P(),) * 8
        + (P(data, None, None),)
    )
    out_specs = (
        (P(data, None, None), P(data, None, None), rows, rows, rows, rows, P("wide", None))
        + (P(),) * 8
    )
    fast = mesh.shape["wide"] == PARTS and mesh.shape["narrow"] == 4
    return jax.shard_map(
        shards_fast if fast else shards_plain,
        mesh=mesh,
        in_specs=in_specs,
        out_specs=out_specs,
        check_vma=False,
    )
```

```python
import functools
import math

import jax
import jax.numpy as jnp
from jax import lax
from jax.experimental import pallas as pl
from jax.experimental.pallas import tpu as pltpu
from jax.sharding import PartitionSpec as P

D_IN = 192
D_OUT = 384
HEADS = 12
HEAD_DIM = 32
FF = 1536
GRID = 14
SIDE = 2 * GRID - 1
TOK = GRID * GRID
PIX = 4 * TOK
EPS = 1e-05
LOG2E = math.log2(math.e)
SCORE_SCALE = HEAD_DIM ** (-0.5)

SLOT = 208
SMALL = 128
LARGE = 256
WIDE_ROWS = 16 * GRID
NARROW_ROWS = 16 * 8
BIAS_ROWS = HEADS * (WIDE_ROWS + NARROW_ROWS)
CHUNK = 480
WIDTH = 768
PARTS = 8
BF = jnp.bfloat16
F32 = jnp.float32
NN = (((1,), (0,)), ((), ()))
NT = (((1,), (1,)), ((), ()))
TN = (((0,), (0,)), ((), ()))


def mm(left, right, dims=NN):
    return lax.dot_general(left, right, dims, preferred_element_type=F32)


def iota(shape, dim):
    return lax.broadcasted_iota(jnp.int32, shape, dim)


def geometry(meta, n):
    high, wide = meta[n, 0], meta[n, 1]
    rows, cols = (high + 1) >> 1, (wide + 1) >> 1
    return high, wide, rows, cols, meta[n, 6]


def cell_of(index, stride):
    row = jnp.where(stride == 8, index >> 3, (index * 4682) >> 16)
    return row, index - stride * row


def packed_index(index, stride, rows, cols):
    row, col = cell_of(index, stride)
    return jnp.where((col < cols) & (row < rows), row * cols + col, -1)


def onehot(mask):
    return jnp.where(mask, 1.0, 0.0).astype(BF)


def packing(shape, stride, rows, cols):
    return onehot(iota(shape, 0) == packed_index(iota((1, shape[1]), 1), stride, rows, cols))


def unpacking(shape, stride, rows, cols):
    return onehot(iota(shape, 1) == packed_index(iota((shape[0], 1), 0), stride, rows, cols))


def split_two(values):
    high = values.astype(BF)
    return high, (values - high.astype(F32)).astype(BF)


def shift_map(cell, stride, lanes):
    spot = iota((1, lanes), 1)
    row, col = cell_of(spot, stride)
    pick = jnp.where((row < GRID) & (col < GRID), SIDE * row + col - cell + GRID - 1, -1)
    return onehot(iota((384, lanes), 0) == pick)


def token_of_pixel(shape, dim, high, wide, stride):
    spot = iota(shape, dim)
    row = (spot * 2341) >> 16
    col = spot - 28 * row
    return jnp.where((row < high) & (col < wide), (row >> 1) * stride + (col >> 1), -1)


def window_share(shape, dim, high, wide, stride):
    row, col = cell_of(iota(shape, dim), stride)
    return jnp.where(2 * row + 1 < high, 0.5, 1.0) * jnp.where(2 * col + 1 < wide, 0.5, 1.0)


def norm_stats(values, axis=0):
    center = jnp.mean(values, axis=axis, keepdims=True)
    shifted = values - center
    spread = jnp.mean(shifted * shifted, axis=axis, keepdims=True)
    return shifted, lax.rsqrt(spread + EPS)


def prepare_kernel(place, mask, short_t, qkv_t, out_t, up_t, down, meta, att, ff):
    att[0:96, 0:192] = qkv_t[0:96, :].astype(BF)
    att[0:48, 192:384] = qkv_t[96:144, :].astype(BF)
    att[48:96, 192:384] = short_t[...].astype(BF)
    ff[0:192, :] = up_t[...].astype(BF)
    ff[192:384, :] = down[...].astype(BF)
    ff[384:432, :] = out_t[...].astype(BF)
    meta_rows(place, mask, meta)


def meta_rows(place, mask, meta):
    count = mask.shape[0]
    ones = mask[...]
    spot = iota(ones.shape, 1)
    row = (spot * 2341) >> 16
    high = jnp.sum(jnp.where(spot == 28 * row, ones, 0).astype(F32), axis=1, keepdims=True)
    wide = jnp.sum(jnp.where(spot < 28, ones, 0).astype(F32), axis=1, keepdims=True)

    def along(column):
        return jnp.broadcast_to(column, (count, 128)).T[:count]

    def total(values):
        return jnp.sum(values, axis=1, keepdims=True)

    rows = (high.astype(jnp.int32) + 1) >> 1
    cols = (wide.astype(jnp.int32) + 1) >> 1
    image = iota((count, 1), 0)
    stride = jnp.where(cols <= 8, 8, GRID)
    key = (stride * rows * count + image).astype(F32)
    rank = total(jnp.where(along(key) < key, 1.0, 0.0))
    chosen = along(rank) == image.astype(F32)

    def sort(column):
        return total(jnp.where(chosen, along(column), 0.0))

    taken = sort(((((rows * cols) + 15) >> 4) << 4).astype(F32))
    small = total(jnp.where(along(key) < SMALL * count + count, 1.0, 0.0)).astype(jnp.int32)
    start = total(jnp.where(iota((count, count), 1) < image, along(taken), 0.0))
    packed = total(along(taken)).astype(jnp.int32)
    chunks = ((packed + CHUNK - 1) * 2185) >> 20
    extra = jnp.where(image == 0, packed, jnp.where(image == 3, chunks, small >> 1))
    extra = jnp.where(image == 1, place[0], jnp.where(image == 2, place[1], extra))
    lane = iota((count, 128), 1)
    result = jnp.zeros((count, 128), jnp.int32)
    stride = jnp.where(image < (small >> 1) * 2, sort(stride.astype(F32)), float(GRID))
    columns = (sort(high), sort(wide), start, extra, sort(image.astype(F32)), rank, stride)
    for k, column in enumerate(columns):
        result = jnp.where(lane == k, column.astype(jnp.int32), result)
    meta[...] = result


def front_kernel(meta, img_a, img_b, cot_a, cot_b, hat, plain, cotp):
    n = pl.program_id(0)
    geo = [geometry(meta, 2 * n), geometry(meta, 2 * n + 1)]
    starts = [pl.multiple_of(meta[2 * n + k, 2], 16) for k in range(2)]

    def body(pixels, size, psize):
        sums = []
        for k, img in enumerate((img_a, img_b)):
            high, wide, rows, cols, stride = geo[k]
            values = img[0, :, :pixels]
            shifted, scale = norm_stats(values.astype(F32))
            normed = (shifted * scale).astype(BF)
            token = token_of_pixel((pixels, 1), 0, high, wide, stride)
            pick = onehot(iota((pixels, size), 1) == token)
            share = window_share((1, size), 1, high, wide, stride)
            sums.append(mm(jnp.concatenate([normed, values], axis=0), pick) * share)
        packed = []
        for k, cot in enumerate((cot_a, cot_b)):
            high, wide, rows, cols, stride = geo[k]
            hat[k, :, :size] = sums[k][:D_IN]
            pick = packing((psize, size), stride, rows, cols)
            first = mm(pick, sums[k][D_IN:].astype(BF), NT).astype(BF)
            pick = packing((psize, TOK), GRID, rows, cols)
            packed.append((first, mm(pick, cot[0]).astype(BF)))
        for k in range(2):
            plain[pl.ds(starts[k], psize), :] = packed[k][0]
            cotp[pl.ds(starts[k], psize), :] = packed[k][1]

    short = (geo[0][0] <= 18) & (geo[1][0] <= 18)
    large = geo[1][4] * geo[1][2] > SMALL
    pl.when(short & jnp.logical_not(large))(functools.partial(body, 512, SMALL, SMALL))
    pl.when(jnp.logical_not(short | large))(functools.partial(body, PIX, SMALL, SMALL))
    pl.when(large)(functools.partial(body, PIX, LARGE, SLOT))

    @pl.when(n == pl.num_programs(0) - 1)
    def _():
        total = pl.multiple_of(meta[0, 3], 16)
        plain[pl.ds(total, CHUNK), :] = jnp.zeros((CHUNK, D_IN), BF)
        cotp[pl.ds(total, CHUNK), :] = jnp.zeros((CHUNK, D_OUT), BF)


def tables_kernel(tab, bias, shift_scr, table_scr):
    shift_scr[...] = jnp.zeros_like(shift_scr)
    table_scr[...] = jnp.zeros_like(table_scr)
    table_scr[:HEADS, : SIDE * SIDE] = tab[...] * LOG2E
    table = table_scr[...]
    for r in range(GRID):
        moved = pltpu.roll(table, (768 - SIDE * (GRID - 1 - r)) % 768, 1)
        for k in range(3):
            shift_scr[k, pl.ds(r, HEADS, stride=16), :] = moved[
                :HEADS, 128 * k : 128 * k + 128
            ]
    top, rest = split_two(jnp.concatenate([shift_scr[k] for k in range(3)], axis=1))
    for cell in range(GRID):
        pick = shift_map(cell, GRID, 256)
        spread = mm(top, pick) + mm(rest, pick)
        for k in range(2):
            bias[k, pl.ds(cell, 192, stride=GRID), :] = spread[:, 128 * k : 128 * k + 128]
    for cell in range(8):
        pick = shift_map(cell, 8, 128)
        bias[0, pl.ds(HEADS * WIDE_ROWS + cell, 192, stride=8), :] = mm(top, pick) + mm(
            rest, pick
        )


def shard_at(meta, e):
    step = (2 if e & 2 else 0) ^ (5 if e & 1 else 0) ^ (1 if e >= 4 else 0)
    return meta[1, 3] ^ meta[2, 3] ^ step


def fetch_shards(meta, mine, other, dest, sems):
    copies = []
    for e in range(PARTS):
        source = mine if e < 4 else other
        copies.append(
            pltpu.make_async_copy(source.at[e & 3], dest.at[shard_at(meta, e)], sems.at[e])
        )
    for copy in copies:
        copy.start()
    return copies


def unpack_qkv(att, qkv_scr):
    for j in range(PARTS):
        qkv_scr[144 * j : 144 * j + 96, :] = att[j, 0:96, 0:192]
        qkv_scr[144 * j + 96 : 144 * j + 144, :] = att[j, 0:48, 192:384]


def slot_valid(shape, dim, stride, rows, cols):
    row, col = cell_of(iota(shape, dim), stride)
    return (col < cols) & (row < rows)


def row_of(vector):
    return vector[...].reshape(1, vector.shape[0])


def columns_of(gain, shift, dest):
    rows = jnp.concatenate(
        [row_of(gain), row_of(shift), jnp.zeros((6, D_IN), F32)], axis=0
    )
    dest[...] = rows.T


def spread_heads(block, tail=None):
    size = block.shape[1]
    parts = []
    for j in range(4):
        rows = [block[32 * j : 32 * j + 32]]
        if j > 0:
            rows.insert(0, jnp.zeros((32 * j, size), BF))
        if j < 3:
            rows.append(jnp.zeros((96 - 32 * j, size), BF))
        if tail is not None:
            rows.append(tail)
        parts.append(jnp.concatenate(rows, axis=0))
    return jnp.concatenate(parts, axis=1)


def table_row(head, stride):
    row = jnp.where(stride == 8, HEADS * WIDE_ROWS + head * NARROW_ROWS, head * WIDE_ROWS)
    return pl.multiple_of(row, 8)


def pooled_pair(geo, size, hat, gain_scr):
    lane_ok = [slot_valid((1, size), 1, g[4], g[2], g[3]) for g in geo]
    pooled = [
        jnp.where(lane_ok[k], hat[k, :, :size] * gain_scr[:, 0:1] + gain_scr[:, 1:2], 0.0)
        for k in range(2)
    ]
    return lane_ok, jnp.concatenate(pooled, axis=1).astype(BF)


def attend_kernel(
    meta, hat, gain, shift, att_mine, att_other, bias,
    qkvt_small, probs_small, qkvt_large, probs_large, mixed, token,
    wqkv_scr, mix_scr, score_scr, att_scr, gain_scr, bias_scr, rows_scr, sems, bias_sems, rows_sem,
):
    n = pl.program_id(0)
    token[...] = jnp.zeros_like(token)
    fetch_bias = [
        pltpu.make_async_copy(bias.at[0], bias_scr.at[0], bias_sems.at[0]),
        pltpu.make_async_copy(
            bias.at[1, pl.ds(0, HEADS * WIDE_ROWS)],
            bias_scr.at[1, pl.ds(0, HEADS * WIDE_ROWS)],
            bias_sems.at[1],
        ),
    ]

    def put_rows(pair, size):
        first = pl.multiple_of(meta[2 * pair, 2], 16)
        return pltpu.make_async_copy(
            rows_scr.at[pair & 1, pl.ds(0, size)], mixed.at[pl.ds(first, size)], rows_sem
        )

    def wait_rows(pair):
        pl.when(pair < meta[4, 3])(lambda: put_rows(pair, 2 * SMALL).wait())
        pl.when(pair >= meta[4, 3])(lambda: put_rows(pair, 2 * SLOT).wait())

    geo = [geometry(meta, 2 * n), geometry(meta, 2 * n + 1)]
    starts = [pl.multiple_of(meta[2 * n + k, 2], 16) for k in range(2)]

    @pl.when(n == 0)
    def _():
        for copy in fetch_bias:
            copy.start()
        copies = fetch_shards(meta, att_mine, att_other, att_scr, sems)
        columns_of(gain, shift, gain_scr)
        for copy in copies:
            copy.wait()
        unpack_qkv(att_scr, wqkv_scr)
        for copy in fetch_bias:
            copy.wait()

    def body(size, keys, psize, qkvt, probs):
        lane_ok, pooled = pooled_pair(geo, size, hat, gain_scr)
        qkv = mm(wqkv_scr[...], pooled).astype(BF)
        first_row = iota((16, size), 0) == 0
        ones = onehot(first_row)
        for k in range(2):
            qkvt[k] = qkv[:, size * k : size * k + size]
        for k in range(2):
            closed = jnp.where(first_row & ~lane_ok[k], -1e30, 0.0).astype(BF)
            for g in range(3):
                key = jnp.concatenate([qkvt[k, 384 + 128 * g : 512 + 128 * g, :], closed], axis=0)
                query = spread_heads(qkvt[k, 128 * g : 128 * g + 128, :], ones)
                score_scr[k, g, :keys, : 4 * size] = mm(key.T[:keys], query)
        for head in range(HEADS):
            at = size * (head % 4)
            for k in range(2):
                scores = score_scr[k, head // 4, :keys, at : at + size] * (SCORE_SCALE * LOG2E)
                if size == SMALL:
                    scores += bias_scr[0, pl.ds(table_row(head, geo[k][4]), keys), :]
                else:
                    scores += jnp.concatenate(
                        [
                            bias_scr[j, pl.ds(table_row(head, geo[k][4]), keys), :]
                            for j in range(2)
                        ],
                        axis=1,
                    )
                expo = jnp.exp2(scores - jnp.max(scores, axis=0, keepdims=True))
                share = expo * (1.0 / jnp.sum(expo, axis=0, keepdims=True))
                probs[k, head] = share.astype(BF)
        for head in range(HEADS):
            at = HEAD_DIM * head
            for k in range(2):
                value = qkvt[k, 768 + at : 800 + at, :keys]
                mix_scr[k, at : at + 32, :size] = mm(value, probs[k, head]).astype(BF)
        packed = []
        for k in range(2):
            pick = packing((psize, size), geo[k][4], geo[k][2], geo[k][3])
            packed.append(mm(pick, mix_scr[k, :, :size], NT).astype(BF))
        slot = n & 1
        rows_scr[slot, 0:psize, :] = packed[0]
        second = pl.multiple_of(starts[1] - starts[0], 16)
        rows_scr[slot, pl.ds(second, psize), :] = packed[1]
        pl.when(n > 0)(lambda: wait_rows(n - 1))
        put_rows(n, 2 * psize).start()

    pl.when(n < meta[4, 3])(
        functools.partial(body, SMALL, SMALL, SMALL, qkvt_small, probs_small)
    )
    pl.when(n >= meta[4, 3])(functools.partial(body, LARGE, SLOT, SLOT, qkvt_large, probs_large))

    @pl.when(n == pl.num_programs(0) - 1)
    def _():
        wait_rows(n)
        total = pl.multiple_of(meta[0, 3], 16)
        rows_scr[0, 0:CHUNK, :] = jnp.zeros((CHUNK, D_OUT), BF)
        blank = pltpu.make_async_copy(
            rows_scr.at[0, pl.ds(0, CHUNK)], mixed.at[pl.ds(total, CHUNK)], rows_sem
        )
        blank.start()
        blank.wait()


def gelu_both(x):
    bell = jnp.exp2((x * x) * (-0.5 * LOG2E))
    half = 0.5 + 0.5 * lax.erf(x * math.sqrt(0.5))
    return x * half, half + (x * bell) * (1.0 / math.sqrt(2.0 * math.pi))


def dense_kernel(
    meta, plain, cotp, mixed, att_mine, att_other, ff_mine, ff_other,
    outbias, gain, shift, downbias, upbias, token,
    outp, gmix, gplain, gff_kept, gff_sent, gshort, small,
    wshort_scr, wout_scr, wup_scr, wdown_scr, up_acc, down_acc, out_acc, short_acc, small_acc,
    up_small, att_scr, att_sems, ff_sems,
):
    i = pl.program_id(0)

    @pl.when(i == 0)
    def _():
        ff_copies = []
        for e in range(PARTS):
            source = (ff_mine if e < 4 else ff_other).at[e & 3]
            shard = shard_at(meta, e)
            for k, (dest, low, size) in enumerate(
                ((wup_scr, 0, 192), (wdown_scr, 192, 192), (wout_scr, 384, 48))
            ):
                ff_copies.append(
                    pltpu.make_async_copy(
                        source.at[pl.ds(low, size)],
                        dest.at[pl.ds(pl.multiple_of(shard * size, 16), size)],
                        ff_sems.at[3 * e + k],
                    )
                )
        for copy in ff_copies:
            copy.start()
        for copy in fetch_shards(meta, att_mine, att_other, att_scr, att_sems):
            copy.wait()
        for j in range(PARTS):
            wshort_scr[48 * j : 48 * j + 48, :] = att_scr[j, 48:96, 192:384]
        up_acc[...] = jnp.zeros_like(up_acc)
        down_acc[...] = jnp.zeros_like(down_acc)
        out_acc[...] = jnp.zeros_like(out_acc)
        short_acc[...] = jnp.zeros_like(short_acc)
        small_acc[...] = jnp.zeros_like(small_acc)
        up_small[...] = jnp.zeros_like(up_small)
        for copy in ff_copies:
            copy.wait()

    @pl.when(i < meta[3, 3])
    def _():
        out_bias, ln_gain, ln_shift, down_bias = map(row_of, (outbias, gain, shift, downbias))
        up_bias = row_of(upbias)
        wout = wout_scr[...]
        wshort = wshort_scr[...]
        first = mm(plain[...], wshort, NT) + mm(mixed[...], wout, NT) + out_bias
        shifted, scale = norm_stats(first, -1)
        hat = shifted * scale
        normed = (hat * ln_gain + ln_shift).astype(BF)
        normed_t = normed.T
        cot = cotp[...]
        cot_t = cot.T
        branch = jnp.zeros((CHUNK, D_OUT), F32)
        grad_normed = jnp.zeros((CHUNK, D_OUT), F32)
        one_rows = jnp.ones((8, CHUNK), BF)
        for j in range(FF // WIDTH):
            some = slice(WIDTH * j, WIDTH * j + WIDTH)
            hidden = mm(normed, wup_scr[some, :], NT) + up_bias[:, some]
            grad_act = mm(cot, wdown_scr[some, :], NT)
            act, slope = gelu_both(hidden)
            act = act.astype(BF)
            grad_hidden = (grad_act * slope).astype(BF)
            branch += mm(act, wdown_scr[some, :])
            grad_normed += mm(grad_hidden, wup_scr[some, :])
            up_acc[:, some] += mm(normed_t, grad_hidden)
            down_acc[:, some] += mm(cot_t, act)
            up_small[:, some] += mm(one_rows, grad_hidden)
        outp[...] = (first + branch + down_bias).astype(BF)
        grad_branch = cot.astype(F32)
        grad_hat = grad_normed * ln_gain
        center = jnp.mean(grad_hat, axis=-1, keepdims=True)
        along = jnp.mean(grad_hat * hat, axis=-1, keepdims=True)
        grad_first = grad_branch + scale * (grad_hat - center - hat * along)
        low = grad_first.astype(BF)
        low_t = low.T
        gmix[...] = mm(low, wout).astype(BF)
        gplain[...] = mm(low, wshort).astype(BF)
        out_acc[...] += mm(low_t, mixed[...])
        short_acc[...] += mm(low_t, plain[...])

        def fold(values):
            return jnp.sum(values.reshape(CHUNK // 8, 8, D_OUT), axis=0)

        small_acc[0:8, :] += fold(grad_first)
        small_acc[8:16, :] += fold(grad_normed * hat)
        small_acc[16:24, :] += fold(grad_normed)
        small_acc[24:32, :] += fold(grad_branch)

    @pl.when(i == meta[3, 3])
    def _():
        for ref in (outp, gmix, gplain):
            ref[...] = jnp.zeros_like(ref)

    @pl.when(i == meta[3, 3] - 1)
    def _():
        own, core = meta[1, 3], meta[2, 3] & 1

        def emit(kept, sent):
            for j in range(PARTS):
                at = own ^ j
                kept[at, 0:192, :] = up_acc[:, 192 * j : 192 * j + 192].astype(BF).T
                sent[at, 0:192, :] = down_acc[:, 192 * j : 192 * j + 192].astype(BF).T
                out_rows = out_acc[48 * j : 48 * j + 48, :].astype(BF)
                kept[at, 192:224, :] = out_rows[0:32]
                sent[at, 192:208, :] = out_rows[32:48]
                sent[at, 208:224, :] = jnp.zeros((16, D_OUT), BF)

        pl.when(core == 0)(functools.partial(emit, gff_kept, gff_sent))
        pl.when(core == 1)(functools.partial(emit, gff_sent, gff_kept))
        gshort[...] = short_acc[...].astype(BF)
        for k in range(4):
            total = small_acc[8 * k : 8 * k + 8, :]
            small[k : k + 1, :] = jnp.sum(total, axis=0, keepdims=True)
            small[4 + k : 5 + k, :] = up_small[0:1, 384 * k : 384 * k + 384]


def expand_kernel(meta, outp, out):
    n = pl.program_id(0)
    at = [meta[4 * n + k, 5] for k in range(4)]
    geo = [geometry(meta, p) for p in at]

    def body(size):
        for k in range(4):
            start = pl.multiple_of(meta[at[k], 2], 16)
            spread = unpacking((TOK, size), GRID, geo[k][2], geo[k][3])
            out[k] = mm(spread, outp[pl.ds(start, size), :]).astype(BF)

    most = functools.reduce(jnp.maximum, [g[2] * g[3] for g in geo])
    pl.when(most <= SMALL)(functools.partial(body, SMALL))
    pl.when(most > SMALL)(functools.partial(body, SLOT))


def attend_back_kernel(
    meta, hat, gain, shift, att_mine, att_other,
    qkvt_small, probs_small, qkvt_large, probs_large, gmix, gplain, gshort, small_dense,
    grads, gqs_kept, gqs_sent, small,
    wqkv_scr, wrow_scr, gm_scr, score_scr, gs_scr, gqkv_scr, wqkv_acc, table_acc, small_acc,
    shift_scr, att_scr, gain_scr, gmix_scr, gplain_scr, gqs_scr, sems, row_sems,
):
    n = pl.program_id(0)
    slot = n & 1

    def get_rows(pair, size):
        first = pl.multiple_of(meta[2 * pair, 2], 16)
        return [
            pltpu.make_async_copy(
                source.at[pl.ds(first, size)],
                dest.at[pair & 1, pl.ds(0, size)],
                row_sems.at[pair & 1, k],
            )
            for k, (source, dest) in enumerate(((gmix, gmix_scr), (gplain, gplain_scr)))
        ]

    def start_rows(pair):
        def start(size):
            for copy in get_rows(pair, size):
                copy.start()

        pl.when(pair < meta[4, 3])(lambda: start(2 * SMALL))
        pl.when(pair >= meta[4, 3])(lambda: start(2 * SLOT))

    pl.when(n == 0)(lambda: start_rows(n))
    pl.when(n + 1 < pl.num_programs(0))(lambda: start_rows(n + 1))
    geo = [geometry(meta, 2 * n), geometry(meta, 2 * n + 1)]
    starts = [pl.multiple_of(meta[2 * n + k, 2], 16) for k in range(2)]

    @pl.when(n == 0)
    def _():
        for copy in fetch_shards(meta, att_mine, att_other, att_scr, sems):
            copy.wait()
        unpack_qkv(att_scr, wqkv_scr)
        columns_of(gain, shift, gain_scr)
        wrow_scr[...] = wqkv_scr[...].T
        wqkv_acc[...] = jnp.zeros_like(wqkv_acc)
        table_acc[...] = jnp.zeros_like(table_acc)
        small_acc[...] = jnp.zeros_like(small_acc)

    def body(size, keys, psize, qkvt, probs):
        picks = [packing((psize, size), g[4], g[2], g[3]) for g in geo]
        second = pl.multiple_of(starts[1] - starts[0], 16)
        spans = [pl.ds(0, psize), pl.ds(second, psize)]
        for copy in get_rows(n, 2 * psize):
            copy.wait()
        for k in range(2):
            gm_scr[k, :, :size] = mm(gmix_scr[slot, spans[k], :], picks[k], TN).astype(BF)
        for k in range(2):
            for g in range(3):
                value = qkvt[k, 768 + 128 * g : 896 + 128 * g, :].T[:keys]
                grad_mix = spread_heads(gm_scr[k, 128 * g : 128 * g + 128, :size])
                score_scr[k, g, :keys, : 4 * size] = mm(value, grad_mix)
        for head in range(HEADS):
            at = size * (head % 4)
            for k in range(2):
                share = probs[k, head].astype(F32)
                grad_share = score_scr[k, head // 4, :keys, at : at + size]
                inner = jnp.sum(share * grad_share, axis=0, keepdims=True)
                grad_scores = share * (grad_share - inner)
                row = table_row(head, geo[k][4])
                for j in range(size // 128):
                    table_acc[j, pl.ds(row, keys), :] += grad_scores[:, 128 * j : 128 * j + 128]
                gs_scr[k, head, :keys, :size] = grad_scores.astype(BF)
        for head in range(HEADS):
            at = HEAD_DIM * head
            for k in range(2):
                low = gs_scr[k, head, :keys, :size]
                key = qkvt[k, 384 + at : 416 + at, :keys]
                query = qkvt[k, at : at + 32, :]
                left, right = size * k, size * k + keys
                gqkv_scr[at : at + 32, left : left + size] = (mm(key, low) * SCORE_SCALE).astype(BF)
                gqkv_scr[384 + at : 416 + at, left:right] = (
                    mm(query, low, NT) * SCORE_SCALE
                ).astype(BF)
                gqkv_scr[768 + at : 800 + at, left:right] = mm(
                    gm_scr[k, at : at + 32, :size], probs[k, head], NT
                ).astype(BF)
        if keys < size:
            for k in range(2):
                gqkv_scr[384:, size * k + keys : size * k + size] = jnp.zeros(
                    (768, size - keys), BF
                )
        lane_ok, pooled = pooled_pair(geo, size, hat, gain_scr)
        gqkv = gqkv_scr[:, : 2 * size]
        wqkv_acc[...] += mm(gqkv, pooled, NT)
        grad_pooled_both = mm(wrow_scr[...], gqkv)
        for k in range(2):
            high, wide = geo[k][:2]
            if size < LARGE:
                grads[k, :, size:] = jnp.zeros((2 * D_IN, LARGE - size), BF)
            grad_pooled = jnp.where(
                lane_ok[k], grad_pooled_both[:, size * k : size * k + size], 0.0
            )
            gain_terms = grad_pooled * hat[k, :, :size]
            for j in range(size // 128):
                small_acc[0] += gain_terms[:, 128 * j : 128 * j + 128]
                small_acc[1] += grad_pooled[:, 128 * j : 128 * j + 128]
            part = window_share((1, size), 1, high, wide, geo[k][4])
            grad_hat = grad_pooled * gain_scr[:, 0:1] * part
            grad_hat = grad_hat - jnp.mean(grad_hat, axis=0, keepdims=True)
            grads[k, 0:192, :size] = grad_hat.astype(BF)
            grads[k, 192:384, :size] = (
                mm(gplain_scr[slot, spans[k], :], picks[k], TN) * part
            ).astype(BF)

    pl.when(n < meta[4, 3])(
        functools.partial(body, SMALL, SMALL, SMALL, qkvt_small, probs_small)
    )
    pl.when(n >= meta[4, 3])(functools.partial(body, LARGE, SLOT, SLOT, qkvt_large, probs_large))

    @pl.when(n == pl.num_programs(0) - 1)
    def _():
        own, narrow = meta[1, 3], meta[2, 3]
        for j in range(PARTS):
            d = own ^ j
            late = d >> 2
            keeper = (d ^ (5 * late)) ^ narrow
            core = keeper & 1
            at = pl.multiple_of(192 * (keeper >> 1) + 96 * late, 32)
            rows_j = [wqkv_acc[144 * j + 48 * k : 144 * j + 48 * k + 48, :] for k in range(3)]
            gqs_scr[core, pl.ds(at, 48), 0:192] = rows_j[0].astype(BF)
            gqs_scr[core, pl.ds(at + 48, 48), 0:192] = rows_j[1].astype(BF)
            gqs_scr[core, pl.ds(at, 48), 192:384] = rows_j[2].astype(BF)
            gqs_scr[core, pl.ds(at + 48, 48), 192:384] = gshort[48 * j : 48 * j + 48, :]
        by_shift = jnp.zeros((192, 384), F32)
        for cell in range(GRID):
            pick = shift_map(cell, GRID, 256)
            terms = jnp.concatenate(
                [table_acc[k, pl.ds(cell, 192, stride=GRID), :] for k in range(2)], axis=1
            )
            by_shift += mm(terms.astype(BF), pick, NT)
        for cell in range(8):
            pick = shift_map(cell, 8, 128)
            terms = table_acc[0, pl.ds(HEADS * WIDE_ROWS + cell, 192, stride=8), :]
            by_shift += mm(terms.astype(BF), pick, NT)
        shift_scr[...] = jnp.zeros_like(shift_scr)
        for k in range(3):
            shift_scr[k, 0:192, :] = by_shift[:, 128 * k : 128 * k + 128]
        table = jnp.zeros((16, 768), F32)
        for r in range(GRID):
            rows_r = jnp.concatenate(
                [shift_scr[k, pl.ds(r, 16, stride=16), :] for k in range(6)], axis=1
            )
            table += pltpu.roll(rows_r, SIDE * (GRID - 1 - r), 1)
        small[0:8, :] = small_dense[...]
        small[8:16, :] = jnp.zeros((8, 384), F32)
        small[8:9, 0:192] = jnp.sum(small_acc[0].T, axis=0, keepdims=True)
        small[8:9, 192:384] = jnp.sum(small_acc[1].T, axis=0, keepdims=True)
        small[16:32, :] = table[:, 0:384]
        small[32:48, :] = table[:, 384:768]
        high, low = split_two(small[...])
        for core, dest in enumerate((gqs_kept, gqs_sent)):
            dest[0:384, :] = gqs_scr[core]
            dest[384:432, :] = high
            dest[432:480, :] = low


def front_back_kernel(first, chained, meta, img, grads_a, grads_b, *rest):
    out = rest[1] if chained else rest[0]
    n = pl.program_id(0) + first
    geo = [geometry(meta, meta[2 * n + k, 5]) for k in range(2)]

    def body(pixels, size):
        for k, grads in enumerate((grads_a, grads_b)):
            high, wide, rows, cols, stride = geo[k]
            shifted, scale = norm_stats(img[k, :, :pixels].astype(F32))
            normed = shifted * scale
            token = token_of_pixel((1, pixels), 1, high, wide, stride)
            spread = mm(grads[0, :, :size], onehot(iota((size, pixels), 0) == token))
            grad_hat = spread[:D_IN]
            along = jnp.mean(grad_hat * normed, axis=0, keepdims=True)
            full = scale * (grad_hat - normed * along) + spread[D_IN:]
            out[k, :, :pixels] = full.astype(BF)
            if pixels < PIX:
                out[k, :, pixels:] = jnp.zeros((D_IN, PIX - pixels), BF)

    short = (geo[0][0] <= 18) & (geo[1][0] <= 18)
    large = jnp.maximum(geo[0][4] * geo[0][2], geo[1][4] * geo[1][2]) > SMALL
    pl.when(short & jnp.logical_not(large))(functools.partial(body, 512, SMALL))
    pl.when(jnp.logical_not(short | large))(functools.partial(body, PIX, SMALL))
    pl.when(large)(functools.partial(body, PIX, LARGE))


def finish_kernel(
    place, mine, got, short_t, qkv_t, out_t, up_t, down,
    ln1_gain, ln1_shift, out_bias, ln2_gain, ln2_shift, up_bias, down_bias, table,
):
    both = mine[0:144, :] + got[0:144, :]
    qkv_t[0:96, :] = both[0:96, 0:192]
    qkv_t[96:144, :] = both[0:48, 192:384]
    short_t[...] = both[48:96, 192:384]
    small = both[96:144, :]
    for k, dest in enumerate((out_bias, ln2_gain, ln2_shift, down_bias)):
        dest[...] = small[k]
    up_bias[...] = jnp.concatenate([small[4 + k : 5 + k] for k in range(4)], axis=1).reshape(FF)
    ln1_gain[...] = small[8, 0:192]
    ln1_shift[...] = small[8, 192:384]
    table[:, 0:384] = small[16 : 16 + HEADS]
    table[:, 384:] = small[32 : 32 + HEADS, 0 : SIDE * SIDE - 384]

    def emit(first, second):
        up_t[...] = first[144:336, :]
        out_t[0:32, :] = first[336:368, :]
        down[...] = second[144:336, :]
        out_t[32:48, :] = second[336:352, :]

    core = place[1] & 1
    pl.when(core == 0)(functools.partial(emit, mine, got))
    pl.when(core == 1)(functools.partial(emit, got, mine))


def per_image(*tail):
    return pl.BlockSpec((1,) + tail, lambda n, *_: (n,) + (0,) * len(tail))


def pair(*tail):
    return pl.BlockSpec((2,) + tail, lambda n, *_: (n,) + (0,) * len(tail))


def pair_member(lane, k, *tail):
    return pl.BlockSpec((1,) + tail, lambda n, meta: (meta[2 * n + k, lane],) + (0,) * len(tail))


def small_pair(*tail):
    return pl.BlockSpec(
        (2,) + tail,
        lambda n, meta: (jnp.minimum(n, jnp.maximum(meta[4, 3] - 1, 0)),) + (0,) * len(tail),
    )


def large_pair(*tail):
    return pl.BlockSpec(
        (2,) + tail, lambda n, meta: (jnp.maximum(n - meta[4, 3], 0),) + (0,) * len(tail)
    )


def attention_pairs():
    return [
        small_pair(3 * D_OUT, SMALL),
        small_pair(HEADS, SMALL, SMALL),
        large_pair(3 * D_OUT, LARGE),
        large_pair(HEADS, SLOT, LARGE),
    ]


def whole(*shape):
    return pl.BlockSpec(shape, lambda n, *_: (0,) * len(shape))


def call(
    kernel, micros, grid, in_specs, out_specs, out_shape, scratch, name, *args, aliases=(), vmem=56
):
    return pl.pallas_call(
        kernel,
        grid_spec=pltpu.PrefetchScalarGridSpec(
            num_scalar_prefetch=1,
            grid=grid,
            in_specs=in_specs,
            out_specs=out_specs,
            scratch_shapes=scratch,
        ),
        out_shape=out_shape,
        input_output_aliases=dict(aliases),
        compiler_params=pltpu.CompilerParams(
            dimension_semantics=("arbitrary",), vmem_limit_bytes=vmem * 2**20
        ),
        name=name,
        cost_estimate=pl.CostEstimate(
            flops=micros * 10**9, bytes_accessed=micros * 10**6, transcendentals=0
        ),
    )(*args)


def shape_of(*dims, dtype=BF):
    return jax.ShapeDtypeStruct(dims, dtype)


def packed_rows(count):
    return (count * SLOT + CHUNK - 1) // CHUNK * CHUNK + CHUNK


TOKEN = jax.ShapeDtypeStruct((8, 128), F32)
ANY = pl.BlockSpec(memory_space=pl.ANY)
GATHERED = [ANY, ANY]


def device_prepare(place, token_mask, w_short, w_qkv, w_out, w_up, w_down):
    count = token_mask.shape[0]
    return call(
        prepare_kernel,
        3,
        (1,),
        [
            whole(count, PIX),
            whole(48, D_IN),
            whole(144, D_IN),
            whole(48, D_OUT),
            whole(192, D_OUT),
            whole(192, D_OUT),
        ],
        [whole(count, 128), whole(96, D_OUT), whole(432, D_OUT)],
        [shape_of(count, 128, dtype=jnp.int32), shape_of(96, D_OUT), shape_of(432, D_OUT)],
        [],
        "prepare",
        place,
        token_mask,
        w_short.T,
        w_qkv.T,
        w_out.T,
        w_up.T,
        w_down,
    )


def device_meta(place, token_mask):
    count = token_mask.shape[0]
    return call(
        meta_rows,
        2,
        (1,),
        [whole(count, PIX)],
        [whole(count, 128)],
        [shape_of(count, 128, dtype=jnp.int32)],
        [],
        "meta",
        place,
        token_mask,
    )[0]


def device_front(meta, images, cotangent):
    count = images.shape[0]
    packed = packed_rows(count)
    return call(
        front_kernel,
        15,
        (count // 2,),
        [pair_member(4, k, D_IN, PIX) for k in range(2)]
        + [pair_member(4, k, TOK, D_OUT) for k in range(2)],
        [pair(D_IN, LARGE), whole(packed, D_IN), whole(packed, D_OUT)],
        [
            shape_of(count, D_IN, LARGE, dtype=F32),
            shape_of(packed, D_IN),
            shape_of(packed, D_OUT),
        ],
        [],
        "front",
        meta,
        images,
        images,
        cotangent,
        cotangent,
        vmem=28,
    )


SMALL_OUTPUTS = [(D_IN,)] * 2 + [(D_OUT,)] * 3 + [(FF,), (D_OUT,), (HEADS, SIDE * SIDE)]


def device_finish(place, mine, got):
    return call(
        finish_kernel,
        2,
        (1,),
        [whole(368, D_OUT), whole(368, D_OUT)],
        [
            whole(48, D_IN),
            whole(144, D_IN),
            whole(48, D_OUT),
            whole(192, D_OUT),
            whole(192, D_OUT),
        ]
        + [whole(*dims) for dims in SMALL_OUTPUTS],
        [
            shape_of(48, D_IN, dtype=F32),
            shape_of(144, D_IN, dtype=F32),
            shape_of(48, D_OUT, dtype=F32),
            shape_of(192, D_OUT, dtype=F32),
            shape_of(192, D_OUT, dtype=F32),
        ]
        + [shape_of(*dims, dtype=F32) for dims in SMALL_OUTPUTS],
        [],
        "finish",
        place,
        mine,
        got,
        vmem=12,
    )


def device_tables(rel_table):
    return pl.pallas_call(
        tables_kernel,
        out_shape=shape_of(2, BIAS_ROWS, 128, dtype=F32),
        scratch_shapes=[pltpu.VMEM((3, 192, 128), F32), pltpu.VMEM((16, 768), F32)],
        compiler_params=pltpu.CompilerParams(vmem_limit_bytes=16 * 2**20),
        name="tables",
        cost_estimate=pl.CostEstimate(
            flops=8 * 10**9, bytes_accessed=8 * 10**6, transcendentals=0
        ),
    )(rel_table)


def device_attend(meta, hat, gain, shift, att, bias):
    count = hat.shape[0]
    packed = packed_rows(count)
    return call(
        attend_kernel,
        30,
        (count // 2,),
        [pair(D_IN, LARGE), whole(D_IN), whole(D_IN)]
        + GATHERED
        + [ANY],
        attention_pairs() + [ANY, whole(8, 128)],
        [
            shape_of(count, 3 * D_OUT, SMALL),
            shape_of(count, HEADS, SMALL, SMALL),
            shape_of(count, 3 * D_OUT, LARGE),
            shape_of(count, HEADS, SLOT, LARGE),
            shape_of(packed, D_OUT),
            TOKEN,
        ],
        [
            pltpu.VMEM((3 * D_OUT, D_IN), BF),
            pltpu.VMEM((2, D_OUT, LARGE), BF),
            pltpu.VMEM((2, 3, SLOT, 4 * LARGE), F32),
            pltpu.VMEM((PARTS, 96, 384), BF),
            pltpu.VMEM((D_IN, 8), F32),
            pltpu.VMEM((2, BIAS_ROWS, 128), F32),
            pltpu.VMEM((2, CHUNK, D_OUT), BF),
            pltpu.SemaphoreType.DMA((PARTS,)),
            pltpu.SemaphoreType.DMA((2,)),
            pltpu.SemaphoreType.DMA,
        ],
        "attend",
        meta,
        hat,
        gain,
        shift,
        *att,
        bias,
        vmem=36,
    )


def device_dense(meta, plain, cotp, mixed, att, ff, params, token):
    packed = plain.shape[0]
    rows_of = lambda width: pl.BlockSpec(
        (CHUNK, width), lambda n, meta: (jnp.minimum(n, meta[3, 3]), 0)
    )
    return call(
        dense_kernel,
        40,
        (packed // CHUNK,),
        [rows_of(D_IN), rows_of(D_OUT), rows_of(D_OUT)]
        + GATHERED
        + GATHERED
        + [whole(D_OUT)] * 4
        + [whole(FF), ANY],
        [
            rows_of(D_OUT),
            rows_of(D_OUT),
            rows_of(D_IN),
            whole(PARTS, 224, 384),
            whole(PARTS, 224, 384),
            whole(D_OUT, D_IN),
            whole(8, D_OUT),
        ],
        [
            shape_of(packed, D_OUT),
            shape_of(packed, D_OUT),
            shape_of(packed, D_IN),
            shape_of(PARTS, 224, 384),
            shape_of(PARTS, 224, 384),
            shape_of(D_OUT, D_IN),
            shape_of(8, D_OUT, dtype=F32),
        ],
        [
            pltpu.VMEM((D_OUT, D_IN), BF),
            pltpu.VMEM((D_OUT, D_OUT), BF),
            pltpu.VMEM((FF, D_OUT), BF),
            pltpu.VMEM((FF, D_OUT), BF),
            pltpu.VMEM((D_OUT, FF), F32),
            pltpu.VMEM((D_OUT, FF), F32),
            pltpu.VMEM((D_OUT, D_OUT), F32),
            pltpu.VMEM((D_OUT, D_IN), F32),
            pltpu.VMEM((32, D_OUT), F32),
            pltpu.VMEM((8, FF), F32),
            pltpu.VMEM((PARTS, 96, 384), BF),
            pltpu.SemaphoreType.DMA((PARTS,)),
            pltpu.SemaphoreType.DMA((3 * PARTS,)),
        ],
        "dense",
        meta,
        plain,
        cotp,
        mixed,
        *att,
        *ff,
        *params,
        token,
        vmem=40,
    )


def device_expand(meta, outp, count):
    return call(
        expand_kernel,
        5,
        (count // 4,),
        [whole(*outp.shape)],
        [pl.BlockSpec((4, TOK, D_OUT), lambda n, *_: (n, 0, 0))],
        [shape_of(count, TOK, D_OUT)],
        [],
        "expand",
        meta,
        outp,
        vmem=24,
    )[0]


def device_attend_back(meta, hat, gain, shift, att, kept, gmix, gplain, gshort, small):
    count = hat.shape[0]
    packed = gmix.shape[0]
    return call(
        attend_back_kernel,
        40,
        (count // 2,),
        [pair(D_IN, LARGE), whole(D_IN), whole(D_IN)]
        + GATHERED
        + attention_pairs()
        + [
            ANY,
            ANY,
            whole(D_OUT, D_IN),
            whole(8, 384),
        ],
        [pair(2 * D_IN, LARGE), whole(480, 384), whole(480, 384), whole(48, 384)],
        [
            shape_of(count, 2 * D_IN, LARGE),
            shape_of(480, 384),
            shape_of(480, 384),
            shape_of(48, 384, dtype=F32),
        ],
        [
            pltpu.VMEM((3 * D_OUT, D_IN), BF),
            pltpu.VMEM((D_IN, 3 * D_OUT), BF),
            pltpu.VMEM((2, D_OUT, LARGE), BF),
            pltpu.VMEM((2, 3, SLOT, 4 * LARGE), F32),
            pltpu.VMEM((2, HEADS, SLOT, LARGE), BF),
            pltpu.VMEM((3 * D_OUT, 2 * LARGE), BF),
            pltpu.VMEM((3 * D_OUT, D_IN), F32),
            pltpu.VMEM((2, BIAS_ROWS, 128), F32),
            pltpu.VMEM((2, D_IN, 128), F32),
            pltpu.VMEM((6, 256, 128), F32),
            pltpu.VMEM((PARTS, 96, 384), BF),
            pltpu.VMEM((D_IN, 8), F32),
            pltpu.VMEM((2, 2 * SLOT, D_OUT), BF),
            pltpu.VMEM((2, 2 * SLOT, D_IN), BF),
            pltpu.VMEM((2, 384, 384), BF),
            pltpu.SemaphoreType.DMA((PARTS,)),
            pltpu.SemaphoreType.DMA((2, 2)),
        ],
        "attend_back",
        meta,
        hat,
        gain,
        shift,
        *att,
        *kept,
        gmix,
        gplain,
        gshort,
        small,
        vmem=52,
    )


def device_front_back(meta, images, grads, first, count, before=None):
    some = lambda *tail: pl.BlockSpec(
        (2,) + tail, lambda n, *_: (n + first,) + (0,) * len(tail)
    )
    member = lambda k, *tail: pl.BlockSpec(
        (1,) + tail, lambda n, meta: (meta[2 * (n + first) + k, 5],) + (0,) * len(tail)
    )
    chained = before is not None
    return call(
        functools.partial(front_back_kernel, first, chained),
        1,
        (count,),
        [some(D_IN, PIX)]
        + [member(k, 2 * D_IN, LARGE) for k in range(2)]
        + ([ANY] if chained else []),
        [some(D_IN, PIX)],
        [shape_of(*images.shape)],
        [],
        "front_back",
        meta,
        images,
        grads,
        grads,
        *([before] if chained else []),
        aliases={4: 0} if chained else {},
        vmem=24,
    )[0]


def shard_grads(ff, qs):
    g_up, g_down = ff[0][:192].T, ff[1][:192]
    g_out = jnp.concatenate([ff[0][192:224], ff[1][192:208]], axis=0).T
    g_qkv = jnp.concatenate([qs[:, :192], qs[:48, 192:]], axis=0).T
    g_short = qs[48:, 192:].T
    return g_short, g_qkv, g_out, g_up, g_down


def tied(*values):
    return lax.optimization_barrier(values)


class FastLinks:
    def __init__(self):
        self.own = lax.axis_index("wide")
        self.narrow = lax.axis_index("narrow")

    def across(self, value, bit):
        return lax.ppermute(value, "narrow", [(i, i ^ bit) for i in range(4)])

    def along(self, value, bits):
        return lax.ppermute(value, "wide", [(i, i ^ bits) for i in range(PARTS)])

    def spread(self, value, bits):
        pairs = [
            (4 * w + k, 4 * (w ^ k ^ bits) + k) for w in range(PARTS) for k in range(4)
        ]
        return lax.ppermute(value, ("wide", "narrow"), pairs)

    def fetch_two(self, value):
        return jnp.stack([self.spread(value, 0), self.spread(value, 5)])


def rounded(value):
    return lax.reduce_precision(value, 8, 7)


def low_sum(left, right):
    return rounded(left.astype(F32) + right.astype(F32)).astype(BF)


def high_sum(left, right):
    return left.astype(F32) + right.astype(F32)


def two_rows(value):
    high = rounded(value)
    return jnp.concatenate([high, rounded(value - high)], axis=0).astype(BF)


def one_row(pair):
    half = pair.shape[0] // 2
    return high_sum(pair[:half], pair[half:])


def tree(parts):
    while len(parts) > 1:
        parts = [high_sum(parts[k], parts[k + 1]) for k in range(0, len(parts), 2)]
    return parts[0]


class PlainLinks:
    own = 0
    narrow = 0

    def gather_weights(self, w_short, w_qkv, w_out, w_up, w_down):
        full = [
            lax.all_gather(w.astype(BF), "wide", axis=axis, tiled=True)
            for w, axis in ((w_short, 1), (w_qkv, 1), (w_out, 1), (w_up, 1), (w_down, 0))
        ]

        def shard(j):
            short, qkv, out, up, down = (
                lax.slice_in_dim(w, j * size, (j + 1) * size, axis=axis)
                for w, size, axis in zip(full, (48, 144, 48, 192, 192), (1, 1, 1, 1, 0))
            )
            qs = jnp.concatenate([qkv.T, short.T], axis=0)
            qs = jnp.concatenate([qs[:96], qs[96:]], axis=1)
            return qs, jnp.concatenate([up.T, down, out.T], axis=0)

        parts = [shard(j) for j in (0, 5, 2, 7, 1, 4, 3, 6)]
        return tuple(
            (jnp.stack([p[k] for p in parts[:4]]), jnp.stack([p[k] for p in parts[4:]]))
            for k in range(2)
        )

    def reduce_grads(self, gff, gqs):
        order = [0, 5, 2, 7, 1, 4, 3, 6]
        gqs = jnp.concatenate([half[:384].reshape(4, 96, 384) for half in gqs])
        parts = [shard_grads([g[j] for g in gff], gqs[order.index(j)]) for j in range(PARTS)]
        out = []
        for k, axis in enumerate((1, 1, 1, 1, 0)):
            whole_grad = jnp.concatenate([p[k] for p in parts], axis=axis)
            shard = lax.psum_scatter(whole_grad, "wide", scatter_dimension=axis, tiled=True)
            out.append(lax.psum(shard, "narrow").astype(F32))
        return out


def outputs(output, grad_images, weights, small):
    table = jnp.concatenate([small[16 : 16 + HEADS], small[32 : 32 + HEADS]], axis=1)
    return (
        output,
        jnp.swapaxes(grad_images, 1, 2),
        *weights,
        small[8, :192],
        small[8, 192:],
        small[0],
        small[1],
        small[2],
        small[4:8].reshape(FF),
        small[3],
        table[:, : SIDE * SIDE],
    )


def shards_plain(
    images, token_mask, w_short, w_qkv, w_out, w_up, w_down, ln1_gain, ln1_shift, out_bias,
    ln2_gain, ln2_shift, up_bias, down_bias, rel_table, cotangent,
):
    links = PlainLinks()
    count = images.shape[0]
    images = jnp.swapaxes(images, 1, 2)
    ln1 = (ln1_gain, ln1_shift)
    params = (out_bias, ln2_gain, ln2_shift, down_bias, up_bias)
    meta = device_meta(jnp.zeros((2,), jnp.int32), token_mask)
    att, ff = links.gather_weights(w_short, w_qkv, w_out, w_up, w_down)
    hat, plain, cotp = device_front(meta, images, cotangent)
    bias = device_tables(rel_table)
    *kept, mixed, token = device_attend(meta, hat, *ln1, att, bias)
    outp, gmix, gplain, *gff, gshort, small = device_dense(
        meta, plain, cotp, mixed, att, ff, params, token
    )
    output = device_expand(meta, outp, count)
    grads, *gqs, small = device_attend_back(
        meta, hat, *ln1, att, kept, gmix, gplain, gshort, small
    )
    grad_images = device_front_back(meta, images, grads, 0, count // 2)
    small = lax.psum(small, ("wide", "narrow"))
    return outputs(output, grad_images, links.reduce_grads(gff, gqs), small)


def shards_fast(
    images, token_mask, w_short, w_qkv, w_out, w_up, w_down, ln1_gain, ln1_shift, out_bias,
    ln2_gain, ln2_shift, up_bias, down_bias, rel_table, cotangent,
):
    links = FastLinks()
    count = images.shape[0]
    images = jnp.swapaxes(images, 1, 2)
    ln1 = (ln1_gain, ln1_shift)
    params = (out_bias, ln2_gain, ln2_shift, down_bias, up_bias)
    place = jnp.stack([links.own, links.narrow]).astype(jnp.int32)
    meta, att, ff = device_prepare(place, token_mask, w_short, w_qkv, w_out, w_up, w_down)

    att, ff = links.fetch_two(att), links.fetch_two(ff)
    hat, plain, cotp = device_front(meta, images, cotangent)
    att, hat, rel_table = tied(att, hat, rel_table)
    att = jnp.concatenate([att, links.across(att, 2)])
    bias = device_tables(rel_table)
    att, bias, ff = tied(att, bias, ff)
    att = (att, links.across(att, 1))
    ff_more = links.across(ff, 2)
    *kept, mixed, token = device_attend(meta, hat, *ln1, att, bias)
    ff_more, token = tied(ff_more, token)
    ff = jnp.concatenate([ff, ff_more])
    ff_other = links.across(ff, 1)
    outp, gmix, gplain, gff_kept, gff_sent, gshort, small = device_dense(
        meta, plain, cotp, mixed, att, (ff, ff_other), params, token
    )

    got = links.across(gff_sent, 1)
    output = device_expand(meta, outp, count)
    got, output, gmix = tied(got, output, gmix)
    terms = [low_sum(gff_kept[d], got[d]) for d in range(PARTS)]
    far = (7, 6, 5, 4, 3)
    moved = {d: links.along(terms[d], d) for d in far}
    grads, gqs_kept, gqs_sent, small = device_attend_back(
        meta, hat, *ln1, att, kept, gmix, gplain, gshort, small
    )
    tie = tied(grads, gqs_kept, gqs_sent, *terms[1:3], *(moved[d] for d in far))
    grads, gqs_kept, gqs_sent = tie[:3]
    pairs = count // 2
    cuts = [k * pairs // 8 for k in (0, 2, 5, 7, 8)]
    done = None

    def beside(k, *got):
        piece = device_front_back(meta, images, grads, cuts[k], cuts[k + 1] - cuts[k], done)
        return tied(piece, *got)

    got = links.across(gqs_sent, 1)
    near = [links.along(tie[2 + d], d) for d in (1, 2)]
    done, got, *near = beside(0, got, *near)
    terms[1:] = [*near, *reversed(tie[5:])]
    held = low_sum(gqs_kept[:384], got[:384])
    small = one_row(gqs_kept[384:]) + one_row(got[384:])
    small = two_rows(small)
    sent, done = tied(jnp.concatenate([held[192:], small]), done)
    got = links.across(sent, 2)
    done, got, *terms = beside(1, got, *terms)
    held = low_sum(held[:192], got[:192])
    small = two_rows(one_row(small) + one_row(got[192:]))
    ff_sum = rounded(tree(terms)).astype(BF)
    *sent, ff_sum, done = tied(
        jnp.concatenate([held[:96], small]), jnp.concatenate([held[96:], small]), ff_sum, done
    )
    got = links.spread(sent[0], 0), links.spread(sent[1], 5)
    ff_got = links.across(ff_sum, 2)
    done, ff_got, *got = beside(2, ff_got, *got)
    held = low_sum(got[0][:96], got[1][:96])
    small = two_rows(one_row(got[0][96:]) + one_row(got[1][96:]))
    mine, done = tied(jnp.concatenate([held, small]), done)
    got = links.across(mine, 2)
    done, got, ff_sum, ff_got = beside(3, got, ff_sum, ff_got)
    mine = jnp.concatenate(
        [
            high_sum(mine[:96], got[:96]),
            one_row(mine[96:]) + one_row(got[96:]),
            high_sum(ff_sum, ff_got),
        ]
    )
    last = device_finish(place, mine, links.across(mine, 1))
    return (output, jnp.swapaxes(done, 1, 2), *(w.T for w in last[:4]), *last[4:])


def solution(mesh):
    data = ("wide", "narrow")
    rows = P(None, "wide")
    in_specs = (
        (P(data, None, None), P(data, None), rows, rows, rows, rows, P("wide", None))
        + (P(),) * 8
        + (P(data, None, None),)
    )
    out_specs = (
        (P(data, None, None), P(data, None, None), rows, rows, rows, rows, P("wide", None))
        + (P(),) * 8
    )
    fast = mesh.shape["wide"] == PARTS and mesh.shape["narrow"] == 4
    return jax.shard_map(
        shards_fast if fast else shards_plain,
        mesh=mesh,
        in_specs=in_specs,
        out_specs=out_specs,
        check_vma=False,
    )
```

```python
import functools
import math

import jax
import jax.numpy as jnp
from jax import lax
from jax.experimental import pallas as pl
from jax.experimental.pallas import tpu as pltpu
from jax.sharding import PartitionSpec as P

D_IN = 192
D_OUT = 384
HEADS = 12
HEAD_DIM = 32
FF = 1536
GRID = 14
SIDE = 2 * GRID - 1
TOK = GRID * GRID
PIX = 4 * TOK
EPS = 1e-05
LOG2E = math.log2(math.e)
SCORE_SCALE = HEAD_DIM ** (-0.5)

SLOT = 208
SMALL = 128
LARGE = 256
WIDE_ROWS = 16 * GRID
NARROW_ROWS = 16 * 8
BIAS_ROWS = HEADS * (WIDE_ROWS + NARROW_ROWS)
CHUNK = 480
WIDTH = 768
PARTS = 8
BF = jnp.bfloat16
F32 = jnp.float32
NN = (((1,), (0,)), ((), ()))
NT = (((1,), (1,)), ((), ()))
TN = (((0,), (0,)), ((), ()))


def mm(left, right, dims=NN):
    return lax.dot_general(left, right, dims, preferred_element_type=F32)


def iota(shape, dim):
    return lax.broadcasted_iota(jnp.int32, shape, dim)


def geometry(meta, n):
    high, wide = meta[n, 0], meta[n, 1]
    rows, cols = (high + 1) >> 1, (wide + 1) >> 1
    return high, wide, rows, cols, meta[n, 6]


def cell_of(index, stride):
    row = jnp.where(stride == 8, index >> 3, (index * 4682) >> 16)
    return row, index - stride * row


def packed_index(index, stride, rows, cols):
    row, col = cell_of(index, stride)
    return jnp.where((col < cols) & (row < rows), row * cols + col, -1)


def onehot(mask):
    return jnp.where(mask, 1.0, 0.0).astype(BF)


def packing(shape, stride, rows, cols):
    return onehot(iota(shape, 0) == packed_index(iota((1, shape[1]), 1), stride, rows, cols))


def unpacking(shape, stride, rows, cols):
    return onehot(iota(shape, 1) == packed_index(iota((shape[0], 1), 0), stride, rows, cols))


def split_two(values):
    high = values.astype(BF)
    return high, (values - high.astype(F32)).astype(BF)


def shift_map(cell, stride, lanes):
    spot = iota((1, lanes), 1)
    row, col = cell_of(spot, stride)
    pick = jnp.where((row < GRID) & (col < GRID), SIDE * row + col - cell + GRID - 1, -1)
    return onehot(iota((384, lanes), 0) == pick)


def token_of_pixel(shape, dim, high, wide, stride):
    spot = iota(shape, dim)
    row = (spot * 2341) >> 16
    col = spot - 28 * row
    return jnp.where((row < high) & (col < wide), (row >> 1) * stride + (col >> 1), -1)


def window_share(shape, dim, high, wide, stride):
    row, col = cell_of(iota(shape, dim), stride)
    return jnp.where(2 * row + 1 < high, 0.5, 1.0) * jnp.where(2 * col + 1 < wide, 0.5, 1.0)


def norm_stats(values, axis=0):
    center = jnp.mean(values, axis=axis, keepdims=True)
    shifted = values - center
    spread = jnp.mean(shifted * shifted, axis=axis, keepdims=True)
    return shifted, lax.rsqrt(spread + EPS)


def prepare_kernel(place, mask, short_t, qkv_t, out_t, up_t, down, meta, att, ff):
    att[0:96, 0:192] = qkv_t[0:96, :].astype(BF)
    att[0:48, 192:384] = qkv_t[96:144, :].astype(BF)
    att[48:96, 192:384] = short_t[...].astype(BF)
    ff[0:192, :] = up_t[...].astype(BF)
    ff[192:384, :] = down[...].astype(BF)
    ff[384:432, :] = out_t[...].astype(BF)
    meta_rows(place, mask, meta)


def meta_rows(place, mask, meta):
    count = mask.shape[0]
    ones = mask[...]
    spot = iota(ones.shape, 1)
    row = (spot * 2341) >> 16
    high = jnp.sum(jnp.where(spot == 28 * row, ones, 0).astype(F32), axis=1, keepdims=True)
    wide = jnp.sum(jnp.where(spot < 28, ones, 0).astype(F32), axis=1, keepdims=True)

    def along(column):
        return jnp.broadcast_to(column, (count, 128)).T[:count]

    def total(values):
        return jnp.sum(values, axis=1, keepdims=True)

    rows = (high.astype(jnp.int32) + 1) >> 1
    cols = (wide.astype(jnp.int32) + 1) >> 1
    image = iota((count, 1), 0)
    stride = jnp.where(cols <= 8, 8, GRID)
    key = (stride * rows * count + image).astype(F32)
    rank = total(jnp.where(along(key) < key, 1.0, 0.0))
    chosen = along(rank) == image.astype(F32)

    def sort(column):
        return total(jnp.where(chosen, along(column), 0.0))

    taken = sort(((((rows * cols) + 15) >> 4) << 4).astype(F32))
    small = total(jnp.where(along(key) < SMALL * count + count, 1.0, 0.0)).astype(jnp.int32)
    start = total(jnp.where(iota((count, count), 1) < image, along(taken), 0.0))
    packed = total(along(taken)).astype(jnp.int32)
    chunks = ((packed + CHUNK - 1) * 2185) >> 20
    extra = jnp.where(image == 0, packed, jnp.where(image == 3, chunks, small >> 1))
    extra = jnp.where(image == 1, place[0], jnp.where(image == 2, place[1], extra))
    lane = iota((count, 128), 1)
    result = jnp.zeros((count, 128), jnp.int32)
    stride = jnp.where(image < (small >> 1) * 2, sort(stride.astype(F32)), float(GRID))
    columns = (sort(high), sort(wide), start, extra, sort(image.astype(F32)), rank, stride)
    for k, column in enumerate(columns):
        result = jnp.where(lane == k, column.astype(jnp.int32), result)
    meta[...] = result


def front_kernel(meta, img_a, img_b, cot_a, cot_b, hat, plain, cotp):
    n = pl.program_id(0)
    geo = [geometry(meta, 2 * n), geometry(meta, 2 * n + 1)]
    starts = [pl.multiple_of(meta[2 * n + k, 2], 16) for k in range(2)]

    def body(pixels, size, psize):
        sums = []
        for k, img in enumerate((img_a, img_b)):
            high, wide, rows, cols, stride = geo[k]
            values = img[0, :, :pixels]
            shifted, scale = norm_stats(values.astype(F32))
            normed = (shifted * scale).astype(BF)
            token = token_of_pixel((pixels, 1), 0, high, wide, stride)
            pick = onehot(iota((pixels, size), 1) == token)
            share = window_share((1, size), 1, high, wide, stride)
            sums.append(mm(jnp.concatenate([normed, values], axis=0), pick) * share)
        packed = []
        for k, cot in enumerate((cot_a, cot_b)):
            high, wide, rows, cols, stride = geo[k]
            hat[k, :, :size] = sums[k][:D_IN]
            pick = packing((psize, size), stride, rows, cols)
            first = mm(pick, sums[k][D_IN:].astype(BF), NT).astype(BF)
            pick = packing((psize, TOK), GRID, rows, cols)
            packed.append((first, mm(pick, cot[0]).astype(BF)))
        for k in range(2):
            plain[pl.ds(starts[k], psize), :] = packed[k][0]
            cotp[pl.ds(starts[k], psize), :] = packed[k][1]

    short = (geo[0][0] <= 18) & (geo[1][0] <= 18)
    large = geo[1][4] * geo[1][2] > SMALL
    pl.when(short & jnp.logical_not(large))(functools.partial(body, 512, SMALL, SMALL))
    pl.when(jnp.logical_not(short | large))(functools.partial(body, PIX, SMALL, SMALL))
    pl.when(large)(functools.partial(body, PIX, LARGE, SLOT))

    @pl.when(n == pl.num_programs(0) - 1)
    def _():
        total = pl.multiple_of(meta[0, 3], 16)
        plain[pl.ds(total, CHUNK), :] = jnp.zeros((CHUNK, D_IN), BF)
        cotp[pl.ds(total, CHUNK), :] = jnp.zeros((CHUNK, D_OUT), BF)


def tables_kernel(tab, bias, shift_scr, table_scr):
    shift_scr[...] = jnp.zeros_like(shift_scr)
    table_scr[...] = jnp.zeros_like(table_scr)
    table_scr[:HEADS, : SIDE * SIDE] = tab[...] * LOG2E
    table = table_scr[...]
    for r in range(GRID):
        moved = pltpu.roll(table, (768 - SIDE * (GRID - 1 - r)) % 768, 1)
        for k in range(3):
            shift_scr[k, pl.ds(r, HEADS, stride=16), :] = moved[
                :HEADS, 128 * k : 128 * k + 128
            ]
    top, rest = split_two(jnp.concatenate([shift_scr[k] for k in range(3)], axis=1))
    for cell in range(GRID):
        pick = shift_map(cell, GRID, 256)
        spread = mm(top, pick) + mm(rest, pick)
        for k in range(2):
            bias[k, pl.ds(cell, 192, stride=GRID), :] = spread[:, 128 * k : 128 * k + 128]
    for cell in range(8):
        pick = shift_map(cell, 8, 128)
        bias[0, pl.ds(HEADS * WIDE_ROWS + cell, 192, stride=8), :] = mm(top, pick) + mm(
            rest, pick
        )


def shard_at(meta, e):
    step = (2 if e & 2 else 0) ^ (5 if e & 1 else 0) ^ (1 if e >= 4 else 0)
    return meta[1, 3] ^ meta[2, 3] ^ step


def fetch_shards(meta, mine, other, dest, sems):
    copies = []
    for e in range(PARTS):
        source = mine if e < 4 else other
        copies.append(
            pltpu.make_async_copy(source.at[e & 3], dest.at[shard_at(meta, e)], sems.at[e])
        )
    for copy in copies:
        copy.start()
    return copies


def unpack_qkv(att, qkv_scr):
    for j in range(PARTS):
        qkv_scr[144 * j : 144 * j + 96, :] = att[j, 0:96, 0:192]
        qkv_scr[144 * j + 96 : 144 * j + 144, :] = att[j, 0:48, 192:384]


def slot_valid(shape, dim, stride, rows, cols):
    row, col = cell_of(iota(shape, dim), stride)
    return (col < cols) & (row < rows)


def row_of(vector):
    return vector[...].reshape(1, vector.shape[0])


def columns_of(gain, shift, dest):
    rows = jnp.concatenate(
        [row_of(gain), row_of(shift), jnp.zeros((6, D_IN), F32)], axis=0
    )
    dest[...] = rows.T


def spread_heads(block, tail=None):
    size = block.shape[1]
    parts = []
    for j in range(4):
        rows = [block[32 * j : 32 * j + 32]]
        if j > 0:
            rows.insert(0, jnp.zeros((32 * j, size), BF))
        if j < 3:
            rows.append(jnp.zeros((96 - 32 * j, size), BF))
        if tail is not None:
            rows.append(tail)
        parts.append(jnp.concatenate(rows, axis=0))
    return jnp.concatenate(parts, axis=1)


def table_row(head, stride):
    row = jnp.where(stride == 8, HEADS * WIDE_ROWS + head * NARROW_ROWS, head * WIDE_ROWS)
    return pl.multiple_of(row, 8)


def pooled_pair(geo, size, hat, gain_scr):
    lane_ok = [slot_valid((1, size), 1, g[4], g[2], g[3]) for g in geo]
    pooled = [
        jnp.where(lane_ok[k], hat[k, :, :size] * gain_scr[:, 0:1] + gain_scr[:, 1:2], 0.0)
        for k in range(2)
    ]
    return lane_ok, jnp.concatenate(pooled, axis=1).astype(BF)


def attend_kernel(
    meta, hat, gain, shift, att_mine, att_other, bias,
    qkvt_small, probs_small, qkvt_large, probs_large, mixed, token,
    wqkv_scr, mix_scr, score_scr, att_scr, gain_scr, bias_scr, rows_scr, sems, bias_sems, rows_sem,
):
    n = pl.program_id(0)
    token[...] = jnp.zeros_like(token)
    fetch_bias = [
        pltpu.make_async_copy(bias.at[0], bias_scr.at[0], bias_sems.at[0]),
        pltpu.make_async_copy(
            bias.at[1, pl.ds(0, HEADS * WIDE_ROWS)],
            bias_scr.at[1, pl.ds(0, HEADS * WIDE_ROWS)],
            bias_sems.at[1],
        ),
    ]

    def put_rows(pair, size):
        first = pl.multiple_of(meta[2 * pair, 2], 16)
        return pltpu.make_async_copy(
            rows_scr.at[pair & 1, pl.ds(0, size)], mixed.at[pl.ds(first, size)], rows_sem
        )

    def wait_rows(pair):
        pl.when(pair < meta[4, 3])(lambda: put_rows(pair, 2 * SMALL).wait())
        pl.when(pair >= meta[4, 3])(lambda: put_rows(pair, 2 * SLOT).wait())

    geo = [geometry(meta, 2 * n), geometry(meta, 2 * n + 1)]
    starts = [pl.multiple_of(meta[2 * n + k, 2], 16) for k in range(2)]

    @pl.when(n == 0)
    def _():
        for copy in fetch_bias:
            copy.start()
        copies = fetch_shards(meta, att_mine, att_other, att_scr, sems)
        columns_of(gain, shift, gain_scr)
        for copy in copies:
            copy.wait()
        unpack_qkv(att_scr, wqkv_scr)
        for copy in fetch_bias:
            copy.wait()

    def body(size, keys, psize, qkvt, probs):
        lane_ok, pooled = pooled_pair(geo, size, hat, gain_scr)
        qkv = mm(wqkv_scr[...], pooled).astype(BF)
        first_row = iota((16, size), 0) == 0
        ones = onehot(first_row)
        for k in range(2):
            qkvt[k] = qkv[:, size * k : size * k + size]
        for k in range(2):
            closed = jnp.where(first_row & ~lane_ok[k], -1e30, 0.0).astype(BF)
            for g in range(3):
                key = jnp.concatenate([qkvt[k, 384 + 128 * g : 512 + 128 * g, :], closed], axis=0)
                query = spread_heads(qkvt[k, 128 * g : 128 * g + 128, :], ones)
                score_scr[k, g, :keys, : 4 * size] = mm(key.T[:keys], query)
        for head in range(HEADS):
            at = size * (head % 4)
            for k in range(2):
                scores = score_scr[k, head // 4, :keys, at : at + size] * (SCORE_SCALE * LOG2E)
                if size == SMALL:
                    scores += bias_scr[0, pl.ds(table_row(head, geo[k][4]), keys), :]
                else:
                    scores += jnp.concatenate(
                        [
                            bias_scr[j, pl.ds(table_row(head, geo[k][4]), keys), :]
                            for j in range(2)
                        ],
                        axis=1,
                    )
                expo = jnp.exp2(scores - jnp.max(scores, axis=0, keepdims=True))
                share = expo * (1.0 / jnp.sum(expo, axis=0, keepdims=True))
                probs[k, head] = share.astype(BF)
        for head in range(HEADS):
            at = HEAD_DIM * head
            for k in range(2):
                value = qkvt[k, 768 + at : 800 + at, :keys]
                mix_scr[k, at : at + 32, :size] = mm(value, probs[k, head]).astype(BF)
        packed = []
        for k in range(2):
            pick = packing((psize, size), geo[k][4], geo[k][2], geo[k][3])
            packed.append(mm(pick, mix_scr[k, :, :size], NT).astype(BF))
        slot = n & 1
        rows_scr[slot, 0:psize, :] = packed[0]
        second = pl.multiple_of(starts[1] - starts[0], 16)
        rows_scr[slot, pl.ds(second, psize), :] = packed[1]
        pl.when(n > 0)(lambda: wait_rows(n - 1))
        put_rows(n, 2 * psize).start()

    pl.when(n < meta[4, 3])(
        functools.partial(body, SMALL, SMALL, SMALL, qkvt_small, probs_small)
    )
    pl.when(n >= meta[4, 3])(functools.partial(body, LARGE, SLOT, SLOT, qkvt_large, probs_large))

    @pl.when(n == pl.num_programs(0) - 1)
    def _():
        wait_rows(n)
        total = pl.multiple_of(meta[0, 3], 16)
        rows_scr[0, 0:CHUNK, :] = jnp.zeros((CHUNK, D_OUT), BF)
        blank = pltpu.make_async_copy(
            rows_scr.at[0, pl.ds(0, CHUNK)], mixed.at[pl.ds(total, CHUNK)], rows_sem
        )
        blank.start()
        blank.wait()


def gelu_both(x):
    bell = jnp.exp2((x * x) * (-0.5 * LOG2E))
    half = 0.5 + 0.5 * lax.erf(x * math.sqrt(0.5))
    return x * half, half + (x * bell) * (1.0 / math.sqrt(2.0 * math.pi))


def dense_kernel(
    meta, plain, cotp, mixed, att_mine, att_other, ff_a, ff_b, ff_c, ff_d,
    outbias, gain, shift, downbias, upbias, token,
    outp, gmix, gplain, gff_kept, gff_sent, gshort, small,
    wshort_scr, wout_scr, wup_scr, wdown_scr, up_acc, down_acc, out_acc, short_acc, small_acc,
    up_small, att_scr, att_sems, ff_sems,
):
    i = pl.program_id(0)

    @pl.when(i == 0)
    def _():
        ff_copies = []
        for e in range(PARTS):
            source = (ff_a, ff_b, ff_c, ff_d)[e >> 1].at[e & 1]
            shard = shard_at(meta, e)
            for k, (dest, low, size) in enumerate(
                ((wup_scr, 0, 192), (wdown_scr, 192, 192), (wout_scr, 384, 48))
            ):
                ff_copies.append(
                    pltpu.make_async_copy(
                        source.at[pl.ds(low, size)],
                        dest.at[pl.ds(pl.multiple_of(shard * size, 16), size)],
                        ff_sems.at[3 * e + k],
                    )
                )
        for copy in ff_copies:
            copy.start()
        for copy in fetch_shards(meta, att_mine, att_other, att_scr, att_sems):
            copy.wait()
        for j in range(PARTS):
            wshort_scr[48 * j : 48 * j + 48, :] = att_scr[j, 48:96, 192:384]
        up_acc[...] = jnp.zeros_like(up_acc)
        down_acc[...] = jnp.zeros_like(down_acc)
        out_acc[...] = jnp.zeros_like(out_acc)
        short_acc[...] = jnp.zeros_like(short_acc)
        small_acc[...] = jnp.zeros_like(small_acc)
        up_small[...] = jnp.zeros_like(up_small)
        for copy in ff_copies:
            copy.wait()

    @pl.when(i < meta[3, 3])
    def _():
        out_bias, ln_gain, ln_shift, down_bias = map(row_of, (outbias, gain, shift, downbias))
        up_bias = row_of(upbias)
        wout = wout_scr[...]
        wshort = wshort_scr[...]
        first = mm(plain[...], wshort, NT) + mm(mixed[...], wout, NT) + out_bias
        shifted, scale = norm_stats(first, -1)
        hat = shifted * scale
        normed = (hat * ln_gain + ln_shift).astype(BF)
        normed_t = normed.T
        cot = cotp[...]
        cot_t = cot.T
        branch = jnp.zeros((CHUNK, D_OUT), F32)
        grad_normed = jnp.zeros((CHUNK, D_OUT), F32)
        one_rows = jnp.ones((8, CHUNK), BF)
        for j in range(FF // WIDTH):
            some = slice(WIDTH * j, WIDTH * j + WIDTH)
            hidden = mm(normed, wup_scr[some, :], NT) + up_bias[:, some]
            grad_act = mm(cot, wdown_scr[some, :], NT)
            act, slope = gelu_both(hidden)
            act = act.astype(BF)
            grad_hidden = (grad_act * slope).astype(BF)
            branch += mm(act, wdown_scr[some, :])
            grad_normed += mm(grad_hidden, wup_scr[some, :])
            up_acc[:, some] += mm(normed_t, grad_hidden)
            down_acc[:, some] += mm(cot_t, act)
            up_small[:, some] += mm(one_rows, grad_hidden)
        outp[...] = (first + branch + down_bias).astype(BF)
        grad_branch = cot.astype(F32)
        grad_hat = grad_normed * ln_gain
        center = jnp.mean(grad_hat, axis=-1, keepdims=True)
        along = jnp.mean(grad_hat * hat, axis=-1, keepdims=True)
        grad_first = grad_branch + scale * (grad_hat - center - hat * along)
        low = grad_first.astype(BF)
        low_t = low.T
        gmix[...] = mm(low, wout).astype(BF)
        gplain[...] = mm(low, wshort).astype(BF)
        out_acc[...] += mm(low_t, mixed[...])
        short_acc[...] += mm(low_t, plain[...])

        def fold(values):
            return jnp.sum(values.reshape(CHUNK // 8, 8, D_OUT), axis=0)

        small_acc[0:8, :] += fold(grad_first)
        small_acc[8:16, :] += fold(grad_normed * hat)
        small_acc[16:24, :] += fold(grad_normed)
        small_acc[24:32, :] += fold(grad_branch)

    @pl.when(i == meta[3, 3])
    def _():
        for ref in (outp, gmix, gplain):
            ref[...] = jnp.zeros_like(ref)

    @pl.when(i == meta[3, 3] - 1)
    def _():
        own, core = meta[1, 3], meta[2, 3] & 1

        def emit(kept, sent):
            for j in range(PARTS):
                at = own ^ j
                kept[at, 0:192, :] = up_acc[:, 192 * j : 192 * j + 192].astype(BF).T
                sent[at, 0:192, :] = down_acc[:, 192 * j : 192 * j + 192].astype(BF).T
                out_rows = out_acc[48 * j : 48 * j + 48, :].astype(BF)
                kept[at, 192:224, :] = out_rows[0:32]
                sent[at, 192:208, :] = out_rows[32:48]
                sent[at, 208:224, :] = jnp.zeros((16, D_OUT), BF)

        pl.when(core == 0)(functools.partial(emit, gff_kept, gff_sent))
        pl.when(core == 1)(functools.partial(emit, gff_sent, gff_kept))
        gshort[...] = short_acc[...].astype(BF)
        for k in range(4):
            total = small_acc[8 * k : 8 * k + 8, :]
            small[k : k + 1, :] = jnp.sum(total, axis=0, keepdims=True)
            small[4 + k : 5 + k, :] = up_small[0:1, 384 * k : 384 * k + 384]


def expand_kernel(meta, outp, out):
    n = pl.program_id(0)
    at = [meta[4 * n + k, 5] for k in range(4)]
    geo = [geometry(meta, p) for p in at]

    def body(size):
        for k in range(4):
            start = pl.multiple_of(meta[at[k], 2], 16)
            spread = unpacking((TOK, size), GRID, geo[k][2], geo[k][3])
            out[k] = mm(spread, outp[pl.ds(start, size), :]).astype(BF)

    most = functools.reduce(jnp.maximum, [g[2] * g[3] for g in geo])
    pl.when(most <= SMALL)(functools.partial(body, SMALL))
    pl.when(most > SMALL)(functools.partial(body, SLOT))


def attend_back_kernel(
    meta, hat, gain, shift, att_mine, att_other,
    qkvt_small, probs_small, qkvt_large, probs_large, gmix, gplain, gshort, small_dense,
    grads, gqs_kept, gqs_sent, small,
    wqkv_scr, wrow_scr, gm_scr, score_scr, gs_scr, gqkv_scr, wqkv_acc, table_acc, small_acc,
    shift_scr, att_scr, gain_scr, gmix_scr, gplain_scr, gqs_scr, sems, row_sems,
):
    n = pl.program_id(0)
    slot = n & 1

    def get_rows(pair, size):
        first = pl.multiple_of(meta[2 * pair, 2], 16)
        return [
            pltpu.make_async_copy(
                source.at[pl.ds(first, size)],
                dest.at[pair & 1, pl.ds(0, size)],
                row_sems.at[pair & 1, k],
            )
            for k, (source, dest) in enumerate(((gmix, gmix_scr), (gplain, gplain_scr)))
        ]

    def start_rows(pair):
        def start(size):
            for copy in get_rows(pair, size):
                copy.start()

        pl.when(pair < meta[4, 3])(lambda: start(2 * SMALL))
        pl.when(pair >= meta[4, 3])(lambda: start(2 * SLOT))

    pl.when(n == 0)(lambda: start_rows(n))
    pl.when(n + 1 < pl.num_programs(0))(lambda: start_rows(n + 1))
    geo = [geometry(meta, 2 * n), geometry(meta, 2 * n + 1)]
    starts = [pl.multiple_of(meta[2 * n + k, 2], 16) for k in range(2)]

    @pl.when(n == 0)
    def _():
        for copy in fetch_shards(meta, att_mine, att_other, att_scr, sems):
            copy.wait()
        unpack_qkv(att_scr, wqkv_scr)
        columns_of(gain, shift, gain_scr)
        wrow_scr[...] = wqkv_scr[...].T
        wqkv_acc[...] = jnp.zeros_like(wqkv_acc)
        table_acc[...] = jnp.zeros_like(table_acc)
        small_acc[...] = jnp.zeros_like(small_acc)

    def body(size, keys, psize, qkvt, probs):
        picks = [packing((psize, size), g[4], g[2], g[3]) for g in geo]
        second = pl.multiple_of(starts[1] - starts[0], 16)
        spans = [pl.ds(0, psize), pl.ds(second, psize)]
        for copy in get_rows(n, 2 * psize):
            copy.wait()
        for k in range(2):
            gm_scr[k, :, :size] = mm(gmix_scr[slot, spans[k], :], picks[k], TN).astype(BF)
        for k in range(2):
            for g in range(3):
                value = qkvt[k, 768 + 128 * g : 896 + 128 * g, :].T[:keys]
                grad_mix = spread_heads(gm_scr[k, 128 * g : 128 * g + 128, :size])
                score_scr[k, g, :keys, : 4 * size] = mm(value, grad_mix)
        for head in range(HEADS):
            at = size * (head % 4)
            for k in range(2):
                share = probs[k, head].astype(F32)
                grad_share = score_scr[k, head // 4, :keys, at : at + size]
                inner = jnp.sum(share * grad_share, axis=0, keepdims=True)
                grad_scores = share * (grad_share - inner)
                row = table_row(head, geo[k][4])
                for j in range(size // 128):
                    table_acc[j, pl.ds(row, keys), :] += grad_scores[:, 128 * j : 128 * j + 128]
                gs_scr[k, head, :keys, :size] = grad_scores.astype(BF)
        for head in range(HEADS):
            at = HEAD_DIM * head
            for k in range(2):
                low = gs_scr[k, head, :keys, :size]
                key = qkvt[k, 384 + at : 416 + at, :keys]
                query = qkvt[k, at : at + 32, :]
                left, right = size * k, size * k + keys
                gqkv_scr[at : at + 32, left : left + size] = (mm(key, low) * SCORE_SCALE).astype(BF)
                gqkv_scr[384 + at : 416 + at, left:right] = (
                    mm(query, low, NT) * SCORE_SCALE
                ).astype(BF)
                gqkv_scr[768 + at : 800 + at, left:right] = mm(
                    gm_scr[k, at : at + 32, :size], probs[k, head], NT
                ).astype(BF)
        if keys < size:
            for k in range(2):
                gqkv_scr[384:, size * k + keys : size * k + size] = jnp.zeros(
                    (768, size - keys), BF
                )
        lane_ok, pooled = pooled_pair(geo, size, hat, gain_scr)
        gqkv = gqkv_scr[:, : 2 * size]
        wqkv_acc[...] += mm(gqkv, pooled, NT)
        grad_pooled_both = mm(wrow_scr[...], gqkv)
        for k in range(2):
            high, wide = geo[k][:2]
            if size < LARGE:
                grads[k, :, size:] = jnp.zeros((2 * D_IN, LARGE - size), BF)
            grad_pooled = jnp.where(
                lane_ok[k], grad_pooled_both[:, size * k : size * k + size], 0.0
            )
            gain_terms = grad_pooled * hat[k, :, :size]
            for j in range(size // 128):
                small_acc[0] += gain_terms[:, 128 * j : 128 * j + 128]
                small_acc[1] += grad_pooled[:, 128 * j : 128 * j + 128]
            part = window_share((1, size), 1, high, wide, geo[k][4])
            grad_hat = grad_pooled * gain_scr[:, 0:1] * part
            grad_hat = grad_hat - jnp.mean(grad_hat, axis=0, keepdims=True)
            grads[k, 0:192, :size] = grad_hat.astype(BF)
            grads[k, 192:384, :size] = (
                mm(gplain_scr[slot, spans[k], :], picks[k], TN) * part
            ).astype(BF)

    pl.when(n < meta[4, 3])(
        functools.partial(body, SMALL, SMALL, SMALL, qkvt_small, probs_small)
    )
    pl.when(n >= meta[4, 3])(functools.partial(body, LARGE, SLOT, SLOT, qkvt_large, probs_large))

    @pl.when(n == pl.num_programs(0) - 1)
    def _():
        own, narrow = meta[1, 3], meta[2, 3]
        for j in range(PARTS):
            d = own ^ j
            late = d >> 2
            keeper = (d ^ (5 * late)) ^ narrow
            core = keeper & 1
            at = pl.multiple_of(192 * (keeper >> 1) + 96 * late, 32)
            rows_j = [wqkv_acc[144 * j + 48 * k : 144 * j + 48 * k + 48, :] for k in range(3)]
            gqs_scr[core, pl.ds(at, 48), 0:192] = rows_j[0].astype(BF)
            gqs_scr[core, pl.ds(at + 48, 48), 0:192] = rows_j[1].astype(BF)
            gqs_scr[core, pl.ds(at, 48), 192:384] = rows_j[2].astype(BF)
            gqs_scr[core, pl.ds(at + 48, 48), 192:384] = gshort[48 * j : 48 * j + 48, :]
        by_shift = jnp.zeros((192, 384), F32)
        for cell in range(GRID):
            pick = shift_map(cell, GRID, 256)
            terms = jnp.concatenate(
                [table_acc[k, pl.ds(cell, 192, stride=GRID), :] for k in range(2)], axis=1
            )
            by_shift += mm(terms.astype(BF), pick, NT)
        for cell in range(8):
            pick = shift_map(cell, 8, 128)
            terms = table_acc[0, pl.ds(HEADS * WIDE_ROWS + cell, 192, stride=8), :]
            by_shift += mm(terms.astype(BF), pick, NT)
        shift_scr[...] = jnp.zeros_like(shift_scr)
        for k in range(3):
            shift_scr[k, 0:192, :] = by_shift[:, 128 * k : 128 * k + 128]
        table = jnp.zeros((16, 768), F32)
        for r in range(GRID):
            rows_r = jnp.concatenate(
                [shift_scr[k, pl.ds(r, 16, stride=16), :] for k in range(6)], axis=1
            )
            table += pltpu.roll(rows_r, SIDE * (GRID - 1 - r), 1)
        small[0:8, :] = small_dense[...]
        small[8:16, :] = jnp.zeros((8, 384), F32)
        small[8:9, 0:192] = jnp.sum(small_acc[0].T, axis=0, keepdims=True)
        small[8:9, 192:384] = jnp.sum(small_acc[1].T, axis=0, keepdims=True)
        small[16:32, :] = table[:, 0:384]
        small[32:48, :] = table[:, 384:768]
        high, low = split_two(small[...])
        for core, dest in enumerate((gqs_kept, gqs_sent)):
            dest[0:384, :] = gqs_scr[core]
            dest[384:432, :] = high
            dest[432:480, :] = low


def front_back_kernel(first, chained, meta, img, grads_a, grads_b, *rest):
    out = rest[1] if chained else rest[0]
    n = pl.program_id(0) + first
    geo = [geometry(meta, meta[2 * n + k, 5]) for k in range(2)]

    def body(pixels, size):
        for k, grads in enumerate((grads_a, grads_b)):
            high, wide, rows, cols, stride = geo[k]
            shifted, scale = norm_stats(img[k, :, :pixels].astype(F32))
            normed = shifted * scale
            token = token_of_pixel((1, pixels), 1, high, wide, stride)
            spread = mm(grads[0, :, :size], onehot(iota((size, pixels), 0) == token))
            grad_hat = spread[:D_IN]
            along = jnp.mean(grad_hat * normed, axis=0, keepdims=True)
            full = scale * (grad_hat - normed * along) + spread[D_IN:]
            out[k, :, :pixels] = full.astype(BF)
            if pixels < PIX:
                out[k, :, pixels:] = jnp.zeros((D_IN, PIX - pixels), BF)

    short = (geo[0][0] <= 18) & (geo[1][0] <= 18)
    large = jnp.maximum(geo[0][4] * geo[0][2], geo[1][4] * geo[1][2]) > SMALL
    pl.when(short & jnp.logical_not(large))(functools.partial(body, 512, SMALL))
    pl.when(jnp.logical_not(short | large))(functools.partial(body, PIX, SMALL))
    pl.when(large)(functools.partial(body, PIX, LARGE))


def finish_kernel(
    place, mine, got, short_t, qkv_t, out_t, up_t, down,
    ln1_gain, ln1_shift, out_bias, ln2_gain, ln2_shift, up_bias, down_bias, table,
):
    both = mine[0:144, :] + got[0:144, :]
    qkv_t[0:96, :] = both[0:96, 0:192]
    qkv_t[96:144, :] = both[0:48, 192:384]
    short_t[...] = both[48:96, 192:384]
    small = both[96:144, :]
    for k, dest in enumerate((out_bias, ln2_gain, ln2_shift, down_bias)):
        dest[...] = small[k]
    up_bias[...] = jnp.concatenate([small[4 + k : 5 + k] for k in range(4)], axis=1).reshape(FF)
    ln1_gain[...] = small[8, 0:192]
    ln1_shift[...] = small[8, 192:384]
    table[:, 0:384] = small[16 : 16 + HEADS]
    table[:, 384:] = small[32 : 32 + HEADS, 0 : SIDE * SIDE - 384]

    def emit(first, second):
        up_t[...] = first[144:336, :]
        out_t[0:32, :] = first[336:368, :]
        down[...] = second[144:336, :]
        out_t[32:48, :] = second[336:352, :]

    core = place[1] & 1
    pl.when(core == 0)(functools.partial(emit, mine, got))
    pl.when(core == 1)(functools.partial(emit, got, mine))


def per_image(*tail):
    return pl.BlockSpec((1,) + tail, lambda n, *_: (n,) + (0,) * len(tail))


def pair(*tail):
    return pl.BlockSpec((2,) + tail, lambda n, *_: (n,) + (0,) * len(tail))


def pair_member(lane, k, *tail):
    return pl.BlockSpec((1,) + tail, lambda n, meta: (meta[2 * n + k, lane],) + (0,) * len(tail))


def small_pair(*tail):
    return pl.BlockSpec(
        (2,) + tail,
        lambda n, meta: (jnp.minimum(n, jnp.maximum(meta[4, 3] - 1, 0)),) + (0,) * len(tail),
    )


def large_pair(*tail):
    return pl.BlockSpec(
        (2,) + tail, lambda n, meta: (jnp.maximum(n - meta[4, 3], 0),) + (0,) * len(tail)
    )


def attention_pairs():
    return [
        small_pair(3 * D_OUT, SMALL),
        small_pair(HEADS, SMALL, SMALL),
        large_pair(3 * D_OUT, LARGE),
        large_pair(HEADS, SLOT, LARGE),
    ]


def whole(*shape):
    return pl.BlockSpec(shape, lambda n, *_: (0,) * len(shape))


def call(
    kernel, micros, grid, in_specs, out_specs, out_shape, scratch, name, *args, aliases=(), vmem=56
):
    return pl.pallas_call(
        kernel,
        grid_spec=pltpu.PrefetchScalarGridSpec(
            num_scalar_prefetch=1,
            grid=grid,
            in_specs=in_specs,
            out_specs=out_specs,
            scratch_shapes=scratch,
        ),
        out_shape=out_shape,
        input_output_aliases=dict(aliases),
        compiler_params=pltpu.CompilerParams(
            dimension_semantics=("arbitrary",), vmem_limit_bytes=vmem * 2**20
        ),
        name=name,
        cost_estimate=pl.CostEstimate(
            flops=micros * 10**9, bytes_accessed=micros * 10**6, transcendentals=0
        ),
    )(*args)


def shape_of(*dims, dtype=BF):
    return jax.ShapeDtypeStruct(dims, dtype)


def packed_rows(count):
    return (count * SLOT + CHUNK - 1) // CHUNK * CHUNK + CHUNK


TOKEN = jax.ShapeDtypeStruct((8, 128), F32)
ANY = pl.BlockSpec(memory_space=pl.ANY)
GATHERED = [ANY, ANY]


def device_prepare(place, token_mask, w_short, w_qkv, w_out, w_up, w_down):
    count = token_mask.shape[0]
    return call(
        prepare_kernel,
        3,
        (1,),
        [
            whole(count, PIX),
            whole(48, D_IN),
            whole(144, D_IN),
            whole(48, D_OUT),
            whole(192, D_OUT),
            whole(192, D_OUT),
        ],
        [whole(count, 128), whole(96, D_OUT), whole(432, D_OUT)],
        [shape_of(count, 128, dtype=jnp.int32), shape_of(96, D_OUT), shape_of(432, D_OUT)],
        [],
        "prepare",
        place,
        token_mask,
        w_short.T,
        w_qkv.T,
        w_out.T,
        w_up.T,
        w_down,
    )


def device_meta(place, token_mask):
    count = token_mask.shape[0]
    return call(
        meta_rows,
        2,
        (1,),
        [whole(count, PIX)],
        [whole(count, 128)],
        [shape_of(count, 128, dtype=jnp.int32)],
        [],
        "meta",
        place,
        token_mask,
    )[0]


def device_front(meta, images, cotangent):
    count = images.shape[0]
    packed = packed_rows(count)
    return call(
        front_kernel,
        15,
        (count // 2,),
        [pair_member(4, k, D_IN, PIX) for k in range(2)]
        + [pair_member(4, k, TOK, D_OUT) for k in range(2)],
        [pair(D_IN, LARGE), whole(packed, D_IN), whole(packed, D_OUT)],
        [
            shape_of(count, D_IN, LARGE, dtype=F32),
            shape_of(packed, D_IN),
            shape_of(packed, D_OUT),
        ],
        [],
        "front",
        meta,
        images,
        images,
        cotangent,
        cotangent,
        vmem=28,
    )


SMALL_OUTPUTS = [(D_IN,)] * 2 + [(D_OUT,)] * 3 + [(FF,), (D_OUT,), (HEADS, SIDE * SIDE)]


def device_finish(place, mine, got):
    return call(
        finish_kernel,
        2,
        (1,),
        [whole(368, D_OUT), whole(368, D_OUT)],
        [
            whole(48, D_IN),
            whole(144, D_IN),
            whole(48, D_OUT),
            whole(192, D_OUT),
            whole(192, D_OUT),
        ]
        + [whole(*dims) for dims in SMALL_OUTPUTS],
        [
            shape_of(48, D_IN, dtype=F32),
            shape_of(144, D_IN, dtype=F32),
            shape_of(48, D_OUT, dtype=F32),
            shape_of(192, D_OUT, dtype=F32),
            shape_of(192, D_OUT, dtype=F32),
        ]
        + [shape_of(*dims, dtype=F32) for dims in SMALL_OUTPUTS],
        [],
        "finish",
        place,
        mine,
        got,
        vmem=12,
    )


def device_tables(rel_table):
    return pl.pallas_call(
        tables_kernel,
        out_shape=shape_of(2, BIAS_ROWS, 128, dtype=F32),
        scratch_shapes=[pltpu.VMEM((3, 192, 128), F32), pltpu.VMEM((16, 768), F32)],
        compiler_params=pltpu.CompilerParams(vmem_limit_bytes=16 * 2**20),
        name="tables",
        cost_estimate=pl.CostEstimate(
            flops=8 * 10**9, bytes_accessed=8 * 10**6, transcendentals=0
        ),
    )(rel_table)


def device_attend(meta, hat, gain, shift, att, bias):
    count = hat.shape[0]
    packed = packed_rows(count)
    return call(
        attend_kernel,
        30,
        (count // 2,),
        [pair(D_IN, LARGE), whole(D_IN), whole(D_IN)]
        + GATHERED
        + [ANY],
        attention_pairs() + [ANY, whole(8, 128)],
        [
            shape_of(count, 3 * D_OUT, SMALL),
            shape_of(count, HEADS, SMALL, SMALL),
            shape_of(count, 3 * D_OUT, LARGE),
            shape_of(count, HEADS, SLOT, LARGE),
            shape_of(packed, D_OUT),
            TOKEN,
        ],
        [
            pltpu.VMEM((3 * D_OUT, D_IN), BF),
            pltpu.VMEM((2, D_OUT, LARGE), BF),
            pltpu.VMEM((2, 3, SLOT, 4 * LARGE), F32),
            pltpu.VMEM((PARTS, 96, 384), BF),
            pltpu.VMEM((D_IN, 8), F32),
            pltpu.VMEM((2, BIAS_ROWS, 128), F32),
            pltpu.VMEM((2, CHUNK, D_OUT), BF),
            pltpu.SemaphoreType.DMA((PARTS,)),
            pltpu.SemaphoreType.DMA((2,)),
            pltpu.SemaphoreType.DMA,
        ],
        "attend",
        meta,
        hat,
        gain,
        shift,
        *att,
        bias,
        vmem=40,
    )


def device_dense(meta, plain, cotp, mixed, att, ff, params, token):
    packed = plain.shape[0]
    rows_of = lambda width: pl.BlockSpec(
        (CHUNK, width), lambda n, meta: (jnp.minimum(n, meta[3, 3]), 0)
    )
    return call(
        dense_kernel,
        40,
        (packed // CHUNK,),
        [rows_of(D_IN), rows_of(D_OUT), rows_of(D_OUT)]
        + GATHERED
        + GATHERED * 2
        + [whole(D_OUT)] * 4
        + [whole(FF), ANY],
        [
            rows_of(D_OUT),
            rows_of(D_OUT),
            rows_of(D_IN),
            whole(PARTS, 224, 384),
            whole(PARTS, 224, 384),
            whole(D_OUT, D_IN),
            whole(8, D_OUT),
        ],
        [
            shape_of(packed, D_OUT),
            shape_of(packed, D_OUT),
            shape_of(packed, D_IN),
            shape_of(PARTS, 224, 384),
            shape_of(PARTS, 224, 384),
            shape_of(D_OUT, D_IN),
            shape_of(8, D_OUT, dtype=F32),
        ],
        [
            pltpu.VMEM((D_OUT, D_IN), BF),
            pltpu.VMEM((D_OUT, D_OUT), BF),
            pltpu.VMEM((FF, D_OUT), BF),
            pltpu.VMEM((FF, D_OUT), BF),
            pltpu.VMEM((D_OUT, FF), F32),
            pltpu.VMEM((D_OUT, FF), F32),
            pltpu.VMEM((D_OUT, D_OUT), F32),
            pltpu.VMEM((D_OUT, D_IN), F32),
            pltpu.VMEM((32, D_OUT), F32),
            pltpu.VMEM((8, FF), F32),
            pltpu.VMEM((PARTS, 96, 384), BF),
            pltpu.SemaphoreType.DMA((PARTS,)),
            pltpu.SemaphoreType.DMA((3 * PARTS,)),
        ],
        "dense",
        meta,
        plain,
        cotp,
        mixed,
        *att,
        *ff,
        *params,
        token,
        vmem=40,
    )


def device_expand(meta, outp, count):
    return call(
        expand_kernel,
        5,
        (count // 4,),
        [whole(*outp.shape)],
        [pl.BlockSpec((4, TOK, D_OUT), lambda n, *_: (n, 0, 0))],
        [shape_of(count, TOK, D_OUT)],
        [],
        "expand",
        meta,
        outp,
        vmem=24,
    )[0]


def device_attend_back(meta, hat, gain, shift, att, kept, gmix, gplain, gshort, small):
    count = hat.shape[0]
    packed = gmix.shape[0]
    return call(
        attend_back_kernel,
        40,
        (count // 2,),
        [pair(D_IN, LARGE), whole(D_IN), whole(D_IN)]
        + GATHERED
        + attention_pairs()
        + [
            ANY,
            ANY,
            whole(D_OUT, D_IN),
            whole(8, 384),
        ],
        [pair(2 * D_IN, LARGE), whole(480, 384), whole(480, 384), whole(48, 384)],
        [
            shape_of(count, 2 * D_IN, LARGE),
            shape_of(480, 384),
            shape_of(480, 384),
            shape_of(48, 384, dtype=F32),
        ],
        [
            pltpu.VMEM((3 * D_OUT, D_IN), BF),
            pltpu.VMEM((D_IN, 3 * D_OUT), BF),
            pltpu.VMEM((2, D_OUT, LARGE), BF),
            pltpu.VMEM((2, 3, SLOT, 4 * LARGE), F32),
            pltpu.VMEM((2, HEADS, SLOT, LARGE), BF),
            pltpu.VMEM((3 * D_OUT, 2 * LARGE), BF),
            pltpu.VMEM((3 * D_OUT, D_IN), F32),
            pltpu.VMEM((2, BIAS_ROWS, 128), F32),
            pltpu.VMEM((2, D_IN, 128), F32),
            pltpu.VMEM((6, 256, 128), F32),
            pltpu.VMEM((PARTS, 96, 384), BF),
            pltpu.VMEM((D_IN, 8), F32),
            pltpu.VMEM((2, 2 * SLOT, D_OUT), BF),
            pltpu.VMEM((2, 2 * SLOT, D_IN), BF),
            pltpu.VMEM((2, 384, 384), BF),
            pltpu.SemaphoreType.DMA((PARTS,)),
            pltpu.SemaphoreType.DMA((2, 2)),
        ],
        "attend_back",
        meta,
        hat,
        gain,
        shift,
        *att,
        *kept,
        gmix,
        gplain,
        gshort,
        small,
        vmem=52,
    )


def device_front_back(meta, images, grads, first, count, before=None):
    some = lambda *tail: pl.BlockSpec(
        (2,) + tail, lambda n, *_: (n + first,) + (0,) * len(tail)
    )
    member = lambda k, *tail: pl.BlockSpec(
        (1,) + tail, lambda n, meta: (meta[2 * (n + first) + k, 5],) + (0,) * len(tail)
    )
    chained = before is not None
    return call(
        functools.partial(front_back_kernel, first, chained),
        1,
        (count,),
        [some(D_IN, PIX)]
        + [member(k, 2 * D_IN, LARGE) for k in range(2)]
        + ([ANY] if chained else []),
        [some(D_IN, PIX)],
        [shape_of(*images.shape)],
        [],
        "front_back",
        meta,
        images,
        grads,
        grads,
        *([before] if chained else []),
        aliases={4: 0} if chained else {},
        vmem=24,
    )[0]


def shard_grads(ff, qs):
    g_up, g_down = ff[0][:192].T, ff[1][:192]
    g_out = jnp.concatenate([ff[0][192:224], ff[1][192:208]], axis=0).T
    g_qkv = jnp.concatenate([qs[:, :192], qs[:48, 192:]], axis=0).T
    g_short = qs[48:, 192:].T
    return g_short, g_qkv, g_out, g_up, g_down


def tied(*values):
    return lax.optimization_barrier(values)


class FastLinks:
    def __init__(self):
        self.own = lax.axis_index("wide")
        self.narrow = lax.axis_index("narrow")

    def across(self, value, bit):
        return lax.ppermute(value, "narrow", [(i, i ^ bit) for i in range(4)])

    def along(self, value, bits):
        return lax.ppermute(value, "wide", [(i, i ^ bits) for i in range(PARTS)])

    def spread(self, value, bits):
        pairs = [
            (4 * w + k, 4 * (w ^ k ^ bits) + k) for w in range(PARTS) for k in range(4)
        ]
        return lax.ppermute(value, ("wide", "narrow"), pairs)

    def fetch_two(self, value):
        return jnp.stack([self.spread(value, 0), self.spread(value, 5)])


def rounded(value):
    return lax.reduce_precision(value, 8, 7)


def low_sum(left, right):
    return rounded(left.astype(F32) + right.astype(F32)).astype(BF)


def high_sum(left, right):
    return left.astype(F32) + right.astype(F32)


def two_rows(value):
    high = rounded(value)
    return jnp.concatenate([high, rounded(value - high)], axis=0).astype(BF)


def one_row(pair):
    half = pair.shape[0] // 2
    return high_sum(pair[:half], pair[half:])


def tree(parts):
    while len(parts) > 1:
        parts = [high_sum(parts[k], parts[k + 1]) for k in range(0, len(parts), 2)]
    return parts[0]


class PlainLinks:
    own = 0
    narrow = 0

    def gather_weights(self, w_short, w_qkv, w_out, w_up, w_down):
        full = [
            lax.all_gather(w.astype(BF), "wide", axis=axis, tiled=True)
            for w, axis in ((w_short, 1), (w_qkv, 1), (w_out, 1), (w_up, 1), (w_down, 0))
        ]

        def shard(j):
            short, qkv, out, up, down = (
                lax.slice_in_dim(w, j * size, (j + 1) * size, axis=axis)
                for w, size, axis in zip(full, (48, 144, 48, 192, 192), (1, 1, 1, 1, 0))
            )
            qs = jnp.concatenate([qkv.T, short.T], axis=0)
            qs = jnp.concatenate([qs[:96], qs[96:]], axis=1)
            return qs, jnp.concatenate([up.T, down, out.T], axis=0)

        parts = [shard(j) for j in (0, 5, 2, 7, 1, 4, 3, 6)]
        return tuple(
            (jnp.stack([p[k] for p in parts[:4]]), jnp.stack([p[k] for p in parts[4:]]))
            for k in range(2)
        )

    def reduce_grads(self, gff, gqs):
        order = [0, 5, 2, 7, 1, 4, 3, 6]
        gqs = jnp.concatenate([half[:384].reshape(4, 96, 384) for half in gqs])
        parts = [shard_grads([g[j] for g in gff], gqs[order.index(j)]) for j in range(PARTS)]
        out = []
        for k, axis in enumerate((1, 1, 1, 1, 0)):
            whole_grad = jnp.concatenate([p[k] for p in parts], axis=axis)
            shard = lax.psum_scatter(whole_grad, "wide", scatter_dimension=axis, tiled=True)
            out.append(lax.psum(shard, "narrow").astype(F32))
        return out


def outputs(output, grad_images, weights, small):
    table = jnp.concatenate([small[16 : 16 + HEADS], small[32 : 32 + HEADS]], axis=1)
    return (
        output,
        jnp.swapaxes(grad_images, 1, 2),
        *weights,
        small[8, :192],
        small[8, 192:],
        small[0],
        small[1],
        small[2],
        small[4:8].reshape(FF),
        small[3],
        table[:, : SIDE * SIDE],
    )


def shards_plain(
    images, token_mask, w_short, w_qkv, w_out, w_up, w_down, ln1_gain, ln1_shift, out_bias,
    ln2_gain, ln2_shift, up_bias, down_bias, rel_table, cotangent,
):
    links = PlainLinks()
    count = images.shape[0]
    images = jnp.swapaxes(images, 1, 2)
    ln1 = (ln1_gain, ln1_shift)
    params = (out_bias, ln2_gain, ln2_shift, down_bias, up_bias)
    meta = device_meta(jnp.zeros((2,), jnp.int32), token_mask)
    att, ff = links.gather_weights(w_short, w_qkv, w_out, w_up, w_down)
    ff = (ff[0][:2], ff[0][2:], ff[1][:2], ff[1][2:])
    hat, plain, cotp = device_front(meta, images, cotangent)
    bias = device_tables(rel_table)
    *kept, mixed, token = device_attend(meta, hat, *ln1, att, bias)
    outp, gmix, gplain, *gff, gshort, small = device_dense(
        meta, plain, cotp, mixed, att, ff, params, token
    )
    output = device_expand(meta, outp, count)
    grads, *gqs, small = device_attend_back(
        meta, hat, *ln1, att, kept, gmix, gplain, gshort, small
    )
    grad_images = device_front_back(meta, images, grads, 0, count // 2)
    small = lax.psum(small, ("wide", "narrow"))
    return outputs(output, grad_images, links.reduce_grads(gff, gqs), small)


def shards_fast(
    images, token_mask, w_short, w_qkv, w_out, w_up, w_down, ln1_gain, ln1_shift, out_bias,
    ln2_gain, ln2_shift, up_bias, down_bias, rel_table, cotangent,
):
    links = FastLinks()
    count = images.shape[0]
    images = jnp.swapaxes(images, 1, 2)
    ln1 = (ln1_gain, ln1_shift)
    params = (out_bias, ln2_gain, ln2_shift, down_bias, up_bias)
    place = jnp.stack([links.own, links.narrow]).astype(jnp.int32)
    meta, att, ff = device_prepare(place, token_mask, w_short, w_qkv, w_out, w_up, w_down)

    att, ff = links.fetch_two(att), links.fetch_two(ff)
    hat, plain, cotp = device_front(meta, images, cotangent)
    att, hat, rel_table = tied(att, hat, rel_table)
    att = jnp.concatenate([att, links.across(att, 2)])
    bias = device_tables(rel_table)
    att, bias, ff = tied(att, bias, ff)
    att = (att, links.across(att, 1))
    ff_more, ff_other = links.across(ff, 2), links.across(ff, 1)
    *kept, mixed, token = device_attend(meta, hat, *ln1, att, bias)
    ff_more, ff_other, token = tied(ff_more, ff_other, token)
    ff = (ff, ff_more, ff_other, links.across(ff_more, 1))
    outp, gmix, gplain, gff_kept, gff_sent, gshort, small = device_dense(
        meta, plain, cotp, mixed, att, ff, params, token
    )

    got = links.across(gff_sent, 1)
    output = device_expand(meta, outp, count)
    got, output, gmix = tied(got, output, gmix)
    terms = [low_sum(gff_kept[d], got[d]) for d in range(PARTS)]
    far = (7, 6, 5, 4, 3)
    moved = {d: links.along(terms[d], d) for d in far}
    grads, gqs_kept, gqs_sent, small = device_attend_back(
        meta, hat, *ln1, att, kept, gmix, gplain, gshort, small
    )
    tie = tied(grads, gqs_kept, gqs_sent, *terms[1:3], *(moved[d] for d in far))
    grads, gqs_kept, gqs_sent = tie[:3]
    pairs = count // 2
    cuts = [k * pairs // 8 for k in (0, 2, 5, 7, 8)]
    done = None

    def beside(k, *got):
        piece = device_front_back(meta, images, grads, cuts[k], cuts[k + 1] - cuts[k], done)
        return tied(piece, *got)

    got = links.across(gqs_sent, 1)
    near = [links.along(tie[2 + d], d) for d in (1, 2)]
    done, got, *near = beside(0, got, *near)
    terms[1:] = [*near, *reversed(tie[5:])]
    held = low_sum(gqs_kept[:384], got[:384])
    small = one_row(gqs_kept[384:]) + one_row(got[384:])
    small = two_rows(small)
    sent, done = tied(jnp.concatenate([held[192:], small]), done)
    got = links.across(sent, 2)
    done, got, *terms = beside(1, got, *terms)
    held = low_sum(held[:192], got[:192])
    small = two_rows(one_row(small) + one_row(got[192:]))
    ff_sum = rounded(tree(terms)).astype(BF)
    *sent, ff_sum, done = tied(
        jnp.concatenate([held[:96], small]), jnp.concatenate([held[96:], small]), ff_sum, done
    )
    got = links.spread(sent[0], 0), links.spread(sent[1], 5)
    ff_got = links.across(ff_sum, 2)
    done, ff_got, *got = beside(2, ff_got, *got)
    held = low_sum(got[0][:96], got[1][:96])
    small = two_rows(one_row(got[0][96:]) + one_row(got[1][96:]))
    mine, done = tied(jnp.concatenate([held, small]), done)
    got = links.across(mine, 2)
    done, got, ff_sum, ff_got = beside(3, got, ff_sum, ff_got)
    mine = jnp.concatenate(
        [
            high_sum(mine[:96], got[:96]),
            one_row(mine[96:]) + one_row(got[96:]),
            high_sum(ff_sum, ff_got),
        ]
    )
    last = device_finish(place, mine, links.across(mine, 1))
    return (output, jnp.swapaxes(done, 1, 2), *(w.T for w in last[:4]), *last[4:])


def solution(mesh):
    data = ("wide", "narrow")
    rows = P(None, "wide")
    in_specs = (
        (P(data, None, None), P(data, None), rows, rows, rows, rows, P("wide", None))
        + (P(),) * 8
        + (P(data, None, None),)
    )
    out_specs = (
        (P(data, None, None), P(data, None, None), rows, rows, rows, rows, P("wide", None))
        + (P(),) * 8
    )
    fast = mesh.shape["wide"] == PARTS and mesh.shape["narrow"] == 4
    return jax.shard_map(
        shards_fast if fast else shards_plain,
        mesh=mesh,
        in_specs=in_specs,
        out_specs=out_specs,
        check_vma=False,
    )
```
